32 devices in a mesh: fsdp: 8 (over y, x, core), rep: 4 (over z).
Axes of the slice: x: 2, y: 2, z: 4, core: 2. Of those that a mesh axis runs over, the one named last changes fastest.
Arguments:
- tokens: bfloat16 [16384, 1024], P(('fsdp', 'rep')), may hold values from -6 to 6
- lengths: int32 [64], P(('fsdp', 'rep')), may hold values from 64 to 256, as said below
- cotangent: float32 [16384, 1024], P(('fsdp', 'rep')), may hold values from -6 to 6
- qkv_weight: bfloat16 [1024, 3072], P('fsdp'), may hold values from -0.1875 to 0.1875
- out_weight: bfloat16 [1024, 1024], P('fsdp'), may hold values from -0.75 to 0.75
- up_weight: bfloat16 [1024, 4096], P('fsdp'), may hold values from -0.1875 to 0.1875
- down_weight: bfloat16 [4096, 1024], P('fsdp'), may hold values from -0.09375 to 0.09375
- biases: bfloat16 [6, 1024], P(None, 'fsdp'), may hold values from -3 to 3
- up_bias: bfloat16 [4096], P('fsdp'), may hold values from -3 to 3
- gains: bfloat16 [2, 1024], P(None, 'fsdp'), may hold values from 0.5 to 1.5
Outputs:
- layer_out: bfloat16 [16384, 1024], P(('fsdp', 'rep'))
- token_grad: float32 [16384, 1024], P(('fsdp', 'rep'))
- qkv_grad: float32 [1024, 3072], P('fsdp')
- out_grad: float32 [1024, 1024], P('fsdp')
- up_grad: float32 [1024, 4096], P('fsdp')
- down_grad: float32 [4096, 1024], P('fsdp')
- biases_grad: float32 [6, 1024], P(None, 'fsdp')
- up_bias_grad: float32 [4096], P('fsdp')
- gains_grad: float32 [2, 1024], P(None, 'fsdp')
The draws below stay inside these ranges and needn't reach their ends.
Inputs may be any that keep to these rules, and one draw needn't show every extreme that they name: lengths[s] is the number of live positions of sequence slot s; in every draw some slot holds 256 live positions and some holds 64.
All inputs are finite; a program needn't handle non-finite values.
Results may differ from the reference program's by a relative error of at most 0.017.
Values may be sent and summed in bfloat16 or wider, within the bound.
A program may use at most 192 MiB of HBM per device.

```python
import math
import jax
import jax.numpy as jnp
from jax import lax

D = 1024
H = 16
HD = 64
FF = 4096
SEQ = 256
SEQS = 64
TOKENS = 16384


def draw_lengths(key, part):
    first_key, second_key = jax.random.split(jax.random.fold_in(key, 17), 2)
    drawn = jax.random.randint(first_key, (SEQS,), SEQ // 4, SEQ + 1)
    places = jax.random.permutation(second_key, SEQS)
    drawn = drawn.at[places[0]].set(SEQ)
    drawn = drawn.at[places[1]].set(SEQ // 4)
    return drawn.astype(jnp.int32)


def levels(stream_key, extent, shards, least, high):
    def one(dim, shards_of):
        draws = jax.random.uniform(jax.random.fold_in(jax.random.fold_in(stream_key, 6), dim), (shards_of,), jnp.float32, least / len(shards), high / len(shards))
        return jnp.repeat(jnp.exp(draws), extent[dim] // shards_of).reshape((-1,) + (1,) * (len(extent) - dim - 1))

    loudness = one(*shards[0])
    for cut in shards[1:]:
        loudness = loudness * one(*cut)
    return loudness


def normal_values(stream_key, extent, deviation, most, shards=(), held_as=jnp.bfloat16):
    result = jax.random.normal(stream_key, extent, jnp.float32) * deviation
    if len(shards) > 0:
        result = levels(stream_key, extent, shards, -0.22, 0.18) * result
    return jnp.clip(result, min=-most, max=most).astype(held_as)


def setup_inputs(seed: int = 0) -> dict:
    streams_of = jax.random.split(jax.random.key(seed), 11)
    tokens = normal_values(streams_of[0], (TOKENS, D), 1.0, 6.0, ((0, 32),))
    lengths = draw_lengths(jax.random.fold_in(streams_of[10], 71), 0)
    cotangent = normal_values(streams_of[2], (TOKENS, D), 1.0, 6.0, ((0, 32),), jnp.float32)
    qkv_weight = normal_values(streams_of[3], (D, 3 * D), D ** -0.5, 0.1875, ((0, 8),))
    out_weight = normal_values(streams_of[4], (D, D), (D // 16) ** -0.5, 0.75, ((0, 8),))
    up_weight = normal_values(streams_of[5], (D, FF), D ** -0.5, 0.1875, ((0, 8),))
    down_weight = normal_values(streams_of[6], (FF, D), FF ** -0.5, 0.09375, ((0, 8),))
    biases = normal_values(streams_of[7], (6, D), 0.3, 3.0, ((1, 8),))
    up_bias = normal_values(streams_of[8], (FF,), 0.3, 3.0, ((0, 8),))
    gains = jnp.clip(1.0 + 0.1 * jax.random.normal(streams_of[9], (2, D), jnp.float32), 0.5, 1.5).astype(jnp.bfloat16)
    return dict(tokens=tokens, lengths=lengths, cotangent=cotangent, qkv_weight=qkv_weight, out_weight=out_weight, up_weight=up_weight, down_weight=down_weight, biases=biases, up_bias=up_bias, gains=gains)


@jax.custom_vjp
def low(v):
    return lax.optimization_barrier(v.astype(jnp.bfloat16)).astype(jnp.float32)

@jax.custom_vjp
def low_back(v):
    return v

def low_keep(v):
    return (low(v), None)

def low_pass(kept, grad):
    return (grad,)

def back_keep(v):
    return (v, None)

def back_low(kept, grad):
    return (low(grad),)
low.defvjp(low_keep, low_pass)
low_back.defvjp(back_keep, back_low)

def layer_norm(hidden, norm_gain, norm_shift):
    center = hidden - lax.optimization_barrier(jnp.mean(hidden, axis=-1, keepdims=True))
    spread = lax.optimization_barrier(jnp.mean(center * center, axis=-1, keepdims=True))
    return center * lax.rsqrt(spread + 1e-05) * norm_gain + norm_shift

def rounded(value):
    return low(low_back(value))

def forward(row_block, live_len, w_qkv, w_out, w_up, w_down, bias_rows, bias_up, gain_rows):
    highest = lax.Precision.HIGHEST
    seq_len = row_block.shape[0]
    score_scale = 1.0 / math.sqrt(HD)
    qkv_sums = jnp.dot(row_block, w_qkv, precision=highest)
    query = rounded(qkv_sums[:, :D] + bias_rows[0]).reshape(seq_len, H, HD)
    key_heads = rounded(qkv_sums[:, D:2 * D]).reshape(seq_len, H, HD)
    value_heads = rounded(qkv_sums[:, 2 * D:] + bias_rows[1]).reshape(seq_len, H, HD)
    raw_scores = low_back(jnp.einsum('shd,thd->hst', query, key_heads, precision=highest) * score_scale)
    live_keys = jnp.arange(seq_len) < live_len
    raw_scores = jnp.where(live_keys[None, None, :], raw_scores, -1e+30)
    exp_scores = jnp.exp(raw_scores - lax.optimization_barrier(jnp.max(raw_scores, axis=-1, keepdims=True)))
    attn_probs = low(exp_scores / lax.optimization_barrier(jnp.sum(exp_scores, axis=-1, keepdims=True)))
    mixed = rounded(jnp.einsum('hst,thd->shd', attn_probs, value_heads, precision=highest).reshape(seq_len, D))
    attn_out = low_back(jnp.dot(mixed, w_out, precision=highest) + bias_rows[2])
    first_norm = layer_norm(row_block + attn_out, gain_rows[0], bias_rows[3])
    inner_sums = low_back(jnp.dot(low(first_norm), w_up, precision=highest) + bias_up)
    act_value = low(jax.nn.gelu(inner_sums, approximate=False))
    branch = low_back(jnp.dot(act_value, w_down, precision=highest) + bias_rows[4])
    return layer_norm(first_norm + branch, gain_rows[1], bias_rows[5])

def reference(tokens, lengths, cotangent, qkv_weight, out_weight, up_weight, down_weight, biases, up_bias, gains):
    slot_count = lengths.shape[0]
    group_size = math.gcd(slot_count, max(1, 4096 // SEQ))
    blocks = slot_count // group_size
    live_rows = (jnp.arange(SEQ)[None, :] < lengths[:, None]).astype(jnp.float32)
    row_items = tokens.astype(jnp.float32).reshape(blocks, group_size, SEQ, D)
    cot_items = (cotangent.reshape(slot_count, SEQ, D) * live_rows[:, :, None]).reshape(blocks, group_size, SEQ, D)
    len_items = lengths.reshape(blocks, group_size)
    params = (qkv_weight.astype(jnp.float32), out_weight.astype(jnp.float32), up_weight.astype(jnp.float32), down_weight.astype(jnp.float32), biases.astype(jnp.float32), up_bias.astype(jnp.float32), gains.astype(jnp.float32))

    def scan_step(running, block_item):
        block_rows, block_lens, block_cot = block_item

        def block_forward(row_group, w_qkv, w_out, w_up, w_down, bias_rows, bias_up, gain_rows):

            def one_sequence(row_block, live_len):
                return forward(row_block, live_len, w_qkv, w_out, w_up, w_down, bias_rows, bias_up, gain_rows)
            return jax.vmap(one_sequence)(row_group, block_lens)
        block_out, pull_back = jax.vjp(block_forward, block_rows, *params)
        cot_grads = pull_back(block_cot)
        running = tuple((grad_sum + grad_part for grad_sum, grad_part in zip(running, cot_grads[1:])))
        return (running, (block_out, cot_grads[0]))
    zero_grads = tuple((jnp.zeros_like(grad_part) for grad_part in params))
    running, (outs_all, grads_all) = lax.scan(scan_step, zero_grads, (row_items, len_items, cot_items))
    return (outs_all.reshape(-1, D).astype(jnp.bfloat16), grads_all.reshape(-1, D), running[0], running[1], running[2], running[3], running[4], running[5], running[6])
```

```python
import math

import jax
import jax.numpy as jnp
from jax import lax
from jax.sharding import PartitionSpec as P

HEAD_SIZE = 64


def matmul(left_side, right_side):
    return jnp.dot(left_side, right_side, preferred_element_type=jnp.float32)


def transposed_left(left_side, right_side):
    return lax.dot_general(
        left_side, right_side, (((0,), (0,)), ((), ())), preferred_element_type=jnp.float32
    )


def transposed_right(left_side, right_side):
    return lax.dot_general(
        left_side, right_side, (((1,), (1,)), ((), ())), preferred_element_type=jnp.float32
    )


def column_sum(values):
    return jnp.sum(values.astype(jnp.float32), axis=0)


def row_mean(values):
    return jnp.mean(values, axis=-1, keepdims=True)


def normalize(hidden):
    center = hidden - row_mean(hidden)
    inverse = lax.rsqrt(row_mean(center * center) + 1e-05)
    return center * inverse, inverse


def norm_back(grad, norm, inverse, gain):
    scaled = grad * gain
    return inverse * (scaled - row_mean(scaled) - norm * row_mean(scaled * norm))


def low(values):
    return values.astype(jnp.bfloat16)


def gather_small(biases, up_bias, gains):
    width, up_width = biases.shape[1], up_bias.shape[0]
    packed = jnp.concatenate([biases.reshape(-1), gains.reshape(-1), up_bias])
    everyone = lax.all_gather(packed, "fsdp", axis=0, tiled=False).astype(jnp.float32)
    rows = everyone[:, : 8 * width].reshape(-1, 8, width).transpose(1, 0, 2).reshape(8, -1)
    return rows[:6], everyone[:, 8 * width : 8 * width + up_width].reshape(-1), rows[6:]


def reduce_weight(grad):
    shard = lax.psum_scatter(low(grad), "fsdp", scatter_dimension=0, tiled=True)
    return lax.psum(shard, "rep").astype(jnp.float32)


def portable(
    tokens,
    lengths,
    cotangent,
    qkv_weight,
    out_weight,
    up_weight,
    down_weight,
    biases,
    up_bias,
    gains,
):
    slots = lengths.shape[0]
    rows, width = tokens.shape
    seq = rows // slots
    heads = width // HEAD_SIZE
    scale = 1.0 / math.sqrt(HEAD_SIZE)
    w_qkv = lax.all_gather(qkv_weight, "fsdp", axis=0, tiled=True)
    w_out = lax.all_gather(out_weight, "fsdp", axis=0, tiled=True)
    w_up = lax.all_gather(up_weight, "fsdp", axis=0, tiled=True)
    w_down = lax.all_gather(down_weight, "fsdp", axis=0, tiled=True)
    bias_rows, bias_up, gain_rows = gather_small(biases, up_bias, gains)

    def split(values):
        return values.reshape(slots, seq, heads, HEAD_SIZE)

    def join(values):
        return values.reshape(rows, width)

    sums = matmul(tokens, w_qkv)
    query = split(low(sums[:, :width] + bias_rows[0]))
    key = split(low(sums[:, width : 2 * width]))
    value = split(low(sums[:, 2 * width :] + bias_rows[1]))
    live = jnp.arange(seq)[None, :] < lengths[:, None]
    scores = scale * jnp.einsum(
        "bshd,bthd->bhst", query, key, preferred_element_type=jnp.float32
    )
    scores = jnp.where(live[:, None, None, :], scores, -1e30)
    exps = jnp.exp(scores - jnp.max(scores, axis=-1, keepdims=True))
    probs = exps / jnp.sum(exps, axis=-1, keepdims=True)
    probs_low = low(probs)
    mixed = low(
        join(jnp.einsum("bhst,bthd->bshd", probs_low, value, preferred_element_type=jnp.float32))
    )
    first, first_inverse = normalize(
        tokens.astype(jnp.float32) + matmul(mixed, w_out) + bias_rows[2]
    )
    first_norm = first * gain_rows[0] + bias_rows[3]
    first_low = low(first_norm)
    inner = matmul(first_low, w_up) + bias_up
    cumulative = 0.5 * (1.0 + lax.erf(inner * math.sqrt(0.5)))
    act_low = low(inner * cumulative)
    slope = low(cumulative + inner * jnp.exp(-0.5 * inner * inner) / math.sqrt(2.0 * math.pi))
    second, second_inverse = normalize(first_norm + matmul(act_low, w_down) + bias_rows[4])
    layer_out = low(second * gain_rows[1] + bias_rows[5])

    grad_out = cotangent * live.reshape(rows, 1).astype(jnp.float32)
    grad_h2 = norm_back(grad_out, second, second_inverse, gain_rows[1])
    grad_branch = low(grad_h2)
    down_grad = reduce_weight(transposed_left(act_low, grad_branch))
    grad_inner = low(transposed_right(grad_branch, w_down) * slope)
    up_grad = reduce_weight(transposed_left(first_low, grad_inner))
    grad_first = grad_h2 + transposed_right(grad_inner, w_up)
    grad_h1 = norm_back(grad_first, first, first_inverse, gain_rows[0])
    grad_attn = low(grad_h1)
    out_grad = reduce_weight(transposed_left(mixed, grad_attn))
    grad_mixed = split(low(transposed_right(grad_attn, w_out)))
    grad_probs = jnp.einsum(
        "bshd,bthd->bhst", grad_mixed, value, preferred_element_type=jnp.float32
    )
    shared = jnp.sum(probs * grad_probs, axis=-1, keepdims=True)
    grad_scores = low(probs * (grad_probs - shared))
    grad_query = scale * jnp.einsum(
        "bhst,bthd->bshd", grad_scores, key, preferred_element_type=jnp.float32
    )
    grad_key = scale * jnp.einsum(
        "bhst,bshd->bthd", grad_scores, query, preferred_element_type=jnp.float32
    )
    grad_value = jnp.einsum(
        "bhst,bshd->bthd", probs_low, grad_mixed, preferred_element_type=jnp.float32
    )
    grad_qkv = jnp.concatenate(
        [join(low(grad_query)), join(low(grad_key)), join(low(grad_value))], axis=1
    )
    qkv_grad = reduce_weight(transposed_left(tokens, grad_qkv))
    token_grad = grad_h1 + transposed_right(grad_qkv, w_qkv)
    small = jnp.stack(
        [
            column_sum(grad_qkv[:, :width]),
            column_sum(grad_qkv[:, 2 * width :]),
            column_sum(grad_attn),
            column_sum(grad_first),
            column_sum(grad_branch),
            column_sum(grad_out),
            column_sum(grad_first * first),
            column_sum(grad_out * second),
        ]
    )
    owner = lax.axis_index("fsdp")
    small, up_sum = lax.psum((small, column_sum(grad_inner)), ("fsdp", "rep"))
    own, own_up = biases.shape[1], up_bias.shape[0]
    small = lax.dynamic_slice(small, (0, owner * own), (8, own))
    up_bias_grad = lax.dynamic_slice(up_sum, (owner * own_up,), (own_up,))
    return (
        layer_out,
        token_grad,
        qkv_grad,
        out_grad,
        up_grad,
        down_grad,
        small[:6],
        up_bias_grad,
        small[6:],
    )


def solution(mesh):
    both = ("fsdp", "rep")
    in_specs = (
        P(both, None),
        P(both),
        P(both, None),
        P("fsdp", None),
        P("fsdp", None),
        P("fsdp", None),
        P("fsdp", None),
        P(None, "fsdp"),
        P("fsdp"),
        P(None, "fsdp"),
    )
    out_specs = (
        P(both, None),
        P(both, None),
        P("fsdp", None),
        P("fsdp", None),
        P("fsdp", None),
        P("fsdp", None),
        P(None, "fsdp"),
        P("fsdp"),
        P(None, "fsdp"),
    )
    return jax.shard_map(
        portable, mesh=mesh, in_specs=in_specs, out_specs=out_specs, check_vma=False
    )
```

```python
import math

import jax
import jax.numpy as jnp
from jax import lax
from jax.experimental import pallas as pl
from jax.experimental.pallas import tpu as pltpu
from jax.sharding import PartitionSpec as P

HEAD_SIZE = 64


def matmul(left_side, right_side):
    return jnp.dot(left_side, right_side, preferred_element_type=jnp.float32)


def transposed_left(left_side, right_side):
    return lax.dot_general(
        left_side, right_side, (((0,), (0,)), ((), ())), preferred_element_type=jnp.float32
    )


def transposed_right(left_side, right_side):
    return lax.dot_general(
        left_side, right_side, (((1,), (1,)), ((), ())), preferred_element_type=jnp.float32
    )


def column_sum(values):
    return jnp.sum(values.astype(jnp.float32), axis=0)


def row_mean(values):
    return jnp.mean(values, axis=-1, keepdims=True)


def normalize(hidden):
    center = hidden - row_mean(hidden)
    inverse = lax.rsqrt(row_mean(center * center) + 1e-05)
    return center * inverse, inverse


def norm_back(grad, norm, inverse, gain):
    scaled = grad * gain
    return inverse * (scaled - row_mean(scaled) - norm * row_mean(scaled * norm))


def low(values):
    return values.astype(jnp.bfloat16)


def gather_small(biases, up_bias, gains):
    width, up_width = biases.shape[1], up_bias.shape[0]
    packed = jnp.concatenate([biases.reshape(-1), gains.reshape(-1), up_bias])
    everyone = lax.all_gather(packed, "fsdp", axis=0, tiled=False).astype(jnp.float32)
    rows = everyone[:, : 8 * width].reshape(-1, 8, width).transpose(1, 0, 2).reshape(8, -1)
    return rows[:6], everyone[:, 8 * width : 8 * width + up_width].reshape(-1), rows[6:]


def reduce_weight(grad):
    shard = lax.psum_scatter(low(grad), "fsdp", scatter_dimension=0, tiled=True)
    return lax.psum(shard, "rep").astype(jnp.float32)


def portable(
    tokens,
    lengths,
    cotangent,
    qkv_weight,
    out_weight,
    up_weight,
    down_weight,
    biases,
    up_bias,
    gains,
):
    slots = lengths.shape[0]
    rows, width = tokens.shape
    seq = rows // slots
    heads = width // HEAD_SIZE
    scale = 1.0 / math.sqrt(HEAD_SIZE)
    w_qkv = lax.all_gather(qkv_weight, "fsdp", axis=0, tiled=True)
    w_out = lax.all_gather(out_weight, "fsdp", axis=0, tiled=True)
    w_up = lax.all_gather(up_weight, "fsdp", axis=0, tiled=True)
    w_down = lax.all_gather(down_weight, "fsdp", axis=0, tiled=True)
    bias_rows, bias_up, gain_rows = gather_small(biases, up_bias, gains)

    def split(values):
        return values.reshape(slots, seq, heads, HEAD_SIZE)

    def join(values):
        return values.reshape(rows, width)

    sums = matmul(tokens, w_qkv)
    query = split(low(sums[:, :width] + bias_rows[0]))
    key = split(low(sums[:, width : 2 * width]))
    value = split(low(sums[:, 2 * width :] + bias_rows[1]))
    live = jnp.arange(seq)[None, :] < lengths[:, None]
    scores = scale * jnp.einsum(
        "bshd,bthd->bhst", query, key, preferred_element_type=jnp.float32
    )
    scores = jnp.where(live[:, None, None, :], scores, -1e30)
    exps = jnp.exp(scores - jnp.max(scores, axis=-1, keepdims=True))
    probs = exps / jnp.sum(exps, axis=-1, keepdims=True)
    probs_low = low(probs)
    mixed = low(
        join(jnp.einsum("bhst,bthd->bshd", probs_low, value, preferred_element_type=jnp.float32))
    )
    first, first_inverse = normalize(
        tokens.astype(jnp.float32) + matmul(mixed, w_out) + bias_rows[2]
    )
    first_norm = first * gain_rows[0] + bias_rows[3]
    first_low = low(first_norm)
    inner = matmul(first_low, w_up) + bias_up
    cumulative = 0.5 * (1.0 + lax.erf(inner * math.sqrt(0.5)))
    act_low = low(inner * cumulative)
    slope = low(cumulative + inner * jnp.exp(-0.5 * inner * inner) / math.sqrt(2.0 * math.pi))
    second, second_inverse = normalize(first_norm + matmul(act_low, w_down) + bias_rows[4])
    layer_out = low(second * gain_rows[1] + bias_rows[5])

    grad_out = cotangent * live.reshape(rows, 1).astype(jnp.float32)
    grad_h2 = norm_back(grad_out, second, second_inverse, gain_rows[1])
    grad_branch = low(grad_h2)
    down_grad = reduce_weight(transposed_left(act_low, grad_branch))
    grad_inner = low(transposed_right(grad_branch, w_down) * slope)
    up_grad = reduce_weight(transposed_left(first_low, grad_inner))
    grad_first = grad_h2 + transposed_right(grad_inner, w_up)
    grad_h1 = norm_back(grad_first, first, first_inverse, gain_rows[0])
    grad_attn = low(grad_h1)
    out_grad = reduce_weight(transposed_left(mixed, grad_attn))
    grad_mixed = split(low(transposed_right(grad_attn, w_out)))
    grad_probs = jnp.einsum(
        "bshd,bthd->bhst", grad_mixed, value, preferred_element_type=jnp.float32
    )
    shared = jnp.sum(probs * grad_probs, axis=-1, keepdims=True)
    grad_scores = low(probs * (grad_probs - shared))
    grad_query = scale * jnp.einsum(
        "bhst,bthd->bshd", grad_scores, key, preferred_element_type=jnp.float32
    )
    grad_key = scale * jnp.einsum(
        "bhst,bshd->bthd", grad_scores, query, preferred_element_type=jnp.float32
    )
    grad_value = jnp.einsum(
        "bhst,bshd->bthd", probs_low, grad_mixed, preferred_element_type=jnp.float32
    )
    grad_qkv = jnp.concatenate(
        [join(low(grad_query)), join(low(grad_key)), join(low(grad_value))], axis=1
    )
    qkv_grad = reduce_weight(transposed_left(tokens, grad_qkv))
    token_grad = grad_h1 + transposed_right(grad_qkv, w_qkv)
    small = jnp.stack(
        [
            column_sum(grad_qkv[:, :width]),
            column_sum(grad_qkv[:, 2 * width :]),
            column_sum(grad_attn),
            column_sum(grad_first),
            column_sum(grad_branch),
            column_sum(grad_out),
            column_sum(grad_first * first),
            column_sum(grad_out * second),
        ]
    )
    owner = lax.axis_index("fsdp")
    small, up_sum = lax.psum((small, column_sum(grad_inner)), ("fsdp", "rep"))
    own, own_up = biases.shape[1], up_bias.shape[0]
    small = lax.dynamic_slice(small, (0, owner * own), (8, own))
    up_bias_grad = lax.dynamic_slice(up_sum, (owner * own_up,), (own_up,))
    return (
        layer_out,
        token_grad,
        qkv_grad,
        out_grad,
        up_grad,
        down_grad,
        small[:6],
        up_bias_grad,
        small[6:],
    )


MESH = pl.DeviceIdType.MESH
F32 = jnp.float32
BF16 = jnp.bfloat16
MIB = 1 << 20


def dot_nn(a, b):
    return lax.dot_general(a, b, (((1,), (0,)), ((), ())), preferred_element_type=F32)


def dot_nt(a, b):
    return lax.dot_general(a, b, (((1,), (1,)), ((), ())), preferred_element_type=F32)


def dot_tn(a, b):
    return lax.dot_general(a, b, (((0,), (0,)), ((), ())), preferred_element_type=F32)


class Place:
    def __init__(self):
        f, z = lax.axis_index("fsdp"), lax.axis_index("rep")
        self.f, self.z = f, z
        self.core = lax.rem(f, 2)
        self.x = lax.rem(lax.div(f, 2), 2)
        self.y = lax.div(f, 4)
        self.chip = lax.div(f, 2)
        self.fx = f + 2 - 4 * self.x
        self.fy = f + 4 - 8 * self.y
        self.fd = self.fx + 4 - 8 * self.y
        self.fs = f + 1 - 2 * self.core
        self.par = lax.rem(z, 2)
        self.zn = z + 1 - 2 * self.par

    def dev(self, f=None, z=None):
        return {"fsdp": self.f if f is None else f, "rep": self.z if z is None else z}


def remote(src, dst, send_sem, recv_sem, device):
    return pltpu.make_async_remote_copy(
        src_ref=src, dst_ref=dst, send_sem=send_sem, recv_sem=recv_sem,
        device_id=device, device_id_type=MESH,
    )


UNITS = 4
KINDS = 15


class Gather:
    def __init__(self, place, unit, shard, full, r, split, send, recv):
        self.p, self.unit, self.shard, self.full = place, unit, shard, full
        self.rows = shard.shape[0]
        self.r, self.n = r, self.rows - r
        self.h = split
        self.lo = r * (1 - place.par)
        self.z_out = self.n * (1 - place.par)
        self.z_in = self.n * place.par
        self.send, self.recv = send, recv

    def at(self, f, lo, n):
        return self.full.at[pl.ds(pl.multiple_of(f * self.rows + lo, 16), n)]

    def copy(self, kind, f, lo, n, device, src=None):
        place = self.at(f, lo, n)
        return remote(
            place if src is None else src, place,
            self.send.at[self.unit, kind], self.recv.at[self.unit, kind], device,
        )

    def pieces(self):
        p, lo, n, h, r = self.p, self.lo, self.n, self.h, self.r
        to_x, to_y, to_s = p.dev(f=p.fx), p.dev(f=p.fy), p.dev(f=p.fs)
        to_z = p.dev(z=p.zn)
        sx, sy, sd = (g + 1 - 2 * p.core for g in (p.fx, p.fy, p.fd))
        return {
            0: (p.fx, p.f, lo, lo, n, to_x),
            1: (p.fy, p.f, lo, lo, n, to_y),
            2: (p.fd, p.fx, lo, lo, h, to_y),
            3: (p.fd, p.fy, lo + h, lo + h, n - h, to_x),
            4: (p.fx, p.fx, self.z_in, self.z_out, r, to_z),
            5: (p.fy, p.fy, self.z_in, self.z_out, r, to_z),
            6: (p.fd, p.fd, self.z_in, self.z_out, r, to_z),
            7: (p.fs, p.f, 0, 0, self.rows, to_s),
            8: (sx, p.fx, lo, lo, n, to_s),
            9: (sx, p.fx, self.z_in, self.z_in, r, to_s),
            10: (sy, p.fy, lo, lo, n, to_s),
            11: (sy, p.fy, self.z_in, self.z_in, r, to_s),
            12: (sd, p.fd, lo, lo, h, to_s),
            13: (sd, p.fd, lo + h, lo + h, n - h, to_s),
            14: (sd, p.fd, self.z_in, self.z_in, r, to_s),
        }

    def start(self, *kinds):
        for kind in kinds:
            _, owner, _, lo, n, device = self.pieces()[kind]
            src = None
            if kind in (0, 1, 7):
                src = self.shard.at[pl.ds(pl.multiple_of(lo, 16), n)]
            self.copy(kind, owner, lo, n, device, src).start()

    def got(self, *kinds):
        for kind in kinds:
            owner, _, lo, _, n, device = self.pieces()[kind]
            self.copy(kind, owner, lo, n, device).wait_recv()

    def sent(self):
        for kind in range(KINDS):
            _, owner, _, lo, n, device = self.pieces()[kind]
            self.copy(kind, owner, lo, n, device).wait_send()

    def direct(self, local_sem):
        self.start(0, 1, 7)
        self.local(local_sem).start()

    def local(self, local_sem):
        return pltpu.make_async_copy(self.shard, self.at(self.p.f, 0, self.rows), local_sem)

    def forward(self):
        self.got(0)
        self.start(2, 4, 8)
        self.got(1)
        self.start(3, 5, 10)

    def finish(self):
        self.got(2, 3)
        self.start(6, 12, 13)
        self.got(4)
        self.start(9)
        self.got(5)
        self.start(11)
        self.got(6)
        self.start(14)
        self.got(7, 8, 9, 10, 11, 12, 13, 14)


def forward_kernel(
    lengths, tokens, cot, small, sh_q, sh_o, sh_u, sh_d,
    layer_out, wq_out, wo_out, wu_out, wd_out, qkv_out, slope_out, act_pair, first_pair, mixed_pair,
    tok_pair, branch_pair, norm_out, inv_out, grad_out_ref, params_out, sums_out, act_out, mixed_out,
    x, wq, wo, wu, wd, qkv, mixed, norm, first_low, act, slope, acc, cot_v, gh2, out_v, gb, smalls, params,
    inv_v, sums, up_rows,
    ag_send, ag_recv, ag_local, sm_send, sm_recv, sm_local, io, pair_send, pair_recv, pair_local,
):
    p = Place()
    rows, width = x.shape
    slots = lengths.shape[0]
    seq = rows // slots
    others = [lax.rem(p.f + k, 8) for k in range(1, 8)]
    barrier = pltpu.get_barrier_semaphore()
    for g in others:
        pl.semaphore_signal(barrier, inc=1, device_id=p.dev(f=g), device_id_type=MESH)
    pl.semaphore_signal(barrier, inc=1, device_id=p.dev(z=p.zn), device_id_type=MESH)
    loads = [
        pltpu.make_async_copy(tokens, x, io.at[0]),
        pltpu.make_async_copy(cot, cot_v, io.at[1]),
        pltpu.make_async_copy(small, smalls.at[p.f], sm_local),
    ]
    for c in loads:
        c.start()
    pl.semaphore_wait(barrier, 8)

    def small_copy(k, owner, device):
        return remote(small, smalls.at[owner], sm_send.at[k], sm_recv.at[k], device)

    for k, g in enumerate(others):
        small_copy(k, p.f, p.dev(f=g)).start()

    shards = (sh_q, sh_o, sh_u, sh_d)
    fulls = (wq, wo, wu, wd)
    cuts = ((32, 48), (32, 48), (32, 48), (160, 176))
    g_q, g_o, g_u, g_d = (
        Gather(p, u, shards[u], fulls[u], *cuts[u], ag_send, ag_recv) for u in range(UNITS)
    )
    g_q.direct(ag_local.at[0])
    g_o.direct(ag_local.at[1])

    mine = pl.ds(pl.multiple_of(p.core * rows, rows), rows)

    def pair(index, chip, src, dst, cols):
        own = pl.ds(pl.multiple_of((2 * chip + p.core) * cols, cols), cols)
        other = pl.ds(pl.multiple_of((2 * chip + 1 - p.core) * cols, cols), cols)
        here = dst.at[mine, pl.ds(chip * cols, cols)]
        return (
            pltpu.make_async_copy(src.at[:, own], here, pair_local.at[index, chip]),
            remote(src.at[:, other], here, pair_send.at[index, chip], pair_recv.at[index, chip], p.dev(f=p.fs)),
        )

    pairs = []

    def start_pair(index, src, dst, cols, chips=range(4)):
        for chip in chips:
            for c in pair(index, chip, src, dst, cols):
                c.start()
            pairs.append((index, chip, src, dst, cols))

    loads[0].wait()
    start_pair(0, x, tok_pair, 128)
    loads[2].wait()
    for k, g in enumerate(others):
        back = lax.rem(p.f + 7 - k, 8)
        small_copy(k, back, p.dev(f=back)).wait_recv()
    for g in range(8):
        part = smalls[g].astype(F32)
        params[:, g * 128 : (g + 1) * 128] = part
        for j in range(4):
            up_rows[g : g + 1, j * 128 : (j + 1) * 128] = part[8 + j : 9 + j]
    g_q.forward()
    g_o.forward()
    g_u.direct(ag_local.at[2])
    g_q.finish()
    g_q.local(ag_local.at[0]).wait()
    stores = [pltpu.make_async_copy(wq, wq_out, io.at[2])]
    stores[-1].start()
    for j in range(3):
        part = dot_nn(x[...], wq[:, j * width : (j + 1) * width])
        if j == 0:
            part = part + params[0:1]
        if j == 2:
            part = part + params[1:2]
        qkv[:, j * width : (j + 1) * width] = part.astype(BF16)
    stores.append(pltpu.make_async_copy(qkv, qkv_out, io.at[3]))
    stores[-1].start()

    left = lax.broadcasted_iota(jnp.int32, (seq, 128), 1) < HEAD_SIZE
    key_row = lax.broadcasted_iota(jnp.int32, (seq, seq), 0)

    def attend(step, carry):
        slot, pair_of = lax.div(step, 8), lax.rem(step, 8)
        at_rows = pl.ds(pl.multiple_of(slot * seq, seq), seq)
        col = pl.multiple_of(pair_of * 128, 128)
        q = qkv[at_rows, pl.ds(col, 128)]
        k = qkv[at_rows, pl.ds(pl.multiple_of(width + col, 128), 128)]
        v = qkv[at_rows, pl.ds(pl.multiple_of(2 * width + col, 128), 128)]
        dead = key_row >= lengths[slot]
        outs = []
        for head in range(2):
            k_head = jnp.where(left if head == 0 else ~left, k, jnp.zeros_like(k))
            scores = dot_nt(k_head, q) * (1.0 / math.sqrt(HEAD_SIZE))
            scores = jnp.where(dead, -1e30, scores)
            exps = jnp.exp(scores - jnp.max(scores, axis=0, keepdims=True))
            probs = exps * (1.0 / jnp.sum(exps, axis=0, keepdims=True))
            outs.append(dot_tn(probs.astype(BF16), v))
        mixed[at_rows, pl.ds(col, 128)] = jnp.where(left, outs[0], outs[1]).astype(BF16)
        return carry

    lax.fori_loop(0, 8 * slots, attend, 0)
    start_pair(1, mixed, mixed_pair, 128)
    g_o.finish()
    g_o.local(ag_local.at[1]).wait()
    g_u.forward()
    g_d.direct(ag_local.at[3])
    stores.append(pltpu.make_async_copy(wo, wo_out, io.at[4]))
    stores[-1].start()
    hidden = x[...].astype(F32) + dot_nn(mixed[...], wo[...]) + params[2:3]
    center = hidden - row_mean(hidden)
    inverse = lax.rsqrt(row_mean(center * center) + 1e-05)
    norm[...] = center * inverse
    inv_v[...] = jnp.broadcast_to(inverse, inv_v.shape)
    acc[...] = norm[...] * params[6:7] + params[3:4]
    first_low[...] = acc[...].astype(BF16)
    start_pair(2, first_low, first_pair, 128)
    stores.append(pltpu.make_async_copy(norm, norm_out, io.at[5]))
    stores.append(pltpu.make_async_copy(inv_v, inv_out, io.at[6]))
    stores[-1].start()
    stores[-2].start()
    g_u.finish()
    g_u.local(ag_local.at[2]).wait()
    stores.append(pltpu.make_async_copy(wu, wu_out, io.at[7]))
    stores[-1].start()

    def up_step(j, carry):
        cols = pl.ds(pl.multiple_of(j * 512, 512), 512)
        inner = dot_nn(first_low[...], wu[:, cols]) + up_rows[pl.ds(j, 1), :]
        phi = 0.5 * (1.0 + lax.erf(inner * math.sqrt(0.5)))
        act[:, cols] = (inner * phi).astype(BF16)
        density = jnp.exp(-0.5 * inner * inner) * (1.0 / math.sqrt(2.0 * math.pi))
        slope[:, cols] = (phi + inner * density).astype(BF16)
        return carry

    lax.fori_loop(0, 4, up_step, 0)
    g_d.forward()
    start_pair(3, act, act_pair, 512, range(2))
    lax.fori_loop(4, 8, up_step, 0)
    start_pair(3, act, act_pair, 512, range(2, 4))
    stores.append(pltpu.make_async_copy(slope, slope_out, io.at[8]))
    stores[-1].start()
    stores.append(pltpu.make_async_copy(act, act_out, io.at[14]))
    stores[-1].start()
    stores.append(pltpu.make_async_copy(mixed, mixed_out, io.at[15]))
    stores[-1].start()
    g_d.finish()
    g_d.local(ag_local.at[3]).wait()
    stores.append(pltpu.make_async_copy(wd, wd_out, io.at[9]))
    stores[-1].start()
    acc[...] += params[4:5]
    for j in range(4):
        acc[...] += dot_nn(act[:, j * 1024 : (j + 1) * 1024], wd[j * 1024 : (j + 1) * 1024, :])
    loads[1].wait()
    hidden = acc[...]
    center = hidden - row_mean(hidden)
    inverse = lax.rsqrt(row_mean(center * center) + 1e-05)
    second = center * inverse
    out_v[...] = (second * params[7:8] + params[5:6]).astype(BF16)
    stores.append(pltpu.make_async_copy(out_v, layer_out, io.at[10]))
    stores[-1].start()
    row_at = lax.broadcasted_iota(jnp.int32, (seq, 1), 0)
    live = jnp.concatenate([(row_at < lengths[s]).astype(F32) for s in range(slots)], axis=0)
    e = cot_v[...] * live
    sums[...] = jnp.zeros_like(sums)
    sums[0:1] = jnp.sum(e * second, axis=0, keepdims=True)
    sums[1:2] = jnp.sum(e, axis=0, keepdims=True)
    scaled = e * params[7:8]
    gh2[...] = inverse * (scaled - row_mean(scaled) - second * row_mean(scaled * second))
    gb[...] = gh2[...].astype(BF16)
    c_local = pltpu.make_async_copy(gb, branch_pair.at[mine], pair_local.at[4, 0])
    c_remote = remote(gb, branch_pair.at[mine], pair_send.at[4, 0], pair_recv.at[4, 0], p.dev(f=p.fs))
    c_local.start()
    c_remote.start()
    sums[2:3] = jnp.sum(gb[...].astype(F32), axis=0, keepdims=True)
    stores.append(pltpu.make_async_copy(gh2, grad_out_ref, io.at[11]))
    stores.append(pltpu.make_async_copy(params, params_out, io.at[12]))
    stores.append(pltpu.make_async_copy(sums, sums_out, io.at[13]))
    for c in stores[-3:]:
        c.start()
    for c in stores:
        c.wait()
    c_local.wait()
    c_remote.wait()
    for args in pairs:
        a, b = pair(*args)
        a.wait()
        b.wait()
    for k, g in enumerate(others):
        small_copy(k, p.f, p.dev(f=g)).wait_send()
    for g in (g_q, g_o, g_u, g_d):
        g.sent()


def forward_call(tokens, lengths, cotangent, qkv_w, out_w, up_w, down_w, small):
    rows, width = tokens.shape
    ff = up_w.shape[1]
    anyspace = pl.BlockSpec(memory_space=pl.ANY)
    shape = jax.ShapeDtypeStruct
    outs = [
        shape((rows, width), BF16),
        shape((width, 3 * width), BF16),
        shape((width, width), BF16),
        shape((width, ff), BF16),
        shape((ff, width), BF16),
        shape((rows, 3 * width), BF16),
        shape((rows, ff), BF16),
        shape((2 * rows, ff // 2), BF16),
        shape((2 * rows, width // 2), BF16),
        shape((2 * rows, width // 2), BF16),
        shape((2 * rows, width // 2), BF16),
        shape((2 * rows, width), BF16),
        shape((rows, width), F32),
        shape((rows, 128), F32),
        shape((rows, width), F32),
        shape((16, width), F32),
        shape((8, width), F32),
        shape((rows, ff), BF16),
        shape((rows, width), BF16),
    ]
    dma = pltpu.SemaphoreType.DMA
    scratch = [
        pltpu.VMEM((rows, width), BF16),
        pltpu.VMEM((width, 3 * width), BF16),
        pltpu.VMEM((width, width), BF16),
        pltpu.VMEM((width, ff), BF16),
        pltpu.VMEM((ff, width), BF16),
        pltpu.VMEM((rows, 3 * width), BF16),
        pltpu.VMEM((rows, width), BF16),
        pltpu.VMEM((rows, width), F32),
        pltpu.VMEM((rows, width), BF16),
        pltpu.VMEM((rows, ff), BF16),
        pltpu.VMEM((rows, ff), BF16),
        pltpu.VMEM((rows, width), F32),
        pltpu.VMEM((rows, width), F32),
        pltpu.VMEM((rows, width), F32),
        pltpu.VMEM((rows, width), BF16),
        pltpu.VMEM((rows, width), BF16),
        pltpu.VMEM((8, 16, 128), BF16),
        pltpu.VMEM((16, width), F32),
        pltpu.VMEM((rows, 128), F32),
        pltpu.VMEM((8, width), F32),
        pltpu.VMEM((8, ff // 8), F32),
        dma((UNITS, KINDS)),
        dma((UNITS, KINDS)),
        dma((UNITS,)),
        dma((7,)),
        dma((7,)),
        dma,
        dma((16,)),
        dma((5, 4)),
        dma((5, 4)),
        dma((5, 4)),
    ]
    return pl.pallas_call(
        forward_kernel,
        out_shape=outs,
        in_specs=[pl.BlockSpec(memory_space=pltpu.SMEM)] + [anyspace] * 7,
        out_specs=[anyspace] * len(outs),
        scratch_shapes=scratch,
        name="forward",
        cost_estimate=pl.CostEstimate(flops=2 * 512 * 12582912, bytes_accessed=60 * MIB, transcendentals=4 * MIB),
        compiler_params=pltpu.CompilerParams(
            collective_id=0, has_side_effects=True, vmem_limit_bytes=60 * MIB
        ),
    )(lengths, tokens, cotangent, small, qkv_w, out_w, up_w, down_w)


def pack_small(biases, up_bias, gains):
    return jnp.concatenate([biases, gains, up_bias.reshape(4, 128), jnp.zeros((4, 128), BF16)], axis=0)


def plane(
    tokens,
    lengths,
    cotangent,
    qkv_weight,
    out_weight,
    up_weight,
    down_weight,
    biases,
    up_bias,
    gains,
):
    slots = lengths.shape[0]
    rows, width = tokens.shape
    seq = rows // slots
    heads = width // HEAD_SIZE
    scale = 1.0 / math.sqrt(HEAD_SIZE)
    got = forward_call(
        tokens, lengths, cotangent, qkv_weight, out_weight, up_weight, down_weight,
        pack_small(biases, up_bias, gains),
    )
    layer_out, w_qkv, w_out, w_up, w_down, qkv, slope = got[:7]
    grad_branch_pair, first, first_inverse, grad_h2, params, sums, act_low, mixed = got[11:]
    first_inverse = first_inverse[:, :1]
    gain_one = params[6]
    first_low = low(first * gain_one + params[3])
    grad_branch = low(grad_h2)

    def split(values):
        return values.reshape(slots, seq, heads, HEAD_SIZE)

    def join(values):
        return values.reshape(rows, width)

    query, key, value = (split(qkv[:, j * width : (j + 1) * width]) for j in range(3))
    live = jnp.arange(seq)[None, :] < lengths[:, None]
    scores = scale * jnp.einsum(
        "bshd,bthd->bhst", query, key, preferred_element_type=jnp.float32
    )
    scores = jnp.where(live[:, None, None, :], scores, -1e30)
    exps = jnp.exp(scores - jnp.max(scores, axis=-1, keepdims=True))
    probs = exps / jnp.sum(exps, axis=-1, keepdims=True)
    probs_low = low(probs)
    down_grad = reduce_weight(transposed_left(act_low, grad_branch))
    grad_inner = low(transposed_right(grad_branch, w_down) * slope)
    up_grad = reduce_weight(transposed_left(first_low, grad_inner))
    grad_first = grad_h2 + transposed_right(grad_inner, w_up)
    grad_h1 = norm_back(grad_first, first, first_inverse, gain_one)
    grad_attn = low(grad_h1)
    out_grad = reduce_weight(transposed_left(mixed, grad_attn))
    grad_mixed = split(low(transposed_right(grad_attn, w_out)))
    grad_probs = jnp.einsum(
        "bshd,bthd->bhst", grad_mixed, value, preferred_element_type=jnp.float32
    )
    shared = jnp.sum(probs * grad_probs, axis=-1, keepdims=True)
    grad_scores = low(probs * (grad_probs - shared))
    grad_query = scale * jnp.einsum(
        "bhst,bthd->bshd", grad_scores, key, preferred_element_type=jnp.float32
    )
    grad_key = scale * jnp.einsum(
        "bhst,bshd->bthd", grad_scores, query, preferred_element_type=jnp.float32
    )
    grad_value = jnp.einsum(
        "bhst,bshd->bthd", probs_low, grad_mixed, preferred_element_type=jnp.float32
    )
    grad_qkv = jnp.concatenate(
        [join(low(grad_query)), join(low(grad_key)), join(low(grad_value))], axis=1
    )
    qkv_grad = reduce_weight(transposed_left(tokens, grad_qkv))
    token_grad = grad_h1 + transposed_right(grad_qkv, w_qkv)
    small = jnp.stack(
        [
            column_sum(grad_qkv[:, :width]),
            column_sum(grad_qkv[:, 2 * width :]),
            column_sum(grad_attn),
            column_sum(grad_first),
            sums[2],
            sums[1],
            column_sum(grad_first * first),
            sums[0],
        ]
    )
    owner = lax.axis_index("fsdp")
    small, up_sum = lax.psum((small, column_sum(grad_inner)), ("fsdp", "rep"))
    own, own_up = biases.shape[1], up_bias.shape[0]
    small = lax.dynamic_slice(small, (0, owner * own), (8, own))
    up_bias_grad = lax.dynamic_slice(up_sum, (owner * own_up,), (own_up,))
    return (
        layer_out,
        token_grad,
        qkv_grad,
        out_grad,
        up_grad,
        down_grad,
        small[:6],
        up_bias_grad,
        small[6:],
    )


def solution(mesh):
    step = plane if dict(mesh.shape) == {"fsdp": 8, "rep": 4} else portable
    both = ("fsdp", "rep")
    in_specs = (
        P(both, None),
        P(both),
        P(both, None),
        P("fsdp", None),
        P("fsdp", None),
        P("fsdp", None),
        P("fsdp", None),
        P(None, "fsdp"),
        P("fsdp"),
        P(None, "fsdp"),
    )
    out_specs = (
        P(both, None),
        P(both, None),
        P("fsdp", None),
        P("fsdp", None),
        P("fsdp", None),
        P("fsdp", None),
        P(None, "fsdp"),
        P("fsdp"),
        P(None, "fsdp"),
    )
    return jax.shard_map(
        step, mesh=mesh, in_specs=in_specs, out_specs=out_specs, check_vma=False
    )
```

```python
import math

import jax
import jax.numpy as jnp
from jax import lax
from jax.experimental import pallas as pl
from jax.experimental.pallas import tpu as pltpu
from jax.sharding import PartitionSpec as P

HEAD_SIZE = 64


def matmul(left_side, right_side):
    return jnp.dot(left_side, right_side, preferred_element_type=jnp.float32)


def transposed_left(left_side, right_side):
    return lax.dot_general(
        left_side, right_side, (((0,), (0,)), ((), ())), preferred_element_type=jnp.float32
    )


def transposed_right(left_side, right_side):
    return lax.dot_general(
        left_side, right_side, (((1,), (1,)), ((), ())), preferred_element_type=jnp.float32
    )


def column_sum(values):
    return jnp.sum(values.astype(jnp.float32), axis=0)


def row_mean(values):
    return jnp.mean(values, axis=-1, keepdims=True)


def normalize(hidden):
    center = hidden - row_mean(hidden)
    inverse = lax.rsqrt(row_mean(center * center) + 1e-05)
    return center * inverse, inverse


def norm_back(grad, norm, inverse, gain):
    scaled = grad * gain
    return inverse * (scaled - row_mean(scaled) - norm * row_mean(scaled * norm))


def low(values):
    return values.astype(jnp.bfloat16)


def gather_small(biases, up_bias, gains):
    width, up_width = biases.shape[1], up_bias.shape[0]
    packed = jnp.concatenate([biases.reshape(-1), gains.reshape(-1), up_bias])
    everyone = lax.all_gather(packed, "fsdp", axis=0, tiled=False).astype(jnp.float32)
    rows = everyone[:, : 8 * width].reshape(-1, 8, width).transpose(1, 0, 2).reshape(8, -1)
    return rows[:6], everyone[:, 8 * width : 8 * width + up_width].reshape(-1), rows[6:]


def reduce_weight(grad):
    shard = lax.psum_scatter(low(grad), "fsdp", scatter_dimension=0, tiled=True)
    return lax.psum(shard, "rep").astype(jnp.float32)


def portable(
    tokens,
    lengths,
    cotangent,
    qkv_weight,
    out_weight,
    up_weight,
    down_weight,
    biases,
    up_bias,
    gains,
):
    slots = lengths.shape[0]
    rows, width = tokens.shape
    seq = rows // slots
    heads = width // HEAD_SIZE
    scale = 1.0 / math.sqrt(HEAD_SIZE)
    w_qkv = lax.all_gather(qkv_weight, "fsdp", axis=0, tiled=True)
    w_out = lax.all_gather(out_weight, "fsdp", axis=0, tiled=True)
    w_up = lax.all_gather(up_weight, "fsdp", axis=0, tiled=True)
    w_down = lax.all_gather(down_weight, "fsdp", axis=0, tiled=True)
    bias_rows, bias_up, gain_rows = gather_small(biases, up_bias, gains)

    def split(values):
        return values.reshape(slots, seq, heads, HEAD_SIZE)

    def join(values):
        return values.reshape(rows, width)

    sums = matmul(tokens, w_qkv)
    query = split(low(sums[:, :width] + bias_rows[0]))
    key = split(low(sums[:, width : 2 * width]))
    value = split(low(sums[:, 2 * width :] + bias_rows[1]))
    live = jnp.arange(seq)[None, :] < lengths[:, None]
    scores = scale * jnp.einsum(
        "bshd,bthd->bhst", query, key, preferred_element_type=jnp.float32
    )
    scores = jnp.where(live[:, None, None, :], scores, -1e30)
    exps = jnp.exp(scores - jnp.max(scores, axis=-1, keepdims=True))
    probs = exps / jnp.sum(exps, axis=-1, keepdims=True)
    probs_low = low(probs)
    mixed = low(
        join(jnp.einsum("bhst,bthd->bshd", probs_low, value, preferred_element_type=jnp.float32))
    )
    first, first_inverse = normalize(
        tokens.astype(jnp.float32) + matmul(mixed, w_out) + bias_rows[2]
    )
    first_norm = first * gain_rows[0] + bias_rows[3]
    first_low = low(first_norm)
    inner = matmul(first_low, w_up) + bias_up
    cumulative = 0.5 * (1.0 + lax.erf(inner * math.sqrt(0.5)))
    act_low = low(inner * cumulative)
    slope = low(cumulative + inner * jnp.exp(-0.5 * inner * inner) / math.sqrt(2.0 * math.pi))
    second, second_inverse = normalize(first_norm + matmul(act_low, w_down) + bias_rows[4])
    layer_out = low(second * gain_rows[1] + bias_rows[5])

    grad_out = cotangent * live.reshape(rows, 1).astype(jnp.float32)
    grad_h2 = norm_back(grad_out, second, second_inverse, gain_rows[1])
    grad_branch = low(grad_h2)
    down_grad = reduce_weight(transposed_left(act_low, grad_branch))
    grad_inner = low(transposed_right(grad_branch, w_down) * slope)
    up_grad = reduce_weight(transposed_left(first_low, grad_inner))
    grad_first = grad_h2 + transposed_right(grad_inner, w_up)
    grad_h1 = norm_back(grad_first, first, first_inverse, gain_rows[0])
    grad_attn = low(grad_h1)
    out_grad = reduce_weight(transposed_left(mixed, grad_attn))
    grad_mixed = split(low(transposed_right(grad_attn, w_out)))
    grad_probs = jnp.einsum(
        "bshd,bthd->bhst", grad_mixed, value, preferred_element_type=jnp.float32
    )
    shared = jnp.sum(probs * grad_probs, axis=-1, keepdims=True)
    grad_scores = low(probs * (grad_probs - shared))
    grad_query = scale * jnp.einsum(
        "bhst,bthd->bshd", grad_scores, key, preferred_element_type=jnp.float32
    )
    grad_key = scale * jnp.einsum(
        "bhst,bshd->bthd", grad_scores, query, preferred_element_type=jnp.float32
    )
    grad_value = jnp.einsum(
        "bhst,bshd->bthd", probs_low, grad_mixed, preferred_element_type=jnp.float32
    )
    grad_qkv = jnp.concatenate(
        [join(low(grad_query)), join(low(grad_key)), join(low(grad_value))], axis=1
    )
    qkv_grad = reduce_weight(transposed_left(tokens, grad_qkv))
    token_grad = grad_h1 + transposed_right(grad_qkv, w_qkv)
    small = jnp.stack(
        [
            column_sum(grad_qkv[:, :width]),
            column_sum(grad_qkv[:, 2 * width :]),
            column_sum(grad_attn),
            column_sum(grad_first),
            column_sum(grad_branch),
            column_sum(grad_out),
            column_sum(grad_first * first),
            column_sum(grad_out * second),
        ]
    )
    owner = lax.axis_index("fsdp")
    small, up_sum = lax.psum((small, column_sum(grad_inner)), ("fsdp", "rep"))
    own, own_up = biases.shape[1], up_bias.shape[0]
    small = lax.dynamic_slice(small, (0, owner * own), (8, own))
    up_bias_grad = lax.dynamic_slice(up_sum, (owner * own_up,), (own_up,))
    return (
        layer_out,
        token_grad,
        qkv_grad,
        out_grad,
        up_grad,
        down_grad,
        small[:6],
        up_bias_grad,
        small[6:],
    )


MESH = pl.DeviceIdType.MESH
F32 = jnp.float32
BF16 = jnp.bfloat16
MIB = 1 << 20


def dot_nn(a, b):
    return lax.dot_general(a, b, (((1,), (0,)), ((), ())), preferred_element_type=F32)


def dot_nt(a, b):
    return lax.dot_general(a, b, (((1,), (1,)), ((), ())), preferred_element_type=F32)


def dot_tn(a, b):
    return lax.dot_general(a, b, (((0,), (0,)), ((), ())), preferred_element_type=F32)


class Place:
    def __init__(self):
        f, z = lax.axis_index("fsdp"), lax.axis_index("rep")
        self.f, self.z = f, z
        self.core = lax.rem(f, 2)
        self.x = lax.rem(lax.div(f, 2), 2)
        self.y = lax.div(f, 4)
        self.chip = lax.div(f, 2)
        self.fx = f + 2 - 4 * self.x
        self.fy = f + 4 - 8 * self.y
        self.fd = self.fx + 4 - 8 * self.y
        self.fs = f + 1 - 2 * self.core
        self.par = lax.rem(z, 2)
        self.zn = z + 1 - 2 * self.par

    def dev(self, f=None, z=None):
        return {"fsdp": self.f if f is None else f, "rep": self.z if z is None else z}


def remote(src, dst, send_sem, recv_sem, device):
    return pltpu.make_async_remote_copy(
        src_ref=src, dst_ref=dst, send_sem=send_sem, recv_sem=recv_sem,
        device_id=device, device_id_type=MESH,
    )


UNITS = 4
KINDS = 15


class Gather:
    def __init__(self, place, unit, shard, full, r, split, send, recv):
        self.p, self.unit, self.shard, self.full = place, unit, shard, full
        self.rows = shard.shape[0]
        self.r, self.n = r, self.rows - r
        self.h = split
        self.lo = r * (1 - place.par)
        self.z_out = self.n * (1 - place.par)
        self.z_in = self.n * place.par
        self.send, self.recv = send, recv

    def at(self, f, lo, n):
        return self.full.at[pl.ds(pl.multiple_of(f * self.rows + lo, 16), n)]

    def copy(self, kind, f, lo, n, device, src=None):
        place = self.at(f, lo, n)
        return remote(
            place if src is None else src, place,
            self.send.at[self.unit, kind], self.recv.at[self.unit, kind], device,
        )

    def pieces(self):
        p, lo, n, h, r = self.p, self.lo, self.n, self.h, self.r
        to_x, to_y, to_s = p.dev(f=p.fx), p.dev(f=p.fy), p.dev(f=p.fs)
        to_z = p.dev(z=p.zn)
        sx, sy, sd = (g + 1 - 2 * p.core for g in (p.fx, p.fy, p.fd))
        return {
            0: (p.fx, p.f, lo, lo, n, to_x),
            1: (p.fy, p.f, lo, lo, n, to_y),
            2: (p.fd, p.fx, lo, lo, h, to_y),
            3: (p.fd, p.fy, lo + h, lo + h, n - h, to_x),
            4: (p.fx, p.fx, self.z_in, self.z_out, r, to_z),
            5: (p.fy, p.fy, self.z_in, self.z_out, r, to_z),
            6: (p.fd, p.fd, self.z_in, self.z_out, r, to_z),
            7: (p.fs, p.f, 0, 0, self.rows, to_s),
            8: (sx, p.fx, lo, lo, n, to_s),
            9: (sx, p.fx, self.z_in, self.z_in, r, to_s),
            10: (sy, p.fy, lo, lo, n, to_s),
            11: (sy, p.fy, self.z_in, self.z_in, r, to_s),
            12: (sd, p.fd, lo, lo, h, to_s),
            13: (sd, p.fd, lo + h, lo + h, n - h, to_s),
            14: (sd, p.fd, self.z_in, self.z_in, r, to_s),
        }

    def start(self, *kinds):
        for kind in kinds:
            _, owner, _, lo, n, device = self.pieces()[kind]
            src = None
            if kind in (0, 1, 7):
                src = self.shard.at[pl.ds(pl.multiple_of(lo, 16), n)]
            self.copy(kind, owner, lo, n, device, src).start()

    def got(self, *kinds):
        for kind in kinds:
            owner, _, lo, _, n, device = self.pieces()[kind]
            self.copy(kind, owner, lo, n, device).wait_recv()

    def sent(self):
        for kind in range(KINDS):
            _, owner, _, lo, n, device = self.pieces()[kind]
            self.copy(kind, owner, lo, n, device).wait_send()

    def direct(self, local_sem):
        self.start(0, 1, 7)
        self.local(local_sem).start()

    def local(self, local_sem):
        return pltpu.make_async_copy(self.shard, self.at(self.p.f, 0, self.rows), local_sem)

    def forward(self):
        self.got(0)
        self.start(2, 4, 8)
        self.got(1)
        self.start(3, 5, 10)

    def finish(self):
        self.got(2, 3)
        self.start(6, 12, 13)
        self.got(4)
        self.start(9)
        self.got(5)
        self.start(11)
        self.got(6)
        self.start(14)
        self.got(7, 8, 9, 10, 11, 12, 13, 14)


def forward_kernel(
    lengths, tokens, cot, small, sh_q, sh_o, sh_u, sh_d,
    layer_out, wq_out, wo_out, wu_out, wd_out, qkv_out, slope_out, act_pair, first_pair, mixed_pair,
    tok_pair, branch_pair, norm_out, inv_out, grad_out_ref, params_out, sums_out,
    x, wq, wo, wu, wd, qkv, mixed, norm, first_low, act, slope, acc, cot_v, gh2, out_v, gb, smalls, params,
    inv_v, sums, up_rows,
    ag_send, ag_recv, ag_local, sm_send, sm_recv, sm_local, io, pair_send, pair_recv, pair_local,
):
    p = Place()
    rows, width = x.shape
    slots = lengths.shape[0]
    seq = rows // slots
    others = [lax.rem(p.f + k, 8) for k in range(1, 8)]
    barrier = pltpu.get_barrier_semaphore()
    for g in others:
        pl.semaphore_signal(barrier, inc=1, device_id=p.dev(f=g), device_id_type=MESH)
    pl.semaphore_signal(barrier, inc=1, device_id=p.dev(z=p.zn), device_id_type=MESH)
    loads = [
        pltpu.make_async_copy(tokens, x, io.at[0]),
        pltpu.make_async_copy(cot, cot_v, io.at[1]),
        pltpu.make_async_copy(small, smalls.at[p.f], sm_local),
    ]
    for c in loads:
        c.start()
    pl.semaphore_wait(barrier, 8)

    def small_copy(k, owner, device):
        return remote(small, smalls.at[owner], sm_send.at[k], sm_recv.at[k], device)

    for k, g in enumerate(others):
        small_copy(k, p.f, p.dev(f=g)).start()

    shards = (sh_q, sh_o, sh_u, sh_d)
    fulls = (wq, wo, wu, wd)
    cuts = ((32, 48), (32, 48), (32, 48), (160, 176))
    g_q, g_o, g_u, g_d = (
        Gather(p, u, shards[u], fulls[u], *cuts[u], ag_send, ag_recv) for u in range(UNITS)
    )
    g_q.direct(ag_local.at[0])
    g_o.direct(ag_local.at[1])

    mine = pl.ds(pl.multiple_of(p.core * rows, rows), rows)

    def pair(index, chip, src, dst, cols):
        own = pl.ds(pl.multiple_of((2 * chip + p.core) * cols, cols), cols)
        other = pl.ds(pl.multiple_of((2 * chip + 1 - p.core) * cols, cols), cols)
        here = dst.at[mine, pl.ds(chip * cols, cols)]
        return (
            pltpu.make_async_copy(src.at[:, own], here, pair_local.at[index, chip]),
            remote(src.at[:, other], here, pair_send.at[index, chip], pair_recv.at[index, chip], p.dev(f=p.fs)),
        )

    pairs = []

    def start_pair(index, src, dst, cols, chips=range(4)):
        for chip in chips:
            for c in pair(index, chip, src, dst, cols):
                c.start()
            pairs.append((index, chip, src, dst, cols))

    loads[0].wait()
    start_pair(0, x, tok_pair, 128)
    loads[2].wait()
    for k, g in enumerate(others):
        back = lax.rem(p.f + 7 - k, 8)
        small_copy(k, back, p.dev(f=back)).wait_recv()
    for g in range(8):
        part = smalls[g].astype(F32)
        params[:, g * 128 : (g + 1) * 128] = part
        for j in range(4):
            up_rows[g : g + 1, j * 128 : (j + 1) * 128] = part[8 + j : 9 + j]
    g_q.forward()
    g_o.forward()
    g_u.direct(ag_local.at[2])
    g_q.finish()
    g_q.local(ag_local.at[0]).wait()
    stores = [pltpu.make_async_copy(wq, wq_out, io.at[2])]
    stores[-1].start()
    for j in range(3):
        part = dot_nn(x[...], wq[:, j * width : (j + 1) * width])
        if j == 0:
            part = part + params[0:1]
        if j == 2:
            part = part + params[1:2]
        qkv[:, j * width : (j + 1) * width] = part.astype(BF16)
    stores.append(pltpu.make_async_copy(qkv, qkv_out, io.at[3]))
    stores[-1].start()

    left = lax.broadcasted_iota(jnp.int32, (seq, 128), 1) < HEAD_SIZE
    key_row = lax.broadcasted_iota(jnp.int32, (seq, seq), 0)

    def attend(step, carry):
        slot, pair_of = lax.div(step, 8), lax.rem(step, 8)
        at_rows = pl.ds(pl.multiple_of(slot * seq, seq), seq)
        col = pl.multiple_of(pair_of * 128, 128)
        q = qkv[at_rows, pl.ds(col, 128)]
        k = qkv[at_rows, pl.ds(pl.multiple_of(width + col, 128), 128)]
        v = qkv[at_rows, pl.ds(pl.multiple_of(2 * width + col, 128), 128)]
        dead = key_row >= lengths[slot]
        outs = []
        for head in range(2):
            k_head = jnp.where(left if head == 0 else ~left, k, jnp.zeros_like(k))
            scores = dot_nt(k_head, q) * (1.0 / math.sqrt(HEAD_SIZE))
            scores = jnp.where(dead, -1e30, scores)
            exps = jnp.exp(scores - jnp.max(scores, axis=0, keepdims=True))
            probs = exps * (1.0 / jnp.sum(exps, axis=0, keepdims=True))
            outs.append(dot_tn(probs.astype(BF16), v))
        mixed[at_rows, pl.ds(col, 128)] = jnp.where(left, outs[0], outs[1]).astype(BF16)
        return carry

    lax.fori_loop(0, 8 * slots, attend, 0)
    start_pair(1, mixed, mixed_pair, 128)
    g_o.finish()
    g_o.local(ag_local.at[1]).wait()
    g_u.forward()
    g_d.direct(ag_local.at[3])
    stores.append(pltpu.make_async_copy(wo, wo_out, io.at[4]))
    stores[-1].start()
    hidden = x[...].astype(F32) + dot_nn(mixed[...], wo[...]) + params[2:3]
    center = hidden - row_mean(hidden)
    inverse = lax.rsqrt(row_mean(center * center) + 1e-05)
    norm[...] = center * inverse
    inv_v[...] = jnp.broadcast_to(inverse, inv_v.shape)
    acc[...] = norm[...] * params[6:7] + params[3:4]
    first_low[...] = acc[...].astype(BF16)
    start_pair(2, first_low, first_pair, 128)
    stores.append(pltpu.make_async_copy(norm, norm_out, io.at[5]))
    stores.append(pltpu.make_async_copy(inv_v, inv_out, io.at[6]))
    stores[-1].start()
    stores[-2].start()
    g_u.finish()
    g_u.local(ag_local.at[2]).wait()
    stores.append(pltpu.make_async_copy(wu, wu_out, io.at[7]))
    stores[-1].start()

    def up_step(j, carry):
        cols = pl.ds(pl.multiple_of(j * 512, 512), 512)
        inner = dot_nn(first_low[...], wu[:, cols]) + up_rows[pl.ds(j, 1), :]
        phi = 0.5 * (1.0 + lax.erf(inner * math.sqrt(0.5)))
        act[:, cols] = (inner * phi).astype(BF16)
        density = jnp.exp(-0.5 * inner * inner) * (1.0 / math.sqrt(2.0 * math.pi))
        slope[:, cols] = (phi + inner * density).astype(BF16)
        return carry

    lax.fori_loop(0, 4, up_step, 0)
    g_d.forward()
    start_pair(3, act, act_pair, 512, range(2))
    lax.fori_loop(4, 8, up_step, 0)
    start_pair(3, act, act_pair, 512, range(2, 4))
    stores.append(pltpu.make_async_copy(slope, slope_out, io.at[8]))
    stores[-1].start()
    g_d.finish()
    g_d.local(ag_local.at[3]).wait()
    stores.append(pltpu.make_async_copy(wd, wd_out, io.at[9]))
    stores[-1].start()
    acc[...] += params[4:5]
    for j in range(4):
        acc[...] += dot_nn(act[:, j * 1024 : (j + 1) * 1024], wd[j * 1024 : (j + 1) * 1024, :])
    loads[1].wait()
    hidden = acc[...]
    center = hidden - row_mean(hidden)
    inverse = lax.rsqrt(row_mean(center * center) + 1e-05)
    second = center * inverse
    out_v[...] = (second * params[7:8] + params[5:6]).astype(BF16)
    stores.append(pltpu.make_async_copy(out_v, layer_out, io.at[10]))
    stores[-1].start()
    row_at = lax.broadcasted_iota(jnp.int32, (seq, 1), 0)
    live = jnp.concatenate([(row_at < lengths[s]).astype(F32) for s in range(slots)], axis=0)
    e = cot_v[...] * live
    sums[...] = jnp.zeros_like(sums)
    sums[0:1] = jnp.sum(e * second, axis=0, keepdims=True)
    sums[1:2] = jnp.sum(e, axis=0, keepdims=True)
    scaled = e * params[7:8]
    gh2[...] = inverse * (scaled - row_mean(scaled) - second * row_mean(scaled * second))
    gb[...] = gh2[...].astype(BF16)
    c_local = pltpu.make_async_copy(gb, branch_pair.at[mine], pair_local.at[4, 0])
    c_remote = remote(gb, branch_pair.at[mine], pair_send.at[4, 0], pair_recv.at[4, 0], p.dev(f=p.fs))
    c_local.start()
    c_remote.start()
    sums[2:3] = jnp.sum(gb[...].astype(F32), axis=0, keepdims=True)
    stores.append(pltpu.make_async_copy(gh2, grad_out_ref, io.at[11]))
    stores.append(pltpu.make_async_copy(params, params_out, io.at[12]))
    stores.append(pltpu.make_async_copy(sums, sums_out, io.at[13]))
    for c in stores[-3:]:
        c.start()
    for c in stores:
        c.wait()
    c_local.wait()
    c_remote.wait()
    for args in pairs:
        a, b = pair(*args)
        a.wait()
        b.wait()
    for k, g in enumerate(others):
        small_copy(k, p.f, p.dev(f=g)).wait_send()
    for g in (g_q, g_o, g_u, g_d):
        g.sent()


def forward_call(tokens, lengths, cotangent, qkv_w, out_w, up_w, down_w, small):
    rows, width = tokens.shape
    ff = up_w.shape[1]
    anyspace = pl.BlockSpec(memory_space=pl.ANY)
    shape = jax.ShapeDtypeStruct
    outs = [
        shape((rows, width), BF16),
        shape((width, 3 * width), BF16),
        shape((width, width), BF16),
        shape((width, ff), BF16),
        shape((ff, width), BF16),
        shape((rows, 3 * width), BF16),
        shape((rows, ff), BF16),
        shape((2 * rows, ff // 2), BF16),
        shape((2 * rows, width // 2), BF16),
        shape((2 * rows, width // 2), BF16),
        shape((2 * rows, width // 2), BF16),
        shape((2 * rows, width), BF16),
        shape((rows, width), F32),
        shape((rows, 128), F32),
        shape((rows, width), F32),
        shape((16, width), F32),
        shape((8, width), F32),
    ]
    dma = pltpu.SemaphoreType.DMA
    scratch = [
        pltpu.VMEM((rows, width), BF16),
        pltpu.VMEM((width, 3 * width), BF16),
        pltpu.VMEM((width, width), BF16),
        pltpu.VMEM((width, ff), BF16),
        pltpu.VMEM((ff, width), BF16),
        pltpu.VMEM((rows, 3 * width), BF16),
        pltpu.VMEM((rows, width), BF16),
        pltpu.VMEM((rows, width), F32),
        pltpu.VMEM((rows, width), BF16),
        pltpu.VMEM((rows, ff), BF16),
        pltpu.VMEM((rows, ff), BF16),
        pltpu.VMEM((rows, width), F32),
        pltpu.VMEM((rows, width), F32),
        pltpu.VMEM((rows, width), F32),
        pltpu.VMEM((rows, width), BF16),
        pltpu.VMEM((rows, width), BF16),
        pltpu.VMEM((8, 16, 128), BF16),
        pltpu.VMEM((16, width), F32),
        pltpu.VMEM((rows, 128), F32),
        pltpu.VMEM((8, width), F32),
        pltpu.VMEM((8, ff // 8), F32),
        dma((UNITS, KINDS)),
        dma((UNITS, KINDS)),
        dma((UNITS,)),
        dma((7,)),
        dma((7,)),
        dma,
        dma((14,)),
        dma((5, 4)),
        dma((5, 4)),
        dma((5, 4)),
    ]
    return pl.pallas_call(
        forward_kernel,
        out_shape=outs,
        in_specs=[pl.BlockSpec(memory_space=pltpu.SMEM)] + [anyspace] * 7,
        out_specs=[anyspace] * len(outs),
        scratch_shapes=scratch,
        name="forward",
        cost_estimate=pl.CostEstimate(flops=2 * 512 * 12582912, bytes_accessed=60 * MIB, transcendentals=4 * MIB),
        compiler_params=pltpu.CompilerParams(
            collective_id=0, has_side_effects=True, vmem_limit_bytes=60 * MIB
        ),
    )(lengths, tokens, cotangent, small, qkv_w, out_w, up_w, down_w)


def pack_small(biases, up_bias, gains):
    return jnp.concatenate([biases, gains, up_bias.reshape(4, 128), jnp.zeros((4, 128), BF16)], axis=0)


BLOCKS = 12
S1X, S1Y, S2X, S2Y, Z1, Z2, FM, FE, FF = range(9)


class Reduce:
    def __init__(self, place, prod, got_x, got_y, end_x, end_y, from_end, from_mid, out_at, send, recv, local):
        self.p = place
        self.prod, self.got_x, self.got_y, self.end_x, self.end_y = prod, got_x, got_y, end_x, end_y
        self.from_end, self.from_mid, self.out_at = from_end, from_mid, out_at
        self.send, self.recv, self.local = send, recv, local
        z = place.z
        self.mid = 1 + lax.div(z, 2)
        self.end = 3 * lax.div(z, 2)
        self.is_mid = z == self.mid
        self.is_end = z == self.end
        self.keep = pl.multiple_of(64 * (self.mid - 1), 64)
        self.give = pl.multiple_of(64 * (2 - self.mid), 64)

    def copy(self, kind, b, sending=True):
        p = self.p
        x, y, xn, yn = p.x, p.y, 1 - p.x, 1 - p.y
        top, low_half = pl.ds(0, 64), pl.ds(64, 64)
        if kind == S1X:
            src, dst, dev = self.prod.at[b, :, xn, top], self.got_x.at[b], p.dev(f=p.fx)
        elif kind == S1Y:
            src, dst, dev = self.prod.at[b, yn, :, low_half], self.got_y.at[b], p.dev(f=p.fy)
        elif kind == S2Y:
            src, dst, dev = self.prod.at[b, yn, x, top], self.end_y.at[b], p.dev(f=p.fy)
        elif kind == S2X:
            src, dst, dev = self.prod.at[b, y, xn, low_half], self.end_x.at[b], p.dev(f=p.fx)
        elif kind == Z1:
            src, dst, dev = self.prod.at[b, y, x], self.from_end.at[b], p.dev(z=self.mid)
        elif kind == Z2:
            src, dst, dev = self.prod.at[b, y, x, pl.ds(self.give, 64)], self.from_mid.at[b], p.dev(z=3 - self.mid)
        elif kind == FM:
            lo = self.keep if sending else self.give
            src, dst, dev = self.prod.at[b, y, x, pl.ds(self.keep, 64)], self.out_at(b, lo), p.dev(z=3 - self.mid)
        elif kind == FE:
            src, dst, dev = self.prod.at[b, y, x, pl.ds(self.keep, 64)], self.out_at(b, self.keep), p.dev(z=self.end)
        else:
            src, dst, dev = self.out_at(b, self.give), self.out_at(b, self.give), p.dev(z=self.end)
        return remote(src, dst, self.send.at[kind, b], self.recv.at[kind, b], dev)

    def begin(self, b):
        self.copy(S1X, b).start()
        self.copy(S1Y, b).start()

    def second(self, b):
        x, y = self.p.x, self.p.y
        self.copy(S1X, b).wait_recv()
        self.prod[b, :, x, 0:64] = self.prod[b, :, x, 0:64] + self.got_x[b]
        self.copy(S2Y, b).start()
        self.copy(S1Y, b).wait_recv()
        self.prod[b, y, :, 64:128] = self.prod[b, y, :, 64:128] + self.got_y[b]
        self.copy(S2X, b).start()

    def along(self, b):
        x, y = self.p.x, self.p.y
        self.copy(S2Y, b).wait_recv()
        self.copy(S2X, b).wait_recv()

        @pl.when(self.is_end)
        def _():
            self.prod[b, y, x, 0:64] = self.prod[b, y, x, 0:64] + self.end_y[b]
            self.prod[b, y, x, 64:128] = self.prod[b, y, x, 64:128] + self.end_x[b]
            self.copy(Z1, b).start()

        @pl.when(self.is_mid)
        def _():
            self.copy(Z1, b).wait_recv()
            for lo, other in ((0, self.end_y), (64, self.end_x)):
                total = self.prod[b, y, x, lo : lo + 64].astype(F32) + other[b].astype(F32)
                total = total + self.from_end[b, lo : lo + 64].astype(F32)
                self.prod[b, y, x, lo : lo + 64] = total.astype(BF16)
            self.copy(Z2, b).start()

    def write(self, b):
        return pltpu.make_async_copy(
            self.prod.at[b, self.p.y, self.p.x, pl.ds(self.keep, 64)], self.out_at(b, self.keep), self.local.at[b]
        )

    def hand_out(self, b):
        x, y = self.p.x, self.p.y

        @pl.when(self.is_mid)
        def _():
            self.copy(Z2, b).wait_recv()
            here = pl.ds(self.keep, 64)
            self.prod[b, y, x, here] = self.prod[b, y, x, here] + self.from_mid[b]
            self.copy(FE, b).start()
            self.copy(FM, b).start()
            self.write(b).start()

    def pass_on(self, b):
        @pl.when(self.is_mid)
        def _():
            self.copy(FM, b, False).wait_recv()
            self.copy(FF, b).start()

    def tick(self, k):
        for lag, step in enumerate((self.second, self.along, self.hand_out, self.pass_on)):
            if 0 <= k - lag < BLOCKS:
                step(k - lag)

    def close(self, b):
        for kind in (S1X, S1Y, S2X, S2Y):
            self.copy(kind, b).wait_send()

        @pl.when(self.is_end)
        def _():
            self.copy(Z1, b).wait_send()
            self.copy(FE, b).wait_recv()
            self.copy(FF, b).wait_recv()

        @pl.when(self.is_mid)
        def _():
            for kind in (Z2, FM, FE, FF):
                self.copy(kind, b).wait_send()
            self.write(b).wait()


def backward_kernel(
    lengths, wq, wo, wu, wd, qkv, slope, act_pair, first_pair, mixed_pair, tok_pair, branch_pair,
    norm_in, inv_in, gh2, params_in, sums_in,
    token_grad, out_q, out_o, out_u, out_d, small_out,
    lhs, wbuf, slope_v, branch, gi, gq, gm, gh, norm, inv, params, sums_v, upsum,
    prod, got_x, got_y, end_x, end_y, from_end, from_mid,
    s_send, s_got, s_total, s_all, s_out,
    rs_send, rs_recv, rs_local, pair_send, pair_recv, load_sem, lhs_sem, w_sem, slope_sem,
    sm_send, sm_recv, smz_send, smz_recv, store_sem,
):
    p = Place()
    rows, width = gh.shape
    slots = lengths.shape[0]
    seq = rows // slots
    planes = [lax.rem(p.f + k, 8) for k in range(1, 8)]
    levels = [lax.rem(p.z + k, 4) for k in range(1, 4)]
    barrier = pltpu.get_barrier_semaphore()
    for g in planes:
        pl.semaphore_signal(barrier, inc=1, device_id=p.dev(f=g), device_id_type=MESH)
    for g in levels:
        pl.semaphore_signal(barrier, inc=1, device_id=p.dev(z=g), device_id_type=MESH)

    mine = pl.ds(pl.multiple_of(p.core * rows, rows), rows)

    def lhs_copies(i):
        if i < 4:
            return [
                pltpu.make_async_copy(
                    act_pair.at[:, pl.ds(chip * 512 + i * 128, 128)],
                    lhs.at[i % 2, :, pl.ds(chip * 128, 128)],
                    lhs_sem.at[i, chip],
                )
                for chip in range(4)
            ]
        src = (first_pair, mixed_pair, tok_pair)[i - 4]
        return [pltpu.make_async_copy(src, lhs.at[i % 2], lhs_sem.at[i, 0])]

    def w_copy(i):
        if i < 8:
            j = i // 2
            src = wu.at[:, pl.ds(j * 1024, 1024)] if i % 2 else wd.at[pl.ds(j * 1024, 1024)]
        elif i == 8:
            src = wo
        else:
            src = wq.at[:, pl.ds((i - 9) * 1024, 1024)]
        return pltpu.make_async_copy(src, wbuf.at[i % 2], w_sem.at[i])

    def slope_copy(j):
        return pltpu.make_async_copy(slope.at[:, pl.ds(j * 1024, 1024)], slope_v.at[j % 2], slope_sem.at[j])

    loads = [
        pltpu.make_async_copy(src, dst, load_sem.at[i])
        for i, (src, dst) in enumerate(
            (
                (branch_pair, branch), (gh2, gh), (qkv, gq.at[mine]), (norm_in, norm), (inv_in, inv),
                (params_in, params), (sums_in, sums_v),
            )
        )
    ]
    for c in lhs_copies(0):
        c.start()
    loads[0].start()
    for c in lhs_copies(1):
        c.start()
    w_copy(0).start()
    slope_copy(0).start()
    for c in loads[1:]:
        c.start()

    def out_at(b, lo):
        if b < 4:
            return out_d.at[pl.ds(pl.multiple_of(128 * b + lo, 16), 64)]
        if b < 8:
            return out_u.at[pl.ds(lo, 64), pl.ds((b - 4) * 1024, 1024)]
        if b == 8:
            return out_o.at[pl.ds(lo, 64)]
        return out_q.at[pl.ds(lo, 64), pl.ds((b - 9) * 1024, 1024)]

    red = Reduce(p, prod, got_x, got_y, end_x, end_y, from_end, from_mid, out_at, rs_send, rs_recv, rs_local)

    def produce(b, left, right):
        prod[b] = dot_tn(left, right).astype(BF16).reshape(2, 2, 128, 1024)
        red.begin(b)

    def to_pair(index, ref, cols):
        here = ref.at[mine, cols]
        return remote(here, here, pair_send.at[index], pair_recv.at[index], p.dev(f=p.fs))

    pl.semaphore_wait(barrier, 10)
    loads[0].wait()
    for b in range(4):
        for c in lhs_copies(b):
            c.wait()
        produce(b, lhs[b % 2], branch[...])
        for c in lhs_copies(b + 2) if b < 4 else ():
            c.start()
    loads[1].wait()

    def block_cols(j):
        return pl.ds(j * 1024, 1024)

    def up_block(j):
        to_pair(j, gi, block_cols(j)).wait_recv()
        produce(4 + j, lhs[0], gi[:, j * 1024 : (j + 1) * 1024])

    for j in range(4):
        w_copy(2 * j).wait()
        w_copy(2 * j + 1).start()
        slope_copy(j).wait()
        if j < 3:
            slope_copy(j + 1).start()
        inner = (dot_nt(branch[mine], wbuf[0]) * slope_v[j % 2].astype(F32)).astype(BF16)
        gi[mine, j * 1024 : (j + 1) * 1024] = inner
        to_pair(j, gi, block_cols(j)).start()
        upsum[j : j + 1] = jnp.sum(inner.astype(F32), axis=0, keepdims=True)
        w_copy(2 * j + 1).wait()
        w_copy(2 * j + 2).start()
        gh[...] += dot_nt(gi[mine, j * 1024 : (j + 1) * 1024], wbuf[1])
        if j == 0:
            for c in lhs_copies(4):
                c.wait()
        if j > 0:
            up_block(j - 1)
            red.tick(j - 1)
    for c in loads[2:]:
        c.wait()
    ga = branch
    e = gh[...]
    scaled = e * params[6:7]
    n = norm[...]
    sums_v[3:4] = jnp.sum(e, axis=0, keepdims=True)
    sums_v[4:5] = jnp.sum(e * n, axis=0, keepdims=True)
    gh[...] = inv[:, 0:1] * (scaled - row_mean(scaled) - n * row_mean(scaled * n))
    ga[mine] = gh[...].astype(BF16)
    whole = pl.ds(0, 1024)
    to_pair(4, ga, whole).start()
    sums_v[5:6] = jnp.sum(ga[mine].astype(F32), axis=0, keepdims=True)
    up_block(3)
    for c in lhs_copies(6):
        c.start()
    w_copy(8).wait()
    w_copy(9).start()
    gm[...] = dot_nt(ga[mine], wbuf[0]).astype(BF16)
    w_copy(10).start()
    for c in lhs_copies(5):
        c.wait()
    to_pair(4, ga, whole).wait_recv()
    produce(8, lhs[1], ga[...])
    red.tick(3)

    left = lax.broadcasted_iota(jnp.int32, (seq, 128), 1) < HEAD_SIZE
    key_row = lax.broadcasted_iota(jnp.int32, (seq, seq), 0)
    scale = 1.0 / math.sqrt(HEAD_SIZE)

    def attend(step, carry):
        slot, pair_of = lax.rem(step, slots), lax.div(step, slots)
        at_rows = pl.ds(pl.multiple_of(slot * seq, seq), seq)
        own_rows = pl.ds(pl.multiple_of(p.core * rows + slot * seq, seq), seq)
        col = pl.multiple_of(pair_of * 128, 128)
        at_q = pl.ds(col, 128)
        at_k = pl.ds(pl.multiple_of(width + col, 128), 128)
        at_v = pl.ds(pl.multiple_of(2 * width + col, 128), 128)
        q, k, v = gq[own_rows, at_q], gq[own_rows, at_k], gq[own_rows, at_v]
        do = gm[at_rows, at_q]
        dead = key_row >= lengths[slot]
        parts = []
        for head in range(2):
            lanes = left if head == 0 else ~left
            k_head = jnp.where(lanes, k, jnp.zeros_like(k))
            v_head = jnp.where(lanes, v, jnp.zeros_like(v))
            scores = jnp.where(dead, -1e30, dot_nt(k_head, q) * scale)
            exps = jnp.exp(scores - jnp.max(scores, axis=0, keepdims=True))
            probs = exps * (1.0 / jnp.sum(exps, axis=0, keepdims=True))
            d_probs = dot_nt(v_head, do)
            shared = jnp.sum(probs * d_probs, axis=0, keepdims=True)
            d_scores = (probs * (d_probs - shared)).astype(BF16)
            parts.append(
                (dot_tn(d_scores, k) * scale, dot_nn(d_scores, q) * scale, dot_nn(probs.astype(BF16), do))
            )
        for at, one, two in zip((at_q, at_k, at_v), *parts):
            gq[own_rows, at] = jnp.where(left, one, two).astype(BF16)
        return carry

    steps = 8 * slots
    for quarter in range(4):
        lax.fori_loop(quarter * steps // 4, (quarter + 1) * steps // 4, attend, 0)
        if quarter % 2:
            for j in range(3):
                to_pair(5 + 3 * (quarter // 2) + j, gq, pl.ds(j * 1024 + 512 * (quarter // 2), 512)).start()
        red.tick(4 + quarter)
    for c in lhs_copies(6):
        c.wait()
    for j in range(3):
        for half in range(2):
            to_pair(5 + 3 * half + j, gq, pl.ds(j * 1024 + 512 * half, 512)).wait_recv()
        produce(9 + j, lhs[0], gq[:, j * 1024 : (j + 1) * 1024])
    sums_v[6:7] = jnp.sum(gq[mine, 0:1024].astype(F32), axis=0, keepdims=True)
    sums_v[7:8] = jnp.sum(gq[mine, 2048:3072].astype(F32), axis=0, keepdims=True)

    order = (6, 7, 5, 3, 2, 1, 4, 0)
    for g in range(8):
        cols = slice(g * 128, (g + 1) * 128)
        for i, row in enumerate(order):
            s_send[g, i : i + 1] = sums_v[row : row + 1, cols]
        for i in range(4):
            lo = (g % 2) * 512 + i * 128
            s_send[g, 8 + i : 9 + i] = upsum[g // 2 : g // 2 + 1, lo : lo + 128]

    def small_to(k):
        g = planes[k]
        return remote(s_send.at[g], s_got.at[p.f], sm_send.at[k], sm_recv.at[k], p.dev(f=g))

    def small_from(k):
        g = lax.rem(p.f + 7 - k, 8)
        return remote(s_send.at[g], s_got.at[g], sm_send.at[k], sm_recv.at[k], p.dev(f=g))

    def level_to(k):
        return remote(s_total, s_all.at[p.z], smz_send.at[k], smz_recv.at[k], p.dev(z=levels[k]))

    def level_from(k):
        g = lax.rem(p.z + 3 - k, 4)
        return remote(s_total, s_all.at[g], smz_send.at[k], smz_recv.at[k], p.dev(z=g))

    for k in range(7):
        small_to(k).start()
    s_got[p.f] = s_send[p.f]

    for j in range(3):
        w_copy(9 + j).wait()
        gh[...] += dot_nt(gq[mine, j * 1024 : (j + 1) * 1024], wbuf[(9 + j) % 2])
        if j == 0:
            w_copy(11).start()
    store = pltpu.make_async_copy(gh, token_grad, store_sem.at[0])
    store.start()
    red.tick(8)
    for k in range(7):
        small_from(k).wait_recv()
    total = s_got[0]
    for g in range(1, 8):
        total = total + s_got[g]
    s_total[...] = total
    for k in range(3):
        level_to(k).start()
    s_all[p.z] = total
    for k in range(9, BLOCKS + 3):
        red.tick(k)
    for k in range(3):
        level_from(k).wait_recv()
    s_out[...] = (s_all[0] + s_all[1]) + (s_all[2] + s_all[3])
    small_store = pltpu.make_async_copy(s_out, small_out, store_sem.at[1])
    small_store.start()
    for b in range(BLOCKS):
        red.close(b)
    for k in range(7):
        small_to(k).wait_send()
    for k in range(3):
        level_to(k).wait_send()
    for j in range(4):
        to_pair(j, gi, block_cols(j)).wait_send()
    to_pair(4, ga, whole).wait_send()
    for j in range(3):
        for half in range(2):
            to_pair(5 + 3 * half + j, gq, pl.ds(j * 1024 + 512 * half, 512)).wait_send()
    store.wait()
    small_store.wait()


def backward_call(lengths, saved):
    wq, wo, wu, wd, qkv, slope = saved[:6]
    rows, width = qkv.shape[0], wo.shape[0]
    ff = wu.shape[1]
    anyspace = pl.BlockSpec(memory_space=pl.ANY)
    shape = jax.ShapeDtypeStruct
    dma = pltpu.SemaphoreType.DMA
    outs = [
        shape((rows, width), F32),
        shape((width // 8, 3 * width), BF16),
        shape((width // 8, width), BF16),
        shape((width // 8, ff), BF16),
        shape((ff // 8, width), BF16),
        shape((16, 128), F32),
    ]
    scratch = [
        pltpu.VMEM((2, 2 * rows, 512), BF16),
        pltpu.VMEM((2, 1024, 1024), BF16),
        pltpu.VMEM((2, rows, 1024), BF16),
        pltpu.VMEM((2 * rows, width), BF16),
        pltpu.VMEM((2 * rows, ff), BF16),
        pltpu.VMEM((2 * rows, 3 * width), BF16),
        pltpu.VMEM((rows, width), BF16),
        pltpu.VMEM((rows, width), F32),
        pltpu.VMEM((rows, width), F32),
        pltpu.VMEM((rows, 128), F32),
        pltpu.VMEM((16, width), F32),
        pltpu.VMEM((8, width), F32),
        pltpu.VMEM((4, width), F32),
        pltpu.VMEM((BLOCKS, 2, 2, 128, 1024), BF16),
        pltpu.VMEM((BLOCKS, 2, 64, 1024), BF16),
        pltpu.VMEM((BLOCKS, 2, 64, 1024), BF16),
        pltpu.VMEM((BLOCKS, 64, 1024), BF16),
        pltpu.VMEM((BLOCKS, 64, 1024), BF16),
        pltpu.VMEM((BLOCKS, 128, 1024), BF16),
        pltpu.VMEM((BLOCKS, 64, 1024), BF16),
        pltpu.VMEM((8, 16, 128), F32),
        pltpu.VMEM((8, 16, 128), F32),
        pltpu.VMEM((16, 128), F32),
        pltpu.VMEM((4, 16, 128), F32),
        pltpu.VMEM((16, 128), F32),
        dma((9, BLOCKS)),
        dma((9, BLOCKS)),
        dma((BLOCKS,)),
        dma((11,)),
        dma((11,)),
        dma((7,)),
        dma((7, 4)),
        dma((12,)),
        dma((4,)),
        dma((7,)),
        dma((7,)),
        dma((3,)),
        dma((3,)),
        dma((2,)),
    ]
    return pl.pallas_call(
        backward_kernel,
        out_shape=outs,
        in_specs=[pl.BlockSpec(memory_space=pltpu.SMEM)] + [anyspace] * len(saved),
        out_specs=[anyspace] * len(outs),
        scratch_shapes=scratch,
        name="backward",
        cost_estimate=pl.CostEstimate(flops=4 * 512 * 12582912, bytes_accessed=60 * MIB, transcendentals=4 * MIB),
        compiler_params=pltpu.CompilerParams(
            collective_id=1, has_side_effects=True, vmem_limit_bytes=60 * MIB
        ),
    )(lengths, *saved)


def plane(
    tokens,
    lengths,
    cotangent,
    qkv_weight,
    out_weight,
    up_weight,
    down_weight,
    biases,
    up_bias,
    gains,
):
    small_in = pack_small(biases, up_bias, gains)
    layer_out, *saved = forward_call(
        tokens, lengths, cotangent, qkv_weight, out_weight, up_weight, down_weight, small_in
    )
    token_grad, *weight_grads, small = backward_call(lengths, saved)
    return (
        layer_out,
        token_grad,
        *(grad.astype(F32) for grad in weight_grads),
        small[:6],
        small[8:12].reshape(-1),
        small[6:8],
    )


def solution(mesh):
    step = plane if dict(mesh.shape) == {"fsdp": 8, "rep": 4} else portable
    both = ("fsdp", "rep")
    in_specs = (
        P(both, None),
        P(both),
        P(both, None),
        P("fsdp", None),
        P("fsdp", None),
        P("fsdp", None),
        P("fsdp", None),
        P(None, "fsdp"),
        P("fsdp"),
        P(None, "fsdp"),
    )
    out_specs = (
        P(both, None),
        P(both, None),
        P("fsdp", None),
        P("fsdp", None),
        P("fsdp", None),
        P("fsdp", None),
        P(None, "fsdp"),
        P("fsdp"),
        P(None, "fsdp"),
    )
    return jax.shard_map(
        step, mesh=mesh, in_specs=in_specs, out_specs=out_specs, check_vma=False
    )
```

```python
import math

import jax
import jax.numpy as jnp
from jax import lax
from jax.experimental import pallas as pl
from jax.experimental.pallas import tpu as pltpu
from jax.sharding import PartitionSpec as P

HEAD_SIZE = 64


def matmul(left_side, right_side):
    return jnp.dot(left_side, right_side, preferred_element_type=jnp.float32)


def transposed_left(left_side, right_side):
    return lax.dot_general(
        left_side, right_side, (((0,), (0,)), ((), ())), preferred_element_type=jnp.float32
    )


def transposed_right(left_side, right_side):
    return lax.dot_general(
        left_side, right_side, (((1,), (1,)), ((), ())), preferred_element_type=jnp.float32
    )


def column_sum(values):
    return jnp.sum(values.astype(jnp.float32), axis=0)


def row_mean(values):
    return jnp.mean(values, axis=-1, keepdims=True)


def normalize(hidden):
    center = hidden - row_mean(hidden)
    inverse = lax.rsqrt(row_mean(center * center) + 1e-05)
    return center * inverse, inverse


def norm_back(grad, norm, inverse, gain):
    scaled = grad * gain
    return inverse * (scaled - row_mean(scaled) - norm * row_mean(scaled * norm))


def low(values):
    return values.astype(jnp.bfloat16)


def gather_small(biases, up_bias, gains):
    width, up_width = biases.shape[1], up_bias.shape[0]
    packed = jnp.concatenate([biases.reshape(-1), gains.reshape(-1), up_bias])
    everyone = lax.all_gather(packed, "fsdp", axis=0, tiled=False).astype(jnp.float32)
    rows = everyone[:, : 8 * width].reshape(-1, 8, width).transpose(1, 0, 2).reshape(8, -1)
    return rows[:6], everyone[:, 8 * width : 8 * width + up_width].reshape(-1), rows[6:]


def reduce_weight(grad):
    shard = lax.psum_scatter(low(grad), "fsdp", scatter_dimension=0, tiled=True)
    return lax.psum(shard, "rep").astype(jnp.float32)


def portable(
    tokens,
    lengths,
    cotangent,
    qkv_weight,
    out_weight,
    up_weight,
    down_weight,
    biases,
    up_bias,
    gains,
):
    slots = lengths.shape[0]
    rows, width = tokens.shape
    seq = rows // slots
    heads = width // HEAD_SIZE
    scale = 1.0 / math.sqrt(HEAD_SIZE)
    w_qkv = lax.all_gather(qkv_weight, "fsdp", axis=0, tiled=True)
    w_out = lax.all_gather(out_weight, "fsdp", axis=0, tiled=True)
    w_up = lax.all_gather(up_weight, "fsdp", axis=0, tiled=True)
    w_down = lax.all_gather(down_weight, "fsdp", axis=0, tiled=True)
    bias_rows, bias_up, gain_rows = gather_small(biases, up_bias, gains)

    def split(values):
        return values.reshape(slots, seq, heads, HEAD_SIZE)

    def join(values):
        return values.reshape(rows, width)

    sums = matmul(tokens, w_qkv)
    query = split(low(sums[:, :width] + bias_rows[0]))
    key = split(low(sums[:, width : 2 * width]))
    value = split(low(sums[:, 2 * width :] + bias_rows[1]))
    live = jnp.arange(seq)[None, :] < lengths[:, None]
    scores = scale * jnp.einsum(
        "bshd,bthd->bhst", query, key, preferred_element_type=jnp.float32
    )
    scores = jnp.where(live[:, None, None, :], scores, -1e30)
    exps = jnp.exp(scores - jnp.max(scores, axis=-1, keepdims=True))
    probs = exps / jnp.sum(exps, axis=-1, keepdims=True)
    probs_low = low(probs)
    mixed = low(
        join(jnp.einsum("bhst,bthd->bshd", probs_low, value, preferred_element_type=jnp.float32))
    )
    first, first_inverse = normalize(
        tokens.astype(jnp.float32) + matmul(mixed, w_out) + bias_rows[2]
    )
    first_norm = first * gain_rows[0] + bias_rows[3]
    first_low = low(first_norm)
    inner = matmul(first_low, w_up) + bias_up
    cumulative = 0.5 * (1.0 + lax.erf(inner * math.sqrt(0.5)))
    act_low = low(inner * cumulative)
    slope = low(cumulative + inner * jnp.exp(-0.5 * inner * inner) / math.sqrt(2.0 * math.pi))
    second, second_inverse = normalize(first_norm + matmul(act_low, w_down) + bias_rows[4])
    layer_out = low(second * gain_rows[1] + bias_rows[5])

    grad_out = cotangent * live.reshape(rows, 1).astype(jnp.float32)
    grad_h2 = norm_back(grad_out, second, second_inverse, gain_rows[1])
    grad_branch = low(grad_h2)
    down_grad = reduce_weight(transposed_left(act_low, grad_branch))
    grad_inner = low(transposed_right(grad_branch, w_down) * slope)
    up_grad = reduce_weight(transposed_left(first_low, grad_inner))
    grad_first = grad_h2 + transposed_right(grad_inner, w_up)
    grad_h1 = norm_back(grad_first, first, first_inverse, gain_rows[0])
    grad_attn = low(grad_h1)
    out_grad = reduce_weight(transposed_left(mixed, grad_attn))
    grad_mixed = split(low(transposed_right(grad_attn, w_out)))
    grad_probs = jnp.einsum(
        "bshd,bthd->bhst", grad_mixed, value, preferred_element_type=jnp.float32
    )
    shared = jnp.sum(probs * grad_probs, axis=-1, keepdims=True)
    grad_scores = low(probs * (grad_probs - shared))
    grad_query = scale * jnp.einsum(
        "bhst,bthd->bshd", grad_scores, key, preferred_element_type=jnp.float32
    )
    grad_key = scale * jnp.einsum(
        "bhst,bshd->bthd", grad_scores, query, preferred_element_type=jnp.float32
    )
    grad_value = jnp.einsum(
        "bhst,bshd->bthd", probs_low, grad_mixed, preferred_element_type=jnp.float32
    )
    grad_qkv = jnp.concatenate(
        [join(low(grad_query)), join(low(grad_key)), join(low(grad_value))], axis=1
    )
    qkv_grad = reduce_weight(transposed_left(tokens, grad_qkv))
    token_grad = grad_h1 + transposed_right(grad_qkv, w_qkv)
    small = jnp.stack(
        [
            column_sum(grad_qkv[:, :width]),
            column_sum(grad_qkv[:, 2 * width :]),
            column_sum(grad_attn),
            column_sum(grad_first),
            column_sum(grad_branch),
            column_sum(grad_out),
            column_sum(grad_first * first),
            column_sum(grad_out * second),
        ]
    )
    owner = lax.axis_index("fsdp")
    small, up_sum = lax.psum((small, column_sum(grad_inner)), ("fsdp", "rep"))
    own, own_up = biases.shape[1], up_bias.shape[0]
    small = lax.dynamic_slice(small, (0, owner * own), (8, own))
    up_bias_grad = lax.dynamic_slice(up_sum, (owner * own_up,), (own_up,))
    return (
        layer_out,
        token_grad,
        qkv_grad,
        out_grad,
        up_grad,
        down_grad,
        small[:6],
        up_bias_grad,
        small[6:],
    )


MESH = pl.DeviceIdType.MESH
F32 = jnp.float32
BF16 = jnp.bfloat16
MIB = 1 << 20


def dot_nn(a, b):
    return lax.dot_general(a, b, (((1,), (0,)), ((), ())), preferred_element_type=F32)


def dot_nt(a, b):
    return lax.dot_general(a, b, (((1,), (1,)), ((), ())), preferred_element_type=F32)


def dot_tn(a, b):
    return lax.dot_general(a, b, (((0,), (0,)), ((), ())), preferred_element_type=F32)


class Place:
    def __init__(self):
        f, z = lax.axis_index("fsdp"), lax.axis_index("rep")
        self.f, self.z = f, z
        self.core = lax.rem(f, 2)
        self.x = lax.rem(lax.div(f, 2), 2)
        self.y = lax.div(f, 4)
        self.chip = lax.div(f, 2)
        self.fx = f + 2 - 4 * self.x
        self.fy = f + 4 - 8 * self.y
        self.fd = self.fx + 4 - 8 * self.y
        self.fs = f + 1 - 2 * self.core
        self.par = lax.rem(z, 2)
        self.zn = z + 1 - 2 * self.par

    def dev(self, f=None, z=None):
        return {"fsdp": self.f if f is None else f, "rep": self.z if z is None else z}


def remote(src, dst, send_sem, recv_sem, device):
    return pltpu.make_async_remote_copy(
        src_ref=src, dst_ref=dst, send_sem=send_sem, recv_sem=recv_sem,
        device_id=device, device_id_type=MESH,
    )


UNITS = 6
KINDS = 13


class Gather:
    def __init__(self, place, unit, shard, full, base, rows, send, recv, local):
        self.p, self.unit, self.shard, self.full = place, unit, shard, full
        self.base, self.rows, self.size = base, rows, shard.shape[0]
        self.send_sem, self.recv_sem, self.local_sem = send, recv, local
        p, half = place, rows // 2
        one, two = half * p.par, half * (1 - p.par)
        to_x, to_y, to_s, to_z = p.dev(f=p.fx), p.dev(f=p.fy), p.dev(f=p.fs), p.dev(z=p.zn)
        sx, sy, sd = (g + 1 - 2 * p.core for g in (p.fx, p.fy, p.fd))
        self.table = (
            ((p.fx, one), (p.f, one), half, to_x),
            ((p.fy, two), (p.f, two), half, to_y),
            ((p.fx, two), (p.fx, one), half, to_z),
            ((p.fy, one), (p.fy, two), half, to_z),
            ((p.fd, one), (p.fx, one), half, to_y),
            ((p.fd, two), (p.fy, two), half, to_x),
            ((p.fs, 0), (p.f, 0), rows, to_s),
            ((sx, one), (p.fx, one), half, to_s),
            ((sy, two), (p.fy, two), half, to_s),
            ((sx, two), (p.fx, two), half, to_s),
            ((sy, one), (p.fy, one), half, to_s),
            ((sd, one), (p.fd, one), half, to_s),
            ((sd, two), (p.fd, two), half, to_s),
        )

    def at(self, owner, lo, n):
        return self.full.at[pl.ds(pl.multiple_of(owner * self.size + self.base + lo, 16), n)]

    def copy(self, kind, sending):
        received, sent, n, device = self.table[kind]
        owner, lo = sent if sending else received
        here = self.at(owner, lo, n)
        src = self.shard.at[pl.ds(pl.multiple_of(self.base + lo, 16), n)] if kind in (0, 1, 6) else here
        return remote(src, here, self.send_sem.at[self.unit, kind], self.recv_sem.at[self.unit, kind], device)

    def start(self, *kinds):
        for kind in kinds:
            self.copy(kind, True).start()

    def got(self, *kinds):
        for kind in kinds:
            self.copy(kind, False).wait_recv()

    def sent(self):
        for kind in range(KINDS):
            self.copy(kind, True).wait_send()

    def own(self):
        src = self.shard.at[pl.ds(self.base, self.rows)]
        return pltpu.make_async_copy(src, self.at(self.p.f, 0, self.rows), self.local_sem.at[self.unit])

    def direct(self):
        self.start(0, 1, 6)
        self.own().start()

    def forward(self):
        self.got(0)
        self.start(4, 2, 7)
        self.got(1)
        self.start(5, 3, 8)

    def relay(self):
        for kind in (4, 5, 2, 3):
            self.got(kind)
            self.start({2: 9, 3: 10, 4: 11, 5: 12}[kind])

    def done(self):
        self.got(6, 7, 8, 9, 10, 11, 12)
        self.own().wait()


def forward_kernel(
    lengths, tokens, cot, small, sh_q, sh_o, sh_u, sh_d,
    layer_out, wq_out, wo_out, wu_out, wd_out, qkv_out, slope_out, act_pair, first_pair, mixed_pair,
    tok_pair, branch_pair, norm_out, inv_out, grad_out_ref, params_out, sums_out,
    x, wq, wo, wu, wd, qkv, mixed, norm, first_low, act, slope, acc, cot_v, gh2, out_v, gb, smalls, params,
    inv_v, sums, up_rows,
    ag_send, ag_recv, ag_local, sm_send, sm_recv, sm_local, io, pair_send, pair_recv, pair_local,
):
    p = Place()
    rows, width = x.shape
    slots = lengths.shape[0]
    seq = rows // slots
    others = [lax.rem(p.f + k, 8) for k in range(1, 8)]
    barrier = pltpu.get_barrier_semaphore()
    for g in others:
        pl.semaphore_signal(barrier, inc=1, device_id=p.dev(f=g), device_id_type=MESH)
    pl.semaphore_signal(barrier, inc=1, device_id=p.dev(z=p.zn), device_id_type=MESH)
    loads = [
        pltpu.make_async_copy(tokens, x, io.at[0]),
        pltpu.make_async_copy(cot, cot_v, io.at[1]),
        pltpu.make_async_copy(small, smalls.at[p.f], sm_local),
    ]
    for c in loads:
        c.start()
    pl.semaphore_wait(barrier, 8)

    def small_copy(k, owner, device):
        return remote(small, smalls.at[owner], sm_send.at[k], sm_recv.at[k], device)

    for k, g in enumerate(others):
        small_copy(k, p.f, p.dev(f=g)).start()

    def gather(unit, shard, full, base, count):
        return Gather(p, unit, shard, full, base, count, ag_send, ag_recv, ag_local)

    g_q, g_o = gather(0, sh_q, wq, 0, 128), gather(1, sh_o, wo, 0, 128)
    g_u, g_v = gather(2, sh_u, wu, 0, 64), gather(3, sh_u, wu, 64, 64)
    g_d, g_e = gather(4, sh_d, wd, 0, 256), gather(5, sh_d, wd, 256, 256)
    g_q.direct()
    g_o.direct()

    mine = pl.ds(pl.multiple_of(p.core * rows, rows), rows)

    def pair(index, chip, src, dst, cols):
        own = pl.ds(pl.multiple_of((2 * chip + p.core) * cols, cols), cols)
        other = pl.ds(pl.multiple_of((2 * chip + 1 - p.core) * cols, cols), cols)
        here = dst.at[mine, pl.ds(chip * cols, cols)]
        return (
            pltpu.make_async_copy(src.at[:, own], here, pair_local.at[index, chip]),
            remote(src.at[:, other], here, pair_send.at[index, chip], pair_recv.at[index, chip], p.dev(f=p.fs)),
        )

    pairs = []

    def start_pair(index, src, dst, cols, chips=range(4)):
        for chip in chips:
            for c in pair(index, chip, src, dst, cols):
                c.start()
            pairs.append((index, chip, src, dst, cols))

    loads[0].wait()
    start_pair(0, x, tok_pair, 128)
    loads[2].wait()
    for k, g in enumerate(others):
        back = lax.rem(p.f + 7 - k, 8)
        small_copy(k, back, p.dev(f=back)).wait_recv()
    for g in range(8):
        part = smalls[g].astype(F32)
        params[:, g * 128 : (g + 1) * 128] = part
        for j in range(4):
            up_rows[g : g + 1, j * 128 : (j + 1) * 128] = part[8 + j : 9 + j]
    g_q.forward()
    g_u.direct()
    g_o.forward()
    g_v.direct()
    g_q.relay()
    g_o.relay()
    g_q.done()
    stores = [pltpu.make_async_copy(wq, wq_out, io.at[2])]
    stores[-1].start()
    for j in range(3):
        part = dot_nn(x[...], wq[:, j * width : (j + 1) * width])
        if j == 0:
            part = part + params[0:1]
        if j == 2:
            part = part + params[1:2]
        qkv[:, j * width : (j + 1) * width] = part.astype(BF16)
    stores.append(pltpu.make_async_copy(qkv, qkv_out, io.at[3]))
    stores[-1].start()

    left = lax.broadcasted_iota(jnp.int32, (seq, 128), 1) < HEAD_SIZE
    key_row = lax.broadcasted_iota(jnp.int32, (seq, seq), 0)

    def attend(step, carry):
        slot, pair_of = lax.div(step, 8), lax.rem(step, 8)
        at_rows = pl.ds(pl.multiple_of(slot * seq, seq), seq)
        col = pl.multiple_of(pair_of * 128, 128)
        q = qkv[at_rows, pl.ds(col, 128)]
        k = qkv[at_rows, pl.ds(pl.multiple_of(width + col, 128), 128)]
        v = qkv[at_rows, pl.ds(pl.multiple_of(2 * width + col, 128), 128)]
        dead = key_row >= lengths[slot]
        outs = []
        for head in range(2):
            k_head = jnp.where(left if head == 0 else ~left, k, jnp.zeros_like(k))
            scores = dot_nt(k_head, q) * (1.0 / math.sqrt(HEAD_SIZE))
            scores = jnp.where(dead, -1e30, scores)
            exps = jnp.exp(scores - jnp.max(scores, axis=0, keepdims=True))
            probs = exps * (1.0 / jnp.sum(exps, axis=0, keepdims=True))
            outs.append(dot_tn(probs.astype(BF16), v))
        mixed[at_rows, pl.ds(col, 128)] = jnp.where(left, outs[0], outs[1]).astype(BF16)
        return carry

    g_u.forward()
    g_d.direct()
    steps = 8 * slots
    lax.fori_loop(0, steps // 3, attend, 0)
    g_v.forward()
    g_u.relay()
    lax.fori_loop(steps // 3, 2 * steps // 3, attend, 0)
    g_e.direct()
    g_v.relay()
    lax.fori_loop(2 * steps // 3, steps, attend, 0)
    start_pair(1, mixed, mixed_pair, 128)
    g_o.done()
    g_d.forward()
    stores.append(pltpu.make_async_copy(wo, wo_out, io.at[4]))
    stores[-1].start()
    hidden = x[...].astype(F32) + dot_nn(mixed[...], wo[...]) + params[2:3]
    center = hidden - row_mean(hidden)
    inverse = lax.rsqrt(row_mean(center * center) + 1e-05)
    norm[...] = center * inverse
    inv_v[...] = jnp.broadcast_to(inverse, inv_v.shape)
    acc[...] = norm[...] * params[6:7] + params[3:4]
    first_low[...] = acc[...].astype(BF16)
    start_pair(2, first_low, first_pair, 128)
    stores.append(pltpu.make_async_copy(norm, norm_out, io.at[5]))
    stores.append(pltpu.make_async_copy(inv_v, inv_out, io.at[6]))
    stores[-1].start()
    stores[-2].start()
    g_d.relay()
    g_u.done()
    g_v.done()
    stores.append(pltpu.make_async_copy(wu, wu_out, io.at[7]))
    stores[-1].start()

    def up_step(j, carry):
        cols = pl.ds(pl.multiple_of(j * 512, 512), 512)
        inner = dot_nn(first_low[...], wu[:, cols]) + up_rows[pl.ds(j, 1), :]
        phi = 0.5 * (1.0 + lax.erf(inner * math.sqrt(0.5)))
        act[:, cols] = (inner * phi).astype(BF16)
        density = jnp.exp(-0.5 * inner * inner) * (1.0 / math.sqrt(2.0 * math.pi))
        slope[:, cols] = (phi + inner * density).astype(BF16)
        return carry

    lax.fori_loop(0, 4, up_step, 0)
    g_e.forward()
    start_pair(3, act, act_pair, 512, range(2))
    lax.fori_loop(4, 8, up_step, 0)
    g_e.relay()
    start_pair(3, act, act_pair, 512, range(2, 4))
    stores.append(pltpu.make_async_copy(slope, slope_out, io.at[8]))
    stores[-1].start()
    acc[...] += params[4:5]

    def down_half(lo):
        for j in range(4):
            cols = (slice(1024 * j + lo, 1024 * j + lo + 256), slice(1024 * j + 512 + lo, 1024 * j + 768 + lo))
            left = jnp.concatenate([act[:, c] for c in cols], axis=1)
            right = jnp.concatenate([wd[c, :] for c in cols], axis=0)
            acc[...] += dot_nn(left, right)

    g_d.done()
    down_half(0)
    g_e.done()
    stores.append(pltpu.make_async_copy(wd, wd_out, io.at[9]))
    stores[-1].start()
    down_half(256)
    loads[1].wait()
    hidden = acc[...]
    center = hidden - row_mean(hidden)
    inverse = lax.rsqrt(row_mean(center * center) + 1e-05)
    second = center * inverse
    out_v[...] = (second * params[7:8] + params[5:6]).astype(BF16)
    stores.append(pltpu.make_async_copy(out_v, layer_out, io.at[10]))
    stores[-1].start()
    row_at = lax.broadcasted_iota(jnp.int32, (seq, 1), 0)
    live = jnp.concatenate([(row_at < lengths[s]).astype(F32) for s in range(slots)], axis=0)
    e = cot_v[...] * live
    sums[...] = jnp.zeros_like(sums)
    sums[0:1] = jnp.sum(e * second, axis=0, keepdims=True)
    sums[1:2] = jnp.sum(e, axis=0, keepdims=True)
    scaled = e * params[7:8]
    gh2[...] = inverse * (scaled - row_mean(scaled) - second * row_mean(scaled * second))
    gb[...] = gh2[...].astype(BF16)
    c_local = pltpu.make_async_copy(gb, branch_pair.at[mine], pair_local.at[4, 0])
    c_remote = remote(gb, branch_pair.at[mine], pair_send.at[4, 0], pair_recv.at[4, 0], p.dev(f=p.fs))
    c_local.start()
    c_remote.start()
    sums[2:3] = jnp.sum(gb[...].astype(F32), axis=0, keepdims=True)
    stores.append(pltpu.make_async_copy(gh2, grad_out_ref, io.at[11]))
    stores.append(pltpu.make_async_copy(params, params_out, io.at[12]))
    stores.append(pltpu.make_async_copy(sums, sums_out, io.at[13]))
    for c in stores[-3:]:
        c.start()
    for c in stores:
        c.wait()
    c_local.wait()
    c_remote.wait()
    for args in pairs:
        a, b = pair(*args)
        a.wait()
        b.wait()
    for k, g in enumerate(others):
        small_copy(k, p.f, p.dev(f=g)).wait_send()
    for g in (g_q, g_o, g_u, g_v, g_d, g_e):
        g.sent()


def forward_call(tokens, lengths, cotangent, qkv_w, out_w, up_w, down_w, small):
    rows, width = tokens.shape
    ff = up_w.shape[1]
    anyspace = pl.BlockSpec(memory_space=pl.ANY)
    shape = jax.ShapeDtypeStruct
    outs = [
        shape((rows, width), BF16),
        shape((width, 3 * width), BF16),
        shape((width, width), BF16),
        shape((width, ff), BF16),
        shape((ff, width), BF16),
        shape((rows, 3 * width), BF16),
        shape((rows, ff), BF16),
        shape((2 * rows, ff // 2), BF16),
        shape((2 * rows, width // 2), BF16),
        shape((2 * rows, width // 2), BF16),
        shape((2 * rows, width // 2), BF16),
        shape((2 * rows, width), BF16),
        shape((rows, width), F32),
        shape((rows, 128), F32),
        shape((rows, width), F32),
        shape((16, width), F32),
        shape((8, width), F32),
    ]
    dma = pltpu.SemaphoreType.DMA
    scratch = [
        pltpu.VMEM((rows, width), BF16),
        pltpu.VMEM((width, 3 * width), BF16),
        pltpu.VMEM((width, width), BF16),
        pltpu.VMEM((width, ff), BF16),
        pltpu.VMEM((ff, width), BF16),
        pltpu.VMEM((rows, 3 * width), BF16),
        pltpu.VMEM((rows, width), BF16),
        pltpu.VMEM((rows, width), F32),
        pltpu.VMEM((rows, width), BF16),
        pltpu.VMEM((rows, ff), BF16),
        pltpu.VMEM((rows, ff), BF16),
        pltpu.VMEM((rows, width), F32),
        pltpu.VMEM((rows, width), F32),
        pltpu.VMEM((rows, width), F32),
        pltpu.VMEM((rows, width), BF16),
        pltpu.VMEM((rows, width), BF16),
        pltpu.VMEM((8, 16, 128), BF16),
        pltpu.VMEM((16, width), F32),
        pltpu.VMEM((rows, 128), F32),
        pltpu.VMEM((8, width), F32),
        pltpu.VMEM((8, ff // 8), F32),
        dma((UNITS, KINDS)),
        dma((UNITS, KINDS)),
        dma((UNITS,)),
        dma((7,)),
        dma((7,)),
        dma,
        dma((14,)),
        dma((5, 4)),
        dma((5, 4)),
        dma((5, 4)),
    ]
    return pl.pallas_call(
        forward_kernel,
        out_shape=outs,
        in_specs=[pl.BlockSpec(memory_space=pltpu.SMEM)] + [anyspace] * 7,
        out_specs=[anyspace] * len(outs),
        scratch_shapes=scratch,
        name="forward",
        cost_estimate=pl.CostEstimate(flops=2 * 512 * 12582912, bytes_accessed=60 * MIB, transcendentals=4 * MIB),
        compiler_params=pltpu.CompilerParams(
            collective_id=0, has_side_effects=True, vmem_limit_bytes=60 * MIB
        ),
    )(lengths, tokens, cotangent, small, qkv_w, out_w, up_w, down_w)


def pack_small(biases, up_bias, gains):
    return jnp.concatenate([biases, gains, up_bias.reshape(4, 128), jnp.zeros((4, 128), BF16)], axis=0)


BLOCKS = 12
PIECES = [(b, 0, 64) for b in range(10)] + [(b, o, 32) for b in (10, 11) for o in (0, 32)]
AHEAD = 2
S1X, S1Y, S2X, S2Y, Z1G, Z1K, Z2, FM, FE, FF = range(10)


class Reduce:
    def __init__(self, place, prod, got_x, got_y, end_x, end_y, from_end, from_mid, out_at, send, recv, local):
        self.p = place
        self.prod, self.got_x, self.got_y, self.end_x, self.end_y = prod, got_x, got_y, end_x, end_y
        self.from_end, self.from_mid, self.out_at = from_end, from_mid, out_at
        self.send, self.recv, self.local = send, recv, local
        z = place.z
        self.mid = 1 + lax.div(z, 2)
        self.end = 3 * lax.div(z, 2)
        self.is_mid = z == self.mid
        self.is_end = z == self.end
        self.made, self.begun, self.ticks = 0, 0, 0

    def keep(self, o, n):
        return pl.ds(pl.multiple_of(64 * (self.mid - 1) + o, 16), n)

    def give(self, o, n):
        return pl.ds(pl.multiple_of(64 * (2 - self.mid) + o, 16), n)

    def copy(self, kind, u, sending=True):
        p = self.p
        b, o, n = PIECES[u]
        x, y, xn, yn = p.x, p.y, 1 - p.x, 1 - p.y
        near, far = pl.ds(o, n), pl.ds(64 + o, n)
        keep, give = self.keep(o, n), self.give(o, n)
        to_mid, to_end, to_other = p.dev(z=self.mid), p.dev(z=self.end), p.dev(z=3 - self.mid)
        own = self.prod.at[b, y, x]
        if kind == S1X:
            src, dst, dev = self.prod.at[b, :, xn, near], self.got_x.at[b, :, near], p.dev(f=p.fx)
        elif kind == S1Y:
            src, dst, dev = self.prod.at[b, yn, :, far], self.got_y.at[b, :, near], p.dev(f=p.fy)
        elif kind == S2Y:
            src, dst, dev = self.prod.at[b, yn, x, near], self.end_y.at[b, near], p.dev(f=p.fy)
        elif kind == S2X:
            src, dst, dev = self.prod.at[b, y, xn, far], self.end_x.at[b, near], p.dev(f=p.fx)
        elif kind == Z1G:
            src, dst, dev = own.at[give], self.from_end.at[b, give], to_mid
        elif kind == Z1K:
            src, dst, dev = own.at[keep], self.from_end.at[b, keep], to_mid
        elif kind == Z2:
            src, dst, dev = own.at[give], self.from_mid.at[b, near], to_other
        elif kind == FM:
            src, dst, dev = own.at[keep], self.out_at(b, keep if sending else give), to_other
        elif kind == FE:
            src, dst, dev = own.at[keep], self.out_at(b, keep), to_end
        else:
            src, dst, dev = self.out_at(b, give), self.out_at(b, give), to_end
        return remote(src, dst, self.send.at[kind, u], self.recv.at[kind, u], dev)

    def advance(self):
        while self.begun < len(PIECES) and PIECES[self.begun][0] < self.made and self.begun < self.ticks + AHEAD:
            self.copy(S1X, self.begun).start()
            self.copy(S1Y, self.begun).start()
            self.begun += 1

    def second(self, u):
        x, y = self.p.x, self.p.y
        b, o, n = PIECES[u]
        near, far = slice(o, o + n), slice(64 + o, 64 + o + n)
        self.copy(S1X, u).wait_recv()
        self.prod[b, :, x, near] = self.prod[b, :, x, near] + self.got_x[b, :, near]
        self.copy(S2Y, u).start()
        self.copy(S1Y, u).wait_recv()
        self.prod[b, y, :, far] = self.prod[b, y, :, far] + self.got_y[b, :, near]
        self.copy(S2X, u).start()

    def along(self, u):
        x, y = self.p.x, self.p.y
        b, o, n = PIECES[u]
        near, far = slice(o, o + n), slice(64 + o, 64 + o + n)
        self.copy(S2Y, u).wait_recv()
        self.prod[b, y, x, near] = self.prod[b, y, x, near] + self.end_y[b, near]
        self.copy(S2X, u).wait_recv()
        self.prod[b, y, x, far] = self.prod[b, y, x, far] + self.end_x[b, near]

        @pl.when(self.is_end)
        def _():
            self.copy(Z1G, u).start()
            self.copy(Z1K, u).start()

    def inward(self, u):
        x, y = self.p.x, self.p.y
        b, o, n = PIECES[u]

        @pl.when(self.is_mid)
        def _():
            give = self.give(o, n)
            self.copy(Z1G, u).wait_recv()
            self.prod[b, y, x, give] = self.prod[b, y, x, give] + self.from_end[b, give]
            self.copy(Z2, u).start()

    def write(self, u):
        b, o, n = PIECES[u]
        keep = self.keep(o, n)
        return pltpu.make_async_copy(
            self.prod.at[b, self.p.y, self.p.x, keep], self.out_at(b, keep), self.local.at[u]
        )

    def hand_out(self, u):
        x, y = self.p.x, self.p.y
        b, o, n = PIECES[u]

        @pl.when(self.is_mid)
        def _():
            keep = self.keep(o, n)
            self.copy(Z1K, u).wait_recv()
            self.copy(Z2, u).wait_recv()
            total = self.prod[b, y, x, keep].astype(F32) + self.from_end[b, keep].astype(F32)
            self.prod[b, y, x, keep] = (total + self.from_mid[b, o : o + n].astype(F32)).astype(BF16)
            self.copy(FM, u).start()
            self.copy(FE, u).start()
            self.write(u).start()

    def pass_on(self, u):
        @pl.when(self.is_mid)
        def _():
            self.copy(FM, u, False).wait_recv()
            self.copy(FF, u).start()

    def tick(self):
        k = self.ticks
        for lag, step in enumerate((self.second, self.along, self.inward, self.hand_out, self.pass_on)):
            if 0 <= k - lag < len(PIECES):
                step(k - lag)
            if lag == 0:
                self.ticks += 1
                self.advance()

    def rest(self):
        while self.ticks < len(PIECES) + 4:
            self.tick()
        for u in range(len(PIECES)):
            self.close(u)

    def close(self, u):
        for kind in (S1X, S1Y, S2X, S2Y):
            self.copy(kind, u).wait_send()

        @pl.when(self.is_end)
        def _():
            self.copy(Z1G, u).wait_send()
            self.copy(Z1K, u).wait_send()
            self.copy(FE, u).wait_recv()
            self.copy(FF, u).wait_recv()

        @pl.when(self.is_mid)
        def _():
            for kind in (Z2, FM, FE, FF):
                self.copy(kind, u).wait_send()
            self.write(u).wait()


def backward_kernel(
    lengths, wq, wo, wu, wd, qkv, slope, act_pair, first_pair, mixed_pair, tok_pair, branch_pair,
    norm_in, inv_in, gh2, params_in, sums_in,
    token_grad, out_q, out_o, out_u, out_d, small_out,
    lhs, wbuf, slope_v, branch, gi, gq, gm, gh, norm, inv, params, sums_v, upsum,
    prod, got_x, got_y, end_x, end_y, from_end, from_mid,
    s_send, s_got, s_total, s_all, s_out,
    rs_send, rs_recv, rs_local, pair_send, pair_recv, load_sem, lhs_sem, w_sem, slope_sem,
    sm_send, sm_recv, smz_send, smz_recv, store_sem,
):
    p = Place()
    rows, width = gh.shape
    slots = lengths.shape[0]
    seq = rows // slots
    planes = [lax.rem(p.f + k, 8) for k in range(1, 8)]
    levels = [lax.rem(p.z + k, 4) for k in range(1, 4)]
    barrier = pltpu.get_barrier_semaphore()
    for g in planes:
        pl.semaphore_signal(barrier, inc=1, device_id=p.dev(f=g), device_id_type=MESH)
    for g in levels:
        pl.semaphore_signal(barrier, inc=1, device_id=p.dev(z=g), device_id_type=MESH)

    mine = pl.ds(pl.multiple_of(p.core * rows, rows), rows)

    def lhs_copies(i):
        if i < 4:
            return [
                pltpu.make_async_copy(
                    act_pair.at[:, pl.ds(chip * 512 + i * 128, 128)],
                    lhs.at[i % 2, :, pl.ds(chip * 128, 128)],
                    lhs_sem.at[i, chip],
                )
                for chip in range(4)
            ]
        src = (first_pair, mixed_pair, tok_pair)[i - 4]
        return [pltpu.make_async_copy(src, lhs.at[i % 2], lhs_sem.at[i, 0])]

    def w_copy(i):
        if i < 8:
            j = i // 2
            src = wu.at[:, pl.ds(j * 1024, 1024)] if i % 2 else wd.at[pl.ds(j * 1024, 1024)]
        elif i == 8:
            src = wo
        else:
            src = wq.at[:, pl.ds((i - 9) * 1024, 1024)]
        return pltpu.make_async_copy(src, wbuf.at[i % 2], w_sem.at[i])

    def slope_copy(j):
        return pltpu.make_async_copy(slope.at[:, pl.ds(j * 1024, 1024)], slope_v.at[j % 2], slope_sem.at[j])

    loads = [
        pltpu.make_async_copy(src, dst, load_sem.at[i])
        for i, (src, dst) in enumerate(
            (
                (branch_pair, branch), (gh2, gh), (qkv, gq.at[mine]), (norm_in, norm), (inv_in, inv),
                (params_in, params), (sums_in, sums_v),
            )
        )
    ]
    for c in lhs_copies(0):
        c.start()
    loads[0].start()
    for c in lhs_copies(1):
        c.start()
    w_copy(0).start()
    slope_copy(0).start()
    for c in loads[1:]:
        c.start()

    def out_at(b, at):
        if b < 4:
            return out_d.at[pl.ds(128 * b, 128)].at[at]
        if b < 8:
            return out_u.at[at, pl.ds((b - 4) * 1024, 1024)]
        if b == 8:
            return out_o.at[at]
        return out_q.at[at, pl.ds((b - 9) * 1024, 1024)]

    red = Reduce(p, prod, got_x, got_y, end_x, end_y, from_end, from_mid, out_at, rs_send, rs_recv, rs_local)

    def produce(b, left, right):
        prod[b] = dot_tn(left, right).astype(BF16).reshape(2, 2, 128, 1024)
        red.made = b + 1
        red.advance()

    def to_pair(index, ref, cols):
        here = ref.at[mine, cols]
        return remote(here, here, pair_send.at[index], pair_recv.at[index], p.dev(f=p.fs))

    pl.semaphore_wait(barrier, 10)
    loads[0].wait()
    for b in range(4):
        for c in lhs_copies(b):
            c.wait()
        produce(b, lhs[b % 2], branch[...])
        for c in lhs_copies(b + 2) if b < 4 else ():
            c.start()
    loads[1].wait()

    def block_cols(j):
        return pl.ds(j * 1024, 1024)

    def up_block(j):
        to_pair(j, gi, block_cols(j)).wait_recv()
        produce(4 + j, lhs[0], gi[:, j * 1024 : (j + 1) * 1024])

    for j in range(4):
        w_copy(2 * j).wait()
        w_copy(2 * j + 1).start()
        slope_copy(j).wait()
        if j < 3:
            slope_copy(j + 1).start()
        inner = (dot_nt(branch[mine], wbuf[0]) * slope_v[j % 2].astype(F32)).astype(BF16)
        gi[mine, j * 1024 : (j + 1) * 1024] = inner
        to_pair(j, gi, block_cols(j)).start()
        upsum[j : j + 1] = jnp.sum(inner.astype(F32), axis=0, keepdims=True)
        w_copy(2 * j + 1).wait()
        w_copy(2 * j + 2).start()
        gh[...] += dot_nt(gi[mine, j * 1024 : (j + 1) * 1024], wbuf[1])
        if j == 0:
            for c in lhs_copies(4):
                c.wait()
        if j > 0:
            up_block(j - 1)
            red.tick()
    for c in loads[2:]:
        c.wait()
    ga = branch
    e = gh[...]
    scaled = e * params[6:7]
    n = norm[...]
    sums_v[3:4] = jnp.sum(e, axis=0, keepdims=True)
    sums_v[4:5] = jnp.sum(e * n, axis=0, keepdims=True)
    gh[...] = inv[:, 0:1] * (scaled - row_mean(scaled) - n * row_mean(scaled * n))
    ga[mine] = gh[...].astype(BF16)
    whole = pl.ds(0, 1024)
    to_pair(4, ga, whole).start()
    sums_v[5:6] = jnp.sum(ga[mine].astype(F32), axis=0, keepdims=True)
    up_block(3)
    for c in lhs_copies(6):
        c.start()
    w_copy(8).wait()
    w_copy(9).start()
    gm[...] = dot_nt(ga[mine], wbuf[0]).astype(BF16)
    w_copy(10).start()
    for c in lhs_copies(5):
        c.wait()
    to_pair(4, ga, whole).wait_recv()
    produce(8, lhs[1], ga[...])
    red.tick()

    left = lax.broadcasted_iota(jnp.int32, (seq, 128), 1) < HEAD_SIZE
    key_row = lax.broadcasted_iota(jnp.int32, (seq, seq), 0)
    scale = 1.0 / math.sqrt(HEAD_SIZE)

    def attend(step, carry):
        slot, pair_of = lax.rem(step, slots), lax.div(step, slots)
        at_rows = pl.ds(pl.multiple_of(slot * seq, seq), seq)
        own_rows = pl.ds(pl.multiple_of(p.core * rows + slot * seq, seq), seq)
        col = pl.multiple_of(pair_of * 128, 128)
        at_q = pl.ds(col, 128)
        at_k = pl.ds(pl.multiple_of(width + col, 128), 128)
        at_v = pl.ds(pl.multiple_of(2 * width + col, 128), 128)
        q, k, v = gq[own_rows, at_q], gq[own_rows, at_k], gq[own_rows, at_v]
        do = gm[at_rows, at_q]
        dead = key_row >= lengths[slot]
        parts = []
        for head in range(2):
            lanes = left if head == 0 else ~left
            k_head = jnp.where(lanes, k, jnp.zeros_like(k))
            v_head = jnp.where(lanes, v, jnp.zeros_like(v))
            scores = jnp.where(dead, -1e30, dot_nt(k_head, q) * scale)
            exps = jnp.exp(scores - jnp.max(scores, axis=0, keepdims=True))
            probs = exps * (1.0 / jnp.sum(exps, axis=0, keepdims=True))
            d_probs = dot_nt(v_head, do)
            shared = jnp.sum(probs * d_probs, axis=0, keepdims=True)
            d_scores = (probs * (d_probs - shared)).astype(BF16)
            parts.append(
                (dot_tn(d_scores, k) * scale, dot_nn(d_scores, q) * scale, dot_nn(probs.astype(BF16), do))
            )
        for at, one, two in zip((at_q, at_k, at_v), *parts):
            gq[own_rows, at] = jnp.where(left, one, two).astype(BF16)
        return carry

    steps = 8 * slots
    for quarter in range(4):
        lax.fori_loop(quarter * steps // 4, (quarter + 1) * steps // 4, attend, 0)
        if quarter % 2:
            for j in range(3):
                to_pair(5 + 3 * (quarter // 2) + j, gq, pl.ds(j * 1024 + 512 * (quarter // 2), 512)).start()
        red.tick()
    for c in lhs_copies(6):
        c.wait()
    for j in range(3):
        for half in range(2):
            to_pair(5 + 3 * half + j, gq, pl.ds(j * 1024 + 512 * half, 512)).wait_recv()
        produce(9 + j, lhs[0], gq[:, j * 1024 : (j + 1) * 1024])
    sums_v[6:7] = jnp.sum(gq[mine, 0:1024].astype(F32), axis=0, keepdims=True)
    sums_v[7:8] = jnp.sum(gq[mine, 2048:3072].astype(F32), axis=0, keepdims=True)

    order = (6, 7, 5, 3, 2, 1, 4, 0)
    for g in range(8):
        cols = slice(g * 128, (g + 1) * 128)
        for i, row in enumerate(order):
            s_send[g, i : i + 1] = sums_v[row : row + 1, cols]
        for i in range(4):
            lo = (g % 2) * 512 + i * 128
            s_send[g, 8 + i : 9 + i] = upsum[g // 2 : g // 2 + 1, lo : lo + 128]

    def small_to(k):
        g = planes[k]
        return remote(s_send.at[g], s_got.at[p.f], sm_send.at[k], sm_recv.at[k], p.dev(f=g))

    def small_from(k):
        g = lax.rem(p.f + 7 - k, 8)
        return remote(s_send.at[g], s_got.at[g], sm_send.at[k], sm_recv.at[k], p.dev(f=g))

    def level_to(k):
        return remote(s_total, s_all.at[p.z], smz_send.at[k], smz_recv.at[k], p.dev(z=levels[k]))

    def level_from(k):
        g = lax.rem(p.z + 3 - k, 4)
        return remote(s_total, s_all.at[g], smz_send.at[k], smz_recv.at[k], p.dev(z=g))

    for k in range(7):
        small_to(k).start()
    s_got[p.f] = s_send[p.f]

    for j in range(3):
        w_copy(9 + j).wait()
        gh[...] += dot_nt(gq[mine, j * 1024 : (j + 1) * 1024], wbuf[(9 + j) % 2])
        if j == 0:
            w_copy(11).start()
    store = pltpu.make_async_copy(gh, token_grad, store_sem.at[0])
    store.start()
    red.tick()
    for k in range(7):
        small_from(k).wait_recv()
    total = s_got[0]
    for g in range(1, 8):
        total = total + s_got[g]
    s_total[...] = total
    for k in range(3):
        level_to(k).start()
    s_all[p.z] = total
    red.tick()
    red.tick()
    for k in range(3):
        level_from(k).wait_recv()
    s_out[...] = (s_all[0] + s_all[1]) + (s_all[2] + s_all[3])
    small_store = pltpu.make_async_copy(s_out, small_out, store_sem.at[1])
    small_store.start()
    red.rest()
    for k in range(7):
        small_to(k).wait_send()
    for k in range(3):
        level_to(k).wait_send()
    for j in range(4):
        to_pair(j, gi, block_cols(j)).wait_send()
    to_pair(4, ga, whole).wait_send()
    for j in range(3):
        for half in range(2):
            to_pair(5 + 3 * half + j, gq, pl.ds(j * 1024 + 512 * half, 512)).wait_send()
    store.wait()
    small_store.wait()


def backward_call(lengths, saved):
    wq, wo, wu, wd, qkv, slope = saved[:6]
    rows, width = qkv.shape[0], wo.shape[0]
    ff = wu.shape[1]
    anyspace = pl.BlockSpec(memory_space=pl.ANY)
    shape = jax.ShapeDtypeStruct
    dma = pltpu.SemaphoreType.DMA
    outs = [
        shape((rows, width), F32),
        shape((width // 8, 3 * width), BF16),
        shape((width // 8, width), BF16),
        shape((width // 8, ff), BF16),
        shape((ff // 8, width), BF16),
        shape((16, 128), F32),
    ]
    scratch = [
        pltpu.VMEM((2, 2 * rows, 512), BF16),
        pltpu.VMEM((2, 1024, 1024), BF16),
        pltpu.VMEM((2, rows, 1024), BF16),
        pltpu.VMEM((2 * rows, width), BF16),
        pltpu.VMEM((2 * rows, ff), BF16),
        pltpu.VMEM((2 * rows, 3 * width), BF16),
        pltpu.VMEM((rows, width), BF16),
        pltpu.VMEM((rows, width), F32),
        pltpu.VMEM((rows, width), F32),
        pltpu.VMEM((rows, 128), F32),
        pltpu.VMEM((16, width), F32),
        pltpu.VMEM((8, width), F32),
        pltpu.VMEM((4, width), F32),
        pltpu.VMEM((BLOCKS, 2, 2, 128, 1024), BF16),
        pltpu.VMEM((BLOCKS, 2, 64, 1024), BF16),
        pltpu.VMEM((BLOCKS, 2, 64, 1024), BF16),
        pltpu.VMEM((BLOCKS, 64, 1024), BF16),
        pltpu.VMEM((BLOCKS, 64, 1024), BF16),
        pltpu.VMEM((BLOCKS, 128, 1024), BF16),
        pltpu.VMEM((BLOCKS, 64, 1024), BF16),
        pltpu.VMEM((8, 16, 128), F32),
        pltpu.VMEM((8, 16, 128), F32),
        pltpu.VMEM((16, 128), F32),
        pltpu.VMEM((4, 16, 128), F32),
        pltpu.VMEM((16, 128), F32),
        dma((10, len(PIECES))),
        dma((10, len(PIECES))),
        dma((len(PIECES),)),
        dma((11,)),
        dma((11,)),
        dma((7,)),
        dma((7, 4)),
        dma((12,)),
        dma((4,)),
        dma((7,)),
        dma((7,)),
        dma((3,)),
        dma((3,)),
        dma((2,)),
    ]
    return pl.pallas_call(
        backward_kernel,
        out_shape=outs,
        in_specs=[pl.BlockSpec(memory_space=pltpu.SMEM)] + [anyspace] * len(saved),
        out_specs=[anyspace] * len(outs),
        scratch_shapes=scratch,
        name="backward",
        cost_estimate=pl.CostEstimate(flops=4 * 512 * 12582912, bytes_accessed=60 * MIB, transcendentals=4 * MIB),
        compiler_params=pltpu.CompilerParams(
            collective_id=1, has_side_effects=True, vmem_limit_bytes=60 * MIB
        ),
    )(lengths, *saved)


def finish_kernel(
    layer_in, token_in, q_in, o_in, u_in, d_in, small,
    layer_out, token_out, q_out, o_out, u_out, d_out, biases_out, up_bias_out, gains_out,
    q_low, o_low, u_low, d_low, layer_v, token_v, small_v, q, o, u, d, sem,
):
    sources = (d_in, u_in, q_in, o_in, token_in, layer_in, small)
    lows, wides = (d_low, u_low, q_low, o_low, token_v, layer_v, small_v), (d, u, q, o, token_v, layer_v)
    results = (d_out, u_out, q_out, o_out, token_out, layer_out)
    ins = [pltpu.make_async_copy(a, b, sem.at[i]) for i, (a, b) in enumerate(zip(sources, lows))]
    outs = [pltpu.make_async_copy(a, b, sem.at[7 + i]) for i, (a, b) in enumerate(zip(wides, results))]
    for c in ins:
        c.start()
    for a, b, c_in, c_out in zip(lows, wides, ins, outs):
        c_in.wait()
        if a is not b:
            b[...] = a[...].astype(F32)
        c_out.start()
    ins[-1].wait()
    biases_out[...] = small_v[0:6]
    gains_out[...] = small_v[6:8]
    for i in range(4):
        up_bias_out[i * 128 : (i + 1) * 128] = small_v[8 + i]
    for c in outs:
        c.wait()


def finish_call(layer_out, token_grad, weight_grads, small):
    anyspace = pl.BlockSpec(memory_space=pl.ANY)
    vmem = pl.BlockSpec(memory_space=pltpu.VMEM)
    shape = jax.ShapeDtypeStruct
    wide = [shape(g.shape, F32) for g in weight_grads]
    outs = [
        shape(layer_out.shape, BF16), shape(token_grad.shape, F32), *wide,
        shape((6, 128), F32), shape((512,), F32), shape((2, 128), F32),
    ]
    return pl.pallas_call(
        finish_kernel,
        out_shape=outs,
        in_specs=[anyspace] * 7,
        out_specs=[anyspace] * 6 + [vmem] * 3,
        scratch_shapes=[pltpu.VMEM(g.shape, BF16) for g in weight_grads]
        + [pltpu.VMEM(g.shape, g.dtype) for g in (layer_out, token_grad, small)]
        + [pltpu.VMEM(g.shape, F32) for g in weight_grads]
        + [pltpu.SemaphoreType.DMA((13,))],
        name="finish",
        compiler_params=pltpu.CompilerParams(vmem_limit_bytes=60 * MIB),
    )(layer_out, token_grad, *weight_grads, small)


def plane(
    tokens,
    lengths,
    cotangent,
    qkv_weight,
    out_weight,
    up_weight,
    down_weight,
    biases,
    up_bias,
    gains,
):
    small_in = pack_small(biases, up_bias, gains)
    layer_out, *saved = forward_call(
        tokens, lengths, cotangent, qkv_weight, out_weight, up_weight, down_weight, small_in
    )
    token_grad, *weight_grads, small = backward_call(lengths, saved)
    return tuple(finish_call(layer_out, token_grad, weight_grads, small))


def solution(mesh):
    step = plane if dict(mesh.shape) == {"fsdp": 8, "rep": 4} else portable
    both = ("fsdp", "rep")
    in_specs = (
        P(both, None),
        P(both),
        P(both, None),
        P("fsdp", None),
        P("fsdp", None),
        P("fsdp", None),
        P("fsdp", None),
        P(None, "fsdp"),
        P("fsdp"),
        P(None, "fsdp"),
    )
    out_specs = (
        P(both, None),
        P(both, None),
        P("fsdp", None),
        P("fsdp", None),
        P("fsdp", None),
        P("fsdp", None),
        P(None, "fsdp"),
        P("fsdp"),
        P(None, "fsdp"),
    )
    return jax.shard_map(
        step, mesh=mesh, in_specs=in_specs, out_specs=out_specs, check_vma=False
    )
```

```python
import math

import jax
import jax.numpy as jnp
from jax import lax
from jax.experimental import pallas as pl
from jax.experimental.pallas import tpu as pltpu
from jax.sharding import PartitionSpec as P

HEAD_SIZE = 64


def matmul(left_side, right_side):
    return jnp.dot(left_side, right_side, preferred_element_type=jnp.float32)


def transposed_left(left_side, right_side):
    return lax.dot_general(
        left_side, right_side, (((0,), (0,)), ((), ())), preferred_element_type=jnp.float32
    )


def transposed_right(left_side, right_side):
    return lax.dot_general(
        left_side, right_side, (((1,), (1,)), ((), ())), preferred_element_type=jnp.float32
    )


def column_sum(values):
    return jnp.sum(values.astype(jnp.float32), axis=0)


def row_mean(values):
    return jnp.mean(values, axis=-1, keepdims=True)


def normalize(hidden):
    center = hidden - row_mean(hidden)
    inverse = lax.rsqrt(row_mean(center * center) + 1e-05)
    return center * inverse, inverse


def norm_back(grad, norm, inverse, gain):
    scaled = grad * gain
    return inverse * (scaled - row_mean(scaled) - norm * row_mean(scaled * norm))


def low(values):
    return values.astype(jnp.bfloat16)


def gather_small(biases, up_bias, gains):
    width, up_width = biases.shape[1], up_bias.shape[0]
    packed = jnp.concatenate([biases.reshape(-1), gains.reshape(-1), up_bias])
    everyone = lax.all_gather(packed, "fsdp", axis=0, tiled=False).astype(jnp.float32)
    rows = everyone[:, : 8 * width].reshape(-1, 8, width).transpose(1, 0, 2).reshape(8, -1)
    return rows[:6], everyone[:, 8 * width : 8 * width + up_width].reshape(-1), rows[6:]


def reduce_weight(grad):
    shard = lax.psum_scatter(low(grad), "fsdp", scatter_dimension=0, tiled=True)
    return lax.psum(shard, "rep").astype(jnp.float32)


def portable(
    tokens,
    lengths,
    cotangent,
    qkv_weight,
    out_weight,
    up_weight,
    down_weight,
    biases,
    up_bias,
    gains,
):
    slots = lengths.shape[0]
    rows, width = tokens.shape
    seq = rows // slots
    heads = width // HEAD_SIZE
    scale = 1.0 / math.sqrt(HEAD_SIZE)
    w_qkv = lax.all_gather(qkv_weight, "fsdp", axis=0, tiled=True)
    w_out = lax.all_gather(out_weight, "fsdp", axis=0, tiled=True)
    w_up = lax.all_gather(up_weight, "fsdp", axis=0, tiled=True)
    w_down = lax.all_gather(down_weight, "fsdp", axis=0, tiled=True)
    bias_rows, bias_up, gain_rows = gather_small(biases, up_bias, gains)

    def split(values):
        return values.reshape(slots, seq, heads, HEAD_SIZE)

    def join(values):
        return values.reshape(rows, width)

    sums = matmul(tokens, w_qkv)
    query = split(low(sums[:, :width] + bias_rows[0]))
    key = split(low(sums[:, width : 2 * width]))
    value = split(low(sums[:, 2 * width :] + bias_rows[1]))
    live = jnp.arange(seq)[None, :] < lengths[:, None]
    scores = scale * jnp.einsum(
        "bshd,bthd->bhst", query, key, preferred_element_type=jnp.float32
    )
    scores = jnp.where(live[:, None, None, :], scores, -1e30)
    exps = jnp.exp(scores - jnp.max(scores, axis=-1, keepdims=True))
    probs = exps / jnp.sum(exps, axis=-1, keepdims=True)
    probs_low = low(probs)
    mixed = low(
        join(jnp.einsum("bhst,bthd->bshd", probs_low, value, preferred_element_type=jnp.float32))
    )
    first, first_inverse = normalize(
        tokens.astype(jnp.float32) + matmul(mixed, w_out) + bias_rows[2]
    )
    first_norm = first * gain_rows[0] + bias_rows[3]
    first_low = low(first_norm)
    inner = matmul(first_low, w_up) + bias_up
    cumulative = 0.5 * (1.0 + lax.erf(inner * math.sqrt(0.5)))
    act_low = low(inner * cumulative)
    slope = low(cumulative + inner * jnp.exp(-0.5 * inner * inner) / math.sqrt(2.0 * math.pi))
    second, second_inverse = normalize(first_norm + matmul(act_low, w_down) + bias_rows[4])
    layer_out = low(second * gain_rows[1] + bias_rows[5])

    grad_out = cotangent * live.reshape(rows, 1).astype(jnp.float32)
    grad_h2 = norm_back(grad_out, second, second_inverse, gain_rows[1])
    grad_branch = low(grad_h2)
    down_grad = reduce_weight(transposed_left(act_low, grad_branch))
    grad_inner = low(transposed_right(grad_branch, w_down) * slope)
    up_grad = reduce_weight(transposed_left(first_low, grad_inner))
    grad_first = grad_h2 + transposed_right(grad_inner, w_up)
    grad_h1 = norm_back(grad_first, first, first_inverse, gain_rows[0])
    grad_attn = low(grad_h1)
    out_grad = reduce_weight(transposed_left(mixed, grad_attn))
    grad_mixed = split(low(transposed_right(grad_attn, w_out)))
    grad_probs = jnp.einsum(
        "bshd,bthd->bhst", grad_mixed, value, preferred_element_type=jnp.float32
    )
    shared = jnp.sum(probs * grad_probs, axis=-1, keepdims=True)
    grad_scores = low(probs * (grad_probs - shared))
    grad_query = scale * jnp.einsum(
        "bhst,bthd->bshd", grad_scores, key, preferred_element_type=jnp.float32
    )
    grad_key = scale * jnp.einsum(
        "bhst,bshd->bthd", grad_scores, query, preferred_element_type=jnp.float32
    )
    grad_value = jnp.einsum(
        "bhst,bshd->bthd", probs_low, grad_mixed, preferred_element_type=jnp.float32
    )
    grad_qkv = jnp.concatenate(
        [join(low(grad_query)), join(low(grad_key)), join(low(grad_value))], axis=1
    )
    qkv_grad = reduce_weight(transposed_left(tokens, grad_qkv))
    token_grad = grad_h1 + transposed_right(grad_qkv, w_qkv)
    small = jnp.stack(
        [
            column_sum(grad_qkv[:, :width]),
            column_sum(grad_qkv[:, 2 * width :]),
            column_sum(grad_attn),
            column_sum(grad_first),
            column_sum(grad_branch),
            column_sum(grad_out),
            column_sum(grad_first * first),
            column_sum(grad_out * second),
        ]
    )
    owner = lax.axis_index("fsdp")
    small, up_sum = lax.psum((small, column_sum(grad_inner)), ("fsdp", "rep"))
    own, own_up = biases.shape[1], up_bias.shape[0]
    small = lax.dynamic_slice(small, (0, owner * own), (8, own))
    up_bias_grad = lax.dynamic_slice(up_sum, (owner * own_up,), (own_up,))
    return (
        layer_out,
        token_grad,
        qkv_grad,
        out_grad,
        up_grad,
        down_grad,
        small[:6],
        up_bias_grad,
        small[6:],
    )


MESH = pl.DeviceIdType.MESH
F32 = jnp.float32
BF16 = jnp.bfloat16
MIB = 1 << 20


def dot_nn(a, b):
    return lax.dot_general(a, b, (((1,), (0,)), ((), ())), preferred_element_type=F32)


def dot_nt(a, b):
    return lax.dot_general(a, b, (((1,), (1,)), ((), ())), preferred_element_type=F32)


def dot_tn(a, b):
    return lax.dot_general(a, b, (((0,), (0,)), ((), ())), preferred_element_type=F32)


class Place:
    def __init__(self):
        f, z = lax.axis_index("fsdp"), lax.axis_index("rep")
        self.f, self.z = f, z
        self.core = lax.rem(f, 2)
        self.x = lax.rem(lax.div(f, 2), 2)
        self.y = lax.div(f, 4)
        self.chip = lax.div(f, 2)
        self.fx = f + 2 - 4 * self.x
        self.fy = f + 4 - 8 * self.y
        self.fd = self.fx + 4 - 8 * self.y
        self.fs = f + 1 - 2 * self.core
        self.par = lax.rem(z, 2)
        self.zn = z + 1 - 2 * self.par

    def dev(self, f=None, z=None):
        return {"fsdp": self.f if f is None else f, "rep": self.z if z is None else z}


def remote(src, dst, send_sem, recv_sem, device):
    return pltpu.make_async_remote_copy(
        src_ref=src, dst_ref=dst, send_sem=send_sem, recv_sem=recv_sem,
        device_id=device, device_id_type=MESH,
    )


UNITS = 8
KINDS = 13


class Gather:
    def __init__(self, place, unit, shard, full, base, rows, extra, send, recv, local):
        self.p, self.unit, self.shard, self.full = place, unit, shard, full
        self.base, self.rows, self.size = base, rows, shard.shape[0]
        self.send_sem, self.recv_sem, self.local_sem = send, recv, local
        p, half = place, rows // 2
        one, two = half * p.par, half * (1 - p.par)
        wide, rest = half + extra, half - extra
        near_x, near_y = rest * p.par, rest * (1 - p.par)
        far_x, far_y = wide * (1 - p.par), wide * p.par
        to_x, to_y, to_s, to_z = p.dev(f=p.fx), p.dev(f=p.fy), p.dev(f=p.fs), p.dev(z=p.zn)
        sx, sy, sd = (g + 1 - 2 * p.core for g in (p.fx, p.fy, p.fd))
        self.table = (
            ((p.fx, near_x), (p.f, near_x), wide, to_x),
            ((p.fy, near_y), (p.f, near_y), wide, to_y),
            ((p.fx, far_x), (p.fx, far_y), rest, to_z),
            ((p.fy, far_y), (p.fy, far_x), rest, to_z),
            ((p.fd, one), (p.fx, one), half, to_y),
            ((p.fd, two), (p.fy, two), half, to_x),
            ((p.fs, 0), (p.f, 0), rows, to_s),
            ((sx, near_x), (p.fx, near_x), wide, to_s),
            ((sy, near_y), (p.fy, near_y), wide, to_s),
            ((sx, far_x), (p.fx, far_x), rest, to_s),
            ((sy, far_y), (p.fy, far_y), rest, to_s),
            ((sd, one), (p.fd, one), half, to_s),
            ((sd, two), (p.fd, two), half, to_s),
        )

    def at(self, owner, lo, n):
        return self.full.at[pl.ds(pl.multiple_of(owner * self.size + self.base + lo, 16), n)]

    def copy(self, kind, sending):
        received, sent, n, device = self.table[kind]
        owner, lo = sent if sending else received
        here = self.at(owner, lo, n)
        src = self.shard.at[pl.ds(pl.multiple_of(self.base + lo, 16), n)] if kind in (0, 1, 6) else here
        return remote(src, here, self.send_sem.at[self.unit, kind], self.recv_sem.at[self.unit, kind], device)

    def start(self, *kinds):
        for kind in kinds:
            self.copy(kind, True).start()

    def got(self, *kinds):
        for kind in kinds:
            self.copy(kind, False).wait_recv()

    def sent(self):
        for kind in range(KINDS):
            self.copy(kind, True).wait_send()

    def own(self):
        src = self.shard.at[pl.ds(self.base, self.rows)]
        return pltpu.make_async_copy(src, self.at(self.p.f, 0, self.rows), self.local_sem.at[self.unit])

    def direct(self):
        self.start(0, 1, 6)
        self.own().start()

    def forward(self):
        self.got(0)
        self.start(4, 2, 7)
        self.got(1)
        self.start(5, 3, 8)

    def relay(self):
        for kind in (4, 5, 2, 3):
            self.got(kind)
            self.start({2: 9, 3: 10, 4: 11, 5: 12}[kind])

    def done(self):
        self.got(6, 7, 8, 9, 10, 11, 12)
        self.own().wait()


def forward_kernel(
    lengths, tokens, cot, small, sh_q, sh_o, sh_u, sh_d,
    layer_out, wq_out, wo_out, wu_out, wd_out, qkv_out, slope_out, act_pair, first_pair, mixed_pair,
    tok_pair, branch_pair, norm_out, inv_out, grad_out_ref, params_out, sums_out,
    x, wq, wo, wu, wd, qkv, mixed, norm, first_low, act, slope, acc, cot_v, gh2, out_v, gb, smalls, params,
    inv_v, sums, up_rows,
    ag_send, ag_recv, ag_local, sm_send, sm_recv, sm_local, io, pair_send, pair_recv, pair_local, wd_sem,
):
    p = Place()
    rows, width = x.shape
    slots = lengths.shape[0]
    seq = rows // slots
    others = [lax.rem(p.f + k, 8) for k in range(1, 8)]
    barrier = pltpu.get_barrier_semaphore()
    for g in others:
        pl.semaphore_signal(barrier, inc=1, device_id=p.dev(f=g), device_id_type=MESH)
    pl.semaphore_signal(barrier, inc=1, device_id=p.dev(z=p.zn), device_id_type=MESH)
    loads = [
        pltpu.make_async_copy(tokens, x, io.at[0]),
        pltpu.make_async_copy(cot, cot_v, io.at[1]),
        pltpu.make_async_copy(small, smalls.at[p.f], sm_local),
    ]
    for c in loads:
        c.start()
    pl.semaphore_wait(barrier, 8)

    def small_copy(k, owner, device):
        return remote(small, smalls.at[owner], sm_send.at[k], sm_recv.at[k], device)

    for k, g in enumerate(others):
        small_copy(k, p.f, p.dev(f=g)).start()

    def gather(unit, shard, full, base, count, extra=0):
        return Gather(p, unit, shard, full, base, count, extra, ag_send, ag_recv, ag_local)

    g_q, g_r = gather(0, sh_q, wq, 0, 64), gather(1, sh_q, wq, 64, 64)
    g_o = gather(2, sh_o, wo, 0, 128)
    g_u, g_v = gather(3, sh_u, wu, 0, 64), gather(4, sh_u, wu, 64, 64)
    g_d, g_e, g_f = gather(5, sh_d, wd, 0, 256), gather(6, sh_d, wd, 256, 128), gather(7, sh_d, wd, 384, 128, 16)
    g_q.direct()
    g_r.direct()
    g_o.direct()

    mine = pl.ds(pl.multiple_of(p.core * rows, rows), rows)

    def pair(index, chip, src, dst, cols):
        own = pl.ds(pl.multiple_of((2 * chip + p.core) * cols, cols), cols)
        other = pl.ds(pl.multiple_of((2 * chip + 1 - p.core) * cols, cols), cols)
        here = dst.at[mine, pl.ds(chip * cols, cols)]
        return (
            pltpu.make_async_copy(src.at[:, own], here, pair_local.at[index, chip]),
            remote(src.at[:, other], here, pair_send.at[index, chip], pair_recv.at[index, chip], p.dev(f=p.fs)),
        )

    pairs = []

    def start_pair(index, src, dst, cols, chips=range(4)):
        for chip in chips:
            for c in pair(index, chip, src, dst, cols):
                c.start()
            pairs.append((index, chip, src, dst, cols))

    loads[0].wait()
    start_pair(0, x, tok_pair, 128)
    g_q.forward()
    g_u.direct()
    g_r.forward()
    g_o.forward()
    g_v.direct()
    loads[2].wait()
    for k, g in enumerate(others):
        back = lax.rem(p.f + 7 - k, 8)
        small_copy(k, back, p.dev(f=back)).wait_recv()
    for g in range(8):
        part = smalls[g].astype(F32)
        params[:, g * 128 : (g + 1) * 128] = part
        for j in range(4):
            up_rows[g : g + 1, j * 128 : (j + 1) * 128] = part[8 + j : 9 + j]
    g_q.relay()
    g_r.relay()
    g_q.done()
    g_r.done()
    g_u.forward()
    g_d.direct()
    stores = [pltpu.make_async_copy(wq, wq_out, io.at[2])]
    stores[-1].start()
    for j in range(3):
        part = dot_nn(x[...], wq[:, j * width : (j + 1) * width])
        if j == 0:
            part = part + params[0:1]
        if j == 2:
            part = part + params[1:2]
        qkv[:, j * width : (j + 1) * width] = part.astype(BF16)
    stores.append(pltpu.make_async_copy(qkv, qkv_out, io.at[3]))
    stores[-1].start()

    left = lax.broadcasted_iota(jnp.int32, (seq, 128), 1) < HEAD_SIZE
    key_row = lax.broadcasted_iota(jnp.int32, (seq, seq), 0)

    def attend(step, carry):
        slot, pair_of = lax.div(step, 8), lax.rem(step, 8)
        at_rows = pl.ds(pl.multiple_of(slot * seq, seq), seq)
        col = pl.multiple_of(pair_of * 128, 128)
        q = qkv[at_rows, pl.ds(col, 128)]
        k = qkv[at_rows, pl.ds(pl.multiple_of(width + col, 128), 128)]
        v = qkv[at_rows, pl.ds(pl.multiple_of(2 * width + col, 128), 128)]
        dead = key_row >= lengths[slot]
        outs = []
        for head in range(2):
            k_head = jnp.where(left if head == 0 else ~left, k, jnp.zeros_like(k))
            scores = dot_nt(k_head, q) * (1.0 / math.sqrt(HEAD_SIZE))
            scores = jnp.where(dead, -1e30, scores)
            exps = jnp.exp(scores - jnp.max(scores, axis=0, keepdims=True))
            probs = exps * (1.0 / jnp.sum(exps, axis=0, keepdims=True))
            outs.append(dot_tn(probs.astype(BF16), v))
        mixed[at_rows, pl.ds(col, 128)] = jnp.where(left, outs[0], outs[1]).astype(BF16)
        return carry

    steps = 8 * slots
    lax.fori_loop(0, steps // 2, attend, 0)
    g_v.forward()
    g_e.direct()
    g_f.direct()
    g_o.relay()
    lax.fori_loop(steps // 2, steps, attend, 0)
    start_pair(1, mixed, mixed_pair, 128)
    g_u.relay()
    g_o.done()
    stores.append(pltpu.make_async_copy(wo, wo_out, io.at[4]))
    stores[-1].start()
    hidden = x[...].astype(F32) + dot_nn(mixed[...], wo[...]) + params[2:3]
    center = hidden - row_mean(hidden)
    inverse = lax.rsqrt(row_mean(center * center) + 1e-05)
    norm[...] = center * inverse
    inv_v[...] = jnp.broadcast_to(inverse, inv_v.shape)
    acc[...] = norm[...] * params[6:7] + params[3:4]
    first_low[...] = acc[...].astype(BF16)
    start_pair(2, first_low, first_pair, 128)
    stores.append(pltpu.make_async_copy(norm, norm_out, io.at[5]))
    stores.append(pltpu.make_async_copy(inv_v, inv_out, io.at[6]))
    stores[-1].start()
    stores[-2].start()
    g_d.forward()
    g_v.relay()
    g_u.done()
    g_v.done()
    stores.append(pltpu.make_async_copy(wu, wu_out, io.at[7]))
    stores[-1].start()

    def up_step(j, carry):
        cols = pl.ds(pl.multiple_of(j * 512, 512), 512)
        inner = dot_nn(first_low[...], wu[:, cols]) + up_rows[pl.ds(j, 1), :]
        phi = 0.5 * (1.0 + lax.erf(inner * math.sqrt(0.5)))
        act[:, cols] = (inner * phi).astype(BF16)
        density = jnp.exp(-0.5 * inner * inner) * (1.0 / math.sqrt(2.0 * math.pi))
        slope[:, cols] = (phi + inner * density).astype(BF16)
        return carry

    lax.fori_loop(0, 4, up_step, 0)
    g_e.forward()
    start_pair(3, act, act_pair, 512, range(2))
    lax.fori_loop(4, 6, up_step, 0)
    g_f.forward()
    lax.fori_loop(6, 8, up_step, 0)
    g_d.relay()
    start_pair(3, act, act_pair, 512, range(2, 4))
    stores.append(pltpu.make_async_copy(slope, slope_out, io.at[8]))
    stores[-1].start()
    acc[...] += params[4:5]

    def down_part(lo, n):
        for j in range(0, 8, 1024 // n):
            cols = [slice(512 * g + lo, 512 * g + lo + n) for g in range(j, j + 1024 // n)]
            left = jnp.concatenate([act[:, c] for c in cols], axis=1)
            right = jnp.concatenate([wd[c, :] for c in cols], axis=0)
            acc[...] += dot_nn(left, right)

    def keep_down(i, lo, n):
        for g in range(8):
            at = pl.ds(g * 512 + lo, n)
            stores.append(pltpu.make_async_copy(wd.at[at], wd_out.at[at], wd_sem.at[g, i]))
            stores[-1].start()

    g_d.done()
    keep_down(0, 0, 256)
    down_part(0, 256)
    g_e.relay()
    g_e.done()
    keep_down(1, 256, 128)
    for k, g in enumerate(others):
        small_copy(k, p.f, p.dev(f=g)).wait_send()
    for g in (g_q, g_r, g_o, g_u, g_v):
        g.sent()
    early = len(stores) - 8
    for c in stores[:early]:
        c.wait()
    for args in pairs[:12]:
        a, b = pair(*args)
        a.wait()
        b.wait()
    down_part(256, 128)
    g_f.relay()
    g_f.done()
    keep_down(2, 384, 128)
    down_part(384, 128)
    loads[1].wait()
    hidden = acc[...]
    center = hidden - row_mean(hidden)
    inverse = lax.rsqrt(row_mean(center * center) + 1e-05)
    second = center * inverse
    out_v[...] = (second * params[7:8] + params[5:6]).astype(BF16)
    stores.append(pltpu.make_async_copy(out_v, layer_out, io.at[10]))
    stores[-1].start()
    row_at = lax.broadcasted_iota(jnp.int32, (seq, 1), 0)
    live = jnp.concatenate([(row_at < lengths[s]).astype(F32) for s in range(slots)], axis=0)
    e = cot_v[...] * live
    sums[...] = jnp.zeros_like(sums)
    sums[0:1] = jnp.sum(e * second, axis=0, keepdims=True)
    sums[1:2] = jnp.sum(e, axis=0, keepdims=True)
    scaled = e * params[7:8]
    gh2[...] = inverse * (scaled - row_mean(scaled) - second * row_mean(scaled * second))
    gb[...] = gh2[...].astype(BF16)
    c_local = pltpu.make_async_copy(gb, branch_pair.at[mine], pair_local.at[4, 0])
    c_remote = remote(gb, branch_pair.at[mine], pair_send.at[4, 0], pair_recv.at[4, 0], p.dev(f=p.fs))
    c_local.start()
    c_remote.start()
    sums[2:3] = jnp.sum(gb[...].astype(F32), axis=0, keepdims=True)
    stores.append(pltpu.make_async_copy(gh2, grad_out_ref, io.at[11]))
    stores.append(pltpu.make_async_copy(params, params_out, io.at[12]))
    stores.append(pltpu.make_async_copy(sums, sums_out, io.at[13]))
    for c in stores[-3:]:
        c.start()
    for c in stores[early:]:
        c.wait()
    c_local.wait()
    c_remote.wait()
    for args in pairs[12:]:
        a, b = pair(*args)
        a.wait()
        b.wait()
    for g in (g_d, g_e, g_f):
        g.sent()


def forward_call(tokens, lengths, cotangent, qkv_w, out_w, up_w, down_w, small):
    rows, width = tokens.shape
    ff = up_w.shape[1]
    anyspace = pl.BlockSpec(memory_space=pl.ANY)
    shape = jax.ShapeDtypeStruct
    outs = [
        shape((rows, width), BF16),
        shape((width, 3 * width), BF16),
        shape((width, width), BF16),
        shape((width, ff), BF16),
        shape((ff, width), BF16),
        shape((rows, 3 * width), BF16),
        shape((rows, ff), BF16),
        shape((2 * rows, ff // 2), BF16),
        shape((2 * rows, width // 2), BF16),
        shape((2 * rows, width // 2), BF16),
        shape((2 * rows, width // 2), BF16),
        shape((2 * rows, width), BF16),
        shape((rows, width), F32),
        shape((rows, 128), F32),
        shape((rows, width), F32),
        shape((16, width), F32),
        shape((8, width), F32),
    ]
    dma = pltpu.SemaphoreType.DMA
    scratch = [
        pltpu.VMEM((rows, width), BF16),
        pltpu.VMEM((width, 3 * width), BF16),
        pltpu.VMEM((width, width), BF16),
        pltpu.VMEM((width, ff), BF16),
        pltpu.VMEM((ff, width), BF16),
        pltpu.VMEM((rows, 3 * width), BF16),
        pltpu.VMEM((rows, width), BF16),
        pltpu.VMEM((rows, width), F32),
        pltpu.VMEM((rows, width), BF16),
        pltpu.VMEM((rows, ff), BF16),
        pltpu.VMEM((rows, ff), BF16),
        pltpu.VMEM((rows, width), F32),
        pltpu.VMEM((rows, width), F32),
        pltpu.VMEM((rows, width), F32),
        pltpu.VMEM((rows, width), BF16),
        pltpu.VMEM((rows, width), BF16),
        pltpu.VMEM((8, 16, 128), BF16),
        pltpu.VMEM((16, width), F32),
        pltpu.VMEM((rows, 128), F32),
        pltpu.VMEM((8, width), F32),
        pltpu.VMEM((8, ff // 8), F32),
        dma((UNITS, KINDS)),
        dma((UNITS, KINDS)),
        dma((UNITS,)),
        dma((7,)),
        dma((7,)),
        dma,
        dma((14,)),
        dma((5, 4)),
        dma((5, 4)),
        dma((5, 4)),
        dma((8, 3)),
    ]
    return pl.pallas_call(
        forward_kernel,
        out_shape=outs,
        in_specs=[pl.BlockSpec(memory_space=pltpu.SMEM)] + [anyspace] * 7,
        out_specs=[anyspace] * len(outs),
        scratch_shapes=scratch,
        name="forward",
        cost_estimate=pl.CostEstimate(flops=2 * 512 * 12582912, bytes_accessed=60 * MIB, transcendentals=4 * MIB),
        compiler_params=pltpu.CompilerParams(
            collective_id=0, has_side_effects=True, vmem_limit_bytes=60 * MIB
        ),
    )(lengths, tokens, cotangent, small, qkv_w, out_w, up_w, down_w)


def pack_small(biases, up_bias, gains):
    return jnp.concatenate([biases, gains, up_bias.reshape(4, 128), jnp.zeros((4, 128), BF16)], axis=0)


BLOCKS = 12
LATE = 0
SHARED = (1, 2)
ORDER = (0, 3, 1, 4, 2, 5, 6, 7, 8, 9)
PIECES = [(b, None, 32) if b in SHARED else (b, 0, 64) for b in ORDER] + [(b, o, 32) for b in (10, 11) for o in (0, 32)]
LATE_FROM = len(PIECES) - LATE
AHEAD = 2
CLOSE = 6
S1X, S1Y, S2X, S2Y, Z1G, Z1K, Z2, FM, FE, FF = range(10)


class Reduce:
    def __init__(self, place, prod, got_x, got_y, end_x, end_y, from_end, from_mid, swapped, out_at, send, recv, local, swap_send, swap_recv):
        self.p = place
        self.prod, self.got_x, self.got_y, self.end_x, self.end_y = prod, got_x, got_y, end_x, end_y
        self.from_end, self.from_mid, self.swapped, self.out_at = from_end, from_mid, swapped, out_at
        self.send, self.recv, self.local = send, recv, local
        self.swap_send, self.swap_recv = swap_send, swap_recv
        z = place.z
        self.mid = 1 + lax.div(z, 2)
        self.end = 3 * lax.div(z, 2)
        self.is_mid = z == self.mid
        self.is_end = z == self.end
        self.made, self.begun, self.ticks, self.closed = set(), 0, 0, 0

    def rows(self, u, theirs=False):
        b, o, n = PIECES[u]
        if o is None:
            o = pl.multiple_of(32 * (1 - self.p.par if theirs else self.p.par), 32)
        return b, o, n

    def z_rows(self, u):
        b, o, n = PIECES[u]
        return (b, 0, 64) if o is None else (b, o, n)

    def keep(self, o, n):
        return pl.ds(pl.multiple_of(64 * (self.mid - 1) + o, 16), n)

    def give(self, o, n):
        return pl.ds(pl.multiple_of(64 * (2 - self.mid) + o, 16), n)

    def copy(self, kind, u, sending=True):
        p = self.p
        b, o, n = self.rows(u, theirs=kind in (Z1G, Z1K) and not sending)
        _, oz, nz = self.z_rows(u)
        late = u >= LATE_FROM
        x, y, xn, yn = p.x, p.y, 1 - p.x, 1 - p.y
        near, far = pl.ds(o, n), pl.ds(64 + o, n)
        keep, give = self.keep(oz, nz), self.give(oz, nz)
        to_mid, to_end, to_other = p.dev(z=self.mid), p.dev(z=self.end), p.dev(z=3 - self.mid)
        own = self.prod.at[b, y, x]
        if kind == S1X:
            src, dst, dev = self.prod.at[b, :, xn, near], self.got_x.at[b, :, near], p.dev(f=p.fx)
        elif kind == S1Y:
            src, dst, dev = self.prod.at[b, yn, :, far], self.got_y.at[b, :, near], p.dev(f=p.fy)
        elif kind == S2Y:
            src, dst, dev = self.prod.at[b, yn, x, near], self.end_y.at[b, near], p.dev(f=p.fy)
        elif kind == S2X:
            src, dst, dev = self.prod.at[b, y, xn, far], self.end_x.at[b, near], p.dev(f=p.fx)
        elif kind == Z1G and late:
            here, there = give, self.keep(o, n)
            src, dst, dev = own.at[here], self.from_end.at[b, there if sending else here], to_other
        elif kind == Z1G:
            src, dst, dev = own.at[self.give(o, n)], self.from_end.at[b, self.give(o, n)], to_mid
        elif kind == Z1K:
            src, dst, dev = own.at[self.keep(o, n)], self.from_end.at[b, self.keep(o, n)], to_mid
        elif kind == Z2:
            src, dst, dev = own.at[give], self.from_mid.at[b, pl.ds(oz, nz)], to_other
        elif kind == FM:
            src, dst, dev = own.at[keep], self.out_at(b, keep if sending else give), to_other
        elif kind == FE:
            src, dst, dev = own.at[keep], self.out_at(b, keep), to_end
        elif late:
            src, dst, dev = own.at[keep], self.out_at(b, keep if sending else give), p.dev(z=3 - self.end)
        else:
            src, dst, dev = self.out_at(b, give), self.out_at(b, give), to_end
        return remote(src, dst, self.send.at[kind, u], self.recv.at[kind, u], dev)

    def swap(self, b, half):
        i = SHARED.index(b)
        src = self.prod.at[b, :, :, pl.ds(pl.multiple_of(64 * half + 32 * (1 - self.p.par), 32), 32)]
        dst = self.swapped.at[i, :, :, pl.ds(32 * half, 32)]
        return remote(src, dst, self.swap_send.at[i, half], self.swap_recv.at[i, half], self.p.dev(z=self.p.zn))

    def produced(self, b):
        self.made.add(b)
        if b in SHARED:
            self.swap(b, 0).start()
            self.swap(b, 1).start()
        self.advance()

    def advance(self):
        while self.begun < len(PIECES) and PIECES[self.begun][0] in self.made and self.begun < self.ticks + AHEAD:
            u = self.begun
            b, o, n = self.rows(u)
            for half, kind in enumerate((S1X, S1Y)):
                if b in SHARED:
                    at = pl.ds(pl.multiple_of(64 * half + o, 32), n)
                    self.swap(b, half).wait()
                    part = self.swapped[SHARED.index(b), :, :, 32 * half : 32 * half + 32]
                    self.prod[b, :, :, at] = self.prod[b, :, :, at] + part
                self.copy(kind, u).start()
            self.begun += 1

    def second(self, u):
        x, y = self.p.x, self.p.y
        b, o, n = self.rows(u)
        near, far = pl.ds(o, n), pl.ds(64 + o, n)
        self.copy(S1X, u).wait_recv()
        self.prod[b, :, x, near] = self.prod[b, :, x, near] + self.got_x[b, :, near]
        self.copy(S2Y, u).start()
        self.copy(S1Y, u).wait_recv()
        self.prod[b, y, :, far] = self.prod[b, y, :, far] + self.got_y[b, :, near]
        self.copy(S2X, u).start()

    def along(self, u):
        x, y = self.p.x, self.p.y
        b, o, n = self.rows(u)
        near, far = pl.ds(o, n), pl.ds(64 + o, n)
        self.copy(S2Y, u).wait_recv()
        self.prod[b, y, x, near] = self.prod[b, y, x, near] + self.end_y[b, near]
        self.copy(S2X, u).wait_recv()
        self.prod[b, y, x, far] = self.prod[b, y, x, far] + self.end_x[b, near]

        @pl.when(self.is_end)
        def _():
            self.copy(Z1G, u).start()
            self.copy(Z1K, u).start()

        if u >= LATE_FROM:

            @pl.when(self.is_mid)
            def _():
                self.copy(Z2, u).start()

    def inward(self, u):
        if u >= LATE_FROM:
            return
        x, y = self.p.x, self.p.y
        b, o, n = self.rows(u, theirs=True)

        @pl.when(self.is_mid)
        def _():
            give = self.give(o, n)
            self.copy(Z1G, u, False).wait_recv()
            if b in SHARED:
                self.prod[b, y, x, give] = self.from_end[b, give]
            else:
                self.prod[b, y, x, give] = self.prod[b, y, x, give] + self.from_end[b, give]
            self.copy(Z2, u).start()

    def write(self, u):
        b, o, n = self.z_rows(u)
        keep = self.keep(o, n)
        return pltpu.make_async_copy(
            self.prod.at[b, self.p.y, self.p.x, keep], self.out_at(b, keep), self.local.at[u]
        )

    def hand_out(self, u):
        x, y = self.p.x, self.p.y
        b, o, n = self.z_rows(u)

        @pl.when(self.is_mid)
        def _():
            keep = self.keep(o, n)
            self.copy(Z1K, u, False).wait_recv()
            if u >= LATE_FROM:
                self.copy(Z1G, u, False).wait_recv()
            if b in SHARED:
                part = self.keep(*self.rows(u, theirs=True)[1:])
                self.prod[b, y, x, part] = self.from_end[b, part]
            self.copy(Z2, u).wait_recv()
            total = self.prod[b, y, x, keep].astype(F32) + self.from_mid[b, o : o + n].astype(F32)
            if b not in SHARED:
                total = total + self.from_end[b, keep].astype(F32)
            if u >= LATE_FROM:
                total = total + self.from_end[b, self.give(o, n)].astype(F32)
            self.prod[b, y, x, keep] = total.astype(BF16)
            if u >= LATE_FROM:
                self.copy(FF, u).start()
            self.copy(FM, u).start()
            self.copy(FE, u).start()
            self.write(u).start()

    def pass_on(self, u):
        @pl.when(self.is_mid)
        def _():
            self.copy(FM, u, False).wait_recv()
            if u < LATE_FROM:
                self.copy(FF, u).start()

    def tick(self):
        k = self.ticks
        for lag, step in enumerate((self.second, self.along, self.inward, self.hand_out, self.pass_on)):
            if 0 <= k - lag < len(PIECES):
                step(k - lag)
            if lag == 0:
                self.ticks += 1
                self.advance()
        while self.closed <= min(k - CLOSE, len(PIECES) - 1):
            self.close(self.closed)
            self.closed += 1

    def rest(self):
        while self.ticks < len(PIECES) + 4:
            self.tick()
        for u in range(self.closed, len(PIECES)):
            self.close(u)

    def close(self, u):
        for kind in (S1X, S1Y, S2X, S2Y):
            self.copy(kind, u).wait_send()

        @pl.when(self.is_end)
        def _():
            self.copy(Z1G, u).wait_send()
            self.copy(Z1K, u).wait_send()
            self.copy(FE, u).wait_recv()
            self.copy(FF, u, False).wait_recv()

        @pl.when(self.is_mid)
        def _():
            for kind in (Z2, FM, FE, FF):
                self.copy(kind, u).wait_send()
            self.write(u).wait()


def backward_kernel(
    lengths, wq, wo, wu, wd, qkv, slope, act_pair, first_pair, mixed_pair, tok_pair, branch_pair,
    norm_in, inv_in, gh2, params_in, sums_in,
    token_grad, out_q, out_o, out_u, out_d, small_out,
    lhs, wbuf, slope_v, branch, gi, gq, gm, gh, norm, inv, params, sums_v, upsum,
    prod, got_x, got_y, end_x, end_y, from_end, from_mid, swapped,
    s_send, s_got, s_total, s_all, s_out,
    rs_send, rs_recv, rs_local, pair_send, pair_recv, load_sem, lhs_sem, w_sem, slope_sem,
    sm_send, sm_recv, smz_send, smz_recv, store_sem, swap_send, swap_recv,
):
    p = Place()
    rows, width = gh.shape
    slots = lengths.shape[0]
    seq = rows // slots
    planes = [lax.rem(p.f + k, 8) for k in range(1, 8)]
    levels = [lax.rem(p.z + k, 4) for k in range(1, 4)]
    barrier = pltpu.get_barrier_semaphore()
    for g in planes:
        pl.semaphore_signal(barrier, inc=1, device_id=p.dev(f=g), device_id_type=MESH)
    for g in levels:
        pl.semaphore_signal(barrier, inc=1, device_id=p.dev(z=g), device_id_type=MESH)

    mine = pl.ds(pl.multiple_of(p.core * rows, rows), rows)

    def lhs_copies(i):
        if i < 4:
            return [
                pltpu.make_async_copy(
                    act_pair.at[:, pl.ds(chip * 512 + i * 128, 128)],
                    lhs.at[i % 2, :, pl.ds(chip * 128, 128)],
                    lhs_sem.at[i, chip],
                )
                for chip in range(4)
            ]
        src = (first_pair, mixed_pair, tok_pair)[i - 4]
        return [pltpu.make_async_copy(src, lhs.at[i % 2], lhs_sem.at[i, 0])]

    def w_copy(i):
        if i < 8:
            j = i // 2
            src = wu.at[:, pl.ds(j * 1024, 1024)] if i % 2 else wd.at[pl.ds(j * 1024, 1024)]
        elif i == 8:
            src = wo
        else:
            src = wq.at[:, pl.ds((i - 9) * 1024, 1024)]
        return pltpu.make_async_copy(src, wbuf.at[i % 2], w_sem.at[i])

    def slope_copy(j):
        return pltpu.make_async_copy(slope.at[:, pl.ds(j * 1024, 1024)], slope_v.at[j % 2], slope_sem.at[j])

    loads = [
        pltpu.make_async_copy(src, dst, load_sem.at[i])
        for i, (src, dst) in enumerate(
            (
                (branch_pair, branch), (gh2, gh), (qkv, gq.at[mine]), (norm_in, norm), (inv_in, inv),
                (params_in, params), (sums_in, sums_v),
            )
        )
    ]
    for c in lhs_copies(0):
        c.start()
    loads[0].start()
    for c in lhs_copies(1):
        c.start()
    w_copy(0).start()
    slope_copy(0).start()
    for c in loads[1:]:
        c.start()

    def out_at(b, at):
        if b < 4:
            return out_d.at[pl.ds(128 * b, 128)].at[at]
        if b < 8:
            return out_u.at[at, pl.ds((b - 4) * 1024, 1024)]
        if b == 8:
            return out_o.at[at]
        return out_q.at[at, pl.ds((b - 9) * 1024, 1024)]

    red = Reduce(
        p, prod, got_x, got_y, end_x, end_y, from_end, from_mid, swapped, out_at, rs_send, rs_recv, rs_local,
        swap_send, swap_recv,
    )

    def produce(b, left, right):
        prod[b] = dot_tn(left, right).astype(BF16).reshape(2, 2, 128, 1024)
        red.produced(b)

    def to_pair(index, ref, cols):
        here = ref.at[mine, cols]
        return remote(here, here, pair_send.at[index], pair_recv.at[index], p.dev(f=p.fs))

    pl.semaphore_wait(barrier, 10)
    loads[0].wait()
    for b in range(4):
        for c in lhs_copies(b):
            c.wait()
        produce(b, lhs[b % 2], branch[...])
        for c in lhs_copies(b + 2) if b < 4 else ():
            c.start()
    loads[1].wait()

    def block_cols(j):
        return pl.ds(j * 1024, 1024)

    def up_block(j):
        to_pair(j, gi, block_cols(j)).wait_recv()
        produce(4 + j, lhs[0], gi[:, j * 1024 : (j + 1) * 1024])

    for j in range(4):
        w_copy(2 * j).wait()
        w_copy(2 * j + 1).start()
        slope_copy(j).wait()
        if j < 3:
            slope_copy(j + 1).start()
        inner = (dot_nt(branch[mine], wbuf[0]) * slope_v[j % 2].astype(F32)).astype(BF16)
        gi[mine, j * 1024 : (j + 1) * 1024] = inner
        to_pair(j, gi, block_cols(j)).start()
        upsum[j : j + 1] = jnp.sum(inner.astype(F32), axis=0, keepdims=True)
        w_copy(2 * j + 1).wait()
        w_copy(2 * j + 2).start()
        gh[...] += dot_nt(gi[mine, j * 1024 : (j + 1) * 1024], wbuf[1])
        if j == 0:
            for c in lhs_copies(4):
                c.wait()
        if j > 0:
            up_block(j - 1)
            red.tick()
    for c in loads[2:]:
        c.wait()
    ga = branch
    e = gh[...]
    scaled = e * params[6:7]
    n = norm[...]
    sums_v[3:4] = jnp.sum(e, axis=0, keepdims=True)
    sums_v[4:5] = jnp.sum(e * n, axis=0, keepdims=True)
    gh[...] = inv[:, 0:1] * (scaled - row_mean(scaled) - n * row_mean(scaled * n))
    ga[mine] = gh[...].astype(BF16)
    whole = pl.ds(0, 1024)
    to_pair(4, ga, whole).start()
    sums_v[5:6] = jnp.sum(ga[mine].astype(F32), axis=0, keepdims=True)
    up_block(3)
    for c in lhs_copies(6):
        c.start()
    w_copy(8).wait()
    w_copy(9).start()
    gm[...] = dot_nt(ga[mine], wbuf[0]).astype(BF16)
    w_copy(10).start()
    for c in lhs_copies(5):
        c.wait()
    to_pair(4, ga, whole).wait_recv()
    produce(8, lhs[1], ga[...])
    red.tick()

    left = lax.broadcasted_iota(jnp.int32, (seq, 128), 1) < HEAD_SIZE
    key_row = lax.broadcasted_iota(jnp.int32, (seq, seq), 0)
    scale = 1.0 / math.sqrt(HEAD_SIZE)

    def attend(step, carry):
        slot, pair_of = lax.rem(step, slots), lax.div(step, slots)
        at_rows = pl.ds(pl.multiple_of(slot * seq, seq), seq)
        own_rows = pl.ds(pl.multiple_of(p.core * rows + slot * seq, seq), seq)
        col = pl.multiple_of(pair_of * 128, 128)
        at_q = pl.ds(col, 128)
        at_k = pl.ds(pl.multiple_of(width + col, 128), 128)
        at_v = pl.ds(pl.multiple_of(2 * width + col, 128), 128)
        q, k, v = gq[own_rows, at_q], gq[own_rows, at_k], gq[own_rows, at_v]
        do = gm[at_rows, at_q]
        dead = key_row >= lengths[slot]
        parts = []
        for head in range(2):
            lanes = left if head == 0 else ~left
            k_head = jnp.where(lanes, k, jnp.zeros_like(k))
            v_head = jnp.where(lanes, v, jnp.zeros_like(v))
            scores = jnp.where(dead, -1e30, dot_nt(k_head, q) * scale)
            exps = jnp.exp(scores - jnp.max(scores, axis=0, keepdims=True))
            probs = exps * (1.0 / jnp.sum(exps, axis=0, keepdims=True))
            d_probs = dot_nt(v_head, do)
            shared = jnp.sum(probs * d_probs, axis=0, keepdims=True)
            d_scores = (probs * (d_probs - shared)).astype(BF16)
            parts.append(
                (dot_tn(d_scores, k) * scale, dot_nn(d_scores, q) * scale, dot_nn(probs.astype(BF16), do))
            )
        for at, one, two in zip((at_q, at_k, at_v), *parts):
            gq[own_rows, at] = jnp.where(left, one, two).astype(BF16)
        return carry

    steps = 8 * slots
    for quarter in range(4):
        lax.fori_loop(quarter * steps // 4, (quarter + 1) * steps // 4, attend, 0)
        if quarter % 2:
            for j in range(3):
                to_pair(5 + 3 * (quarter // 2) + j, gq, pl.ds(j * 1024 + 512 * (quarter // 2), 512)).start()
        red.tick()
    for c in lhs_copies(6):
        c.wait()
    for j in range(3):
        for half in range(2):
            to_pair(5 + 3 * half + j, gq, pl.ds(j * 1024 + 512 * half, 512)).wait_recv()
        produce(9 + j, lhs[0], gq[:, j * 1024 : (j + 1) * 1024])
    sums_v[6:7] = jnp.sum(gq[mine, 0:1024].astype(F32), axis=0, keepdims=True)
    sums_v[7:8] = jnp.sum(gq[mine, 2048:3072].astype(F32), axis=0, keepdims=True)

    order = (6, 7, 5, 3, 2, 1, 4, 0)
    for g in range(8):
        cols = slice(g * 128, (g + 1) * 128)
        for i, row in enumerate(order):
            s_send[g, i : i + 1] = sums_v[row : row + 1, cols]
        for i in range(4):
            lo = (g % 2) * 512 + i * 128
            s_send[g, 8 + i : 9 + i] = upsum[g // 2 : g // 2 + 1, lo : lo + 128]

    def small_to(k):
        g = planes[k]
        return remote(s_send.at[g], s_got.at[p.f], sm_send.at[k], sm_recv.at[k], p.dev(f=g))

    def small_from(k):
        g = lax.rem(p.f + 7 - k, 8)
        return remote(s_send.at[g], s_got.at[g], sm_send.at[k], sm_recv.at[k], p.dev(f=g))

    def level_to(k):
        return remote(s_total, s_all.at[p.z], smz_send.at[k], smz_recv.at[k], p.dev(z=levels[k]))

    def level_from(k):
        g = lax.rem(p.z + 3 - k, 4)
        return remote(s_total, s_all.at[g], smz_send.at[k], smz_recv.at[k], p.dev(z=g))

    for k in range(7):
        small_to(k).start()
    s_got[p.f] = s_send[p.f]

    for j in range(3):
        w_copy(9 + j).wait()
        gh[...] += dot_nt(gq[mine, j * 1024 : (j + 1) * 1024], wbuf[(9 + j) % 2])
        if j == 0:
            w_copy(11).start()
    store = pltpu.make_async_copy(gh, token_grad, store_sem.at[0])
    store.start()
    red.tick()
    for k in range(7):
        small_from(k).wait_recv()
    total = s_got[0]
    for g in range(1, 8):
        total = total + s_got[g]
    s_total[...] = total
    for k in range(3):
        level_to(k).start()
    s_all[p.z] = total
    red.tick()
    red.tick()
    for k in range(3):
        level_from(k).wait_recv()
    s_out[...] = (s_all[0] + s_all[1]) + (s_all[2] + s_all[3])
    small_store = pltpu.make_async_copy(s_out, small_out, store_sem.at[1])
    small_store.start()
    for k in range(7):
        small_to(k).wait_send()
    for k in range(3):
        level_to(k).wait_send()
    for j in range(4):
        to_pair(j, gi, block_cols(j)).wait_send()
    to_pair(4, ga, whole).wait_send()
    for j in range(3):
        for half in range(2):
            to_pair(5 + 3 * half + j, gq, pl.ds(j * 1024 + 512 * half, 512)).wait_send()
    store.wait()
    small_store.wait()
    red.rest()


def backward_call(lengths, saved):
    wq, wo, wu, wd, qkv, slope = saved[:6]
    rows, width = qkv.shape[0], wo.shape[0]
    ff = wu.shape[1]
    anyspace = pl.BlockSpec(memory_space=pl.ANY)
    shape = jax.ShapeDtypeStruct
    dma = pltpu.SemaphoreType.DMA
    outs = [
        shape((rows, width), F32),
        shape((width // 8, 3 * width), BF16),
        shape((width // 8, width), BF16),
        shape((width // 8, ff), BF16),
        shape((ff // 8, width), BF16),
        shape((16, 128), F32),
    ]
    scratch = [
        pltpu.VMEM((2, 2 * rows, 512), BF16),
        pltpu.VMEM((2, 1024, 1024), BF16),
        pltpu.VMEM((2, rows, 1024), BF16),
        pltpu.VMEM((2 * rows, width), BF16),
        pltpu.VMEM((2 * rows, ff), BF16),
        pltpu.VMEM((2 * rows, 3 * width), BF16),
        pltpu.VMEM((rows, width), BF16),
        pltpu.VMEM((rows, width), F32),
        pltpu.VMEM((rows, width), F32),
        pltpu.VMEM((rows, 128), F32),
        pltpu.VMEM((16, width), F32),
        pltpu.VMEM((8, width), F32),
        pltpu.VMEM((4, width), F32),
        pltpu.VMEM((BLOCKS, 2, 2, 128, 1024), BF16),
        pltpu.VMEM((BLOCKS, 2, 64, 1024), BF16),
        pltpu.VMEM((BLOCKS, 2, 64, 1024), BF16),
        pltpu.VMEM((BLOCKS, 64, 1024), BF16),
        pltpu.VMEM((BLOCKS, 64, 1024), BF16),
        pltpu.VMEM((BLOCKS, 128, 1024), BF16),
        pltpu.VMEM((BLOCKS, 64, 1024), BF16),
        pltpu.VMEM((len(SHARED), 2, 2, 64, 1024), BF16),
        pltpu.VMEM((8, 16, 128), F32),
        pltpu.VMEM((8, 16, 128), F32),
        pltpu.VMEM((16, 128), F32),
        pltpu.VMEM((4, 16, 128), F32),
        pltpu.VMEM((16, 128), F32),
        dma((10, len(PIECES))),
        dma((10, len(PIECES))),
        dma((len(PIECES),)),
        dma((11,)),
        dma((11,)),
        dma((7,)),
        dma((7, 4)),
        dma((12,)),
        dma((4,)),
        dma((7,)),
        dma((7,)),
        dma((3,)),
        dma((3,)),
        dma((2,)),
        dma((len(SHARED), 2)),
        dma((len(SHARED), 2)),
    ]
    return pl.pallas_call(
        backward_kernel,
        out_shape=outs,
        in_specs=[pl.BlockSpec(memory_space=pltpu.SMEM)] + [anyspace] * len(saved),
        out_specs=[anyspace] * len(outs),
        scratch_shapes=scratch,
        name="backward",
        cost_estimate=pl.CostEstimate(flops=4 * 512 * 12582912, bytes_accessed=60 * MIB, transcendentals=4 * MIB),
        compiler_params=pltpu.CompilerParams(
            collective_id=1, has_side_effects=True, vmem_limit_bytes=60 * MIB
        ),
    )(lengths, *saved)


def finish_kernel(
    layer_in, token_in, q_in, o_in, u_in, d_in, small,
    layer_out, token_out, q_out, o_out, u_out, d_out, biases_out, up_bias_out, gains_out,
    q_low, o_low, u_low, d_low, layer_v, token_v, small_v, q, o, u, d, sem,
):
    sources = (d_in, u_in, q_in, o_in, token_in, layer_in, small)
    lows, wides = (d_low, u_low, q_low, o_low, token_v, layer_v, small_v), (d, u, q, o, token_v, layer_v)
    results = (d_out, u_out, q_out, o_out, token_out, layer_out)
    ins = [pltpu.make_async_copy(a, b, sem.at[i]) for i, (a, b) in enumerate(zip(sources, lows))]
    outs = [pltpu.make_async_copy(a, b, sem.at[7 + i]) for i, (a, b) in enumerate(zip(wides, results))]
    for c in ins:
        c.start()
    for a, b, c_in, c_out in zip(lows, wides, ins, outs):
        c_in.wait()
        if a is not b:
            b[...] = a[...].astype(F32)
        c_out.start()
    ins[-1].wait()
    biases_out[...] = small_v[0:6]
    gains_out[...] = small_v[6:8]
    for i in range(4):
        up_bias_out[i * 128 : (i + 1) * 128] = small_v[8 + i]
    for c in outs:
        c.wait()


def finish_call(layer_out, token_grad, weight_grads, small):
    anyspace = pl.BlockSpec(memory_space=pl.ANY)
    vmem = pl.BlockSpec(memory_space=pltpu.VMEM)
    shape = jax.ShapeDtypeStruct
    wide = [shape(g.shape, F32) for g in weight_grads]
    outs = [
        shape(layer_out.shape, BF16), shape(token_grad.shape, F32), *wide,
        shape((6, 128), F32), shape((512,), F32), shape((2, 128), F32),
    ]
    return pl.pallas_call(
        finish_kernel,
        out_shape=outs,
        in_specs=[anyspace] * 7,
        out_specs=[anyspace] * 6 + [vmem] * 3,
        scratch_shapes=[pltpu.VMEM(g.shape, BF16) for g in weight_grads]
        + [pltpu.VMEM(g.shape, g.dtype) for g in (layer_out, token_grad, small)]
        + [pltpu.VMEM(g.shape, F32) for g in weight_grads]
        + [pltpu.SemaphoreType.DMA((13,))],
        name="finish",
        compiler_params=pltpu.CompilerParams(vmem_limit_bytes=60 * MIB),
    )(layer_out, token_grad, *weight_grads, small)


def plane(
    tokens,
    lengths,
    cotangent,
    qkv_weight,
    out_weight,
    up_weight,
    down_weight,
    biases,
    up_bias,
    gains,
):
    small_in = pack_small(biases, up_bias, gains)
    layer_out, *saved = forward_call(
        tokens, lengths, cotangent, qkv_weight, out_weight, up_weight, down_weight, small_in
    )
    token_grad, *weight_grads, small = backward_call(lengths, saved)
    return tuple(finish_call(layer_out, token_grad, weight_grads, small))


def solution(mesh):
    step = plane if dict(mesh.shape) == {"fsdp": 8, "rep": 4} else portable
    both = ("fsdp", "rep")
    in_specs = (
        P(both, None),
        P(both),
        P(both, None),
        P("fsdp", None),
        P("fsdp", None),
        P("fsdp", None),
        P("fsdp", None),
        P(None, "fsdp"),
        P("fsdp"),
        P(None, "fsdp"),
    )
    out_specs = (
        P(both, None),
        P(both, None),
        P("fsdp", None),
        P("fsdp", None),
        P("fsdp", None),
        P("fsdp", None),
        P(None, "fsdp"),
        P("fsdp"),
        P(None, "fsdp"),
    )
    return jax.shard_map(
        step, mesh=mesh, in_specs=in_specs, out_specs=out_specs, check_vma=False
    )
```

```python
import math

import jax
import jax.numpy as jnp
from jax import lax
from jax.experimental import pallas as pl
from jax.experimental.pallas import tpu as pltpu
from jax.sharding import PartitionSpec as P

HEAD_SIZE = 64


def matmul(left_side, right_side):
    return jnp.dot(left_side, right_side, preferred_element_type=jnp.float32)


def transposed_left(left_side, right_side):
    return lax.dot_general(
        left_side, right_side, (((0,), (0,)), ((), ())), preferred_element_type=jnp.float32
    )


def transposed_right(left_side, right_side):
    return lax.dot_general(
        left_side, right_side, (((1,), (1,)), ((), ())), preferred_element_type=jnp.float32
    )


def column_sum(values):
    return jnp.sum(values.astype(jnp.float32), axis=0)


def row_mean(values):
    return jnp.mean(values, axis=-1, keepdims=True)


def normalize(hidden):
    center = hidden - row_mean(hidden)
    inverse = lax.rsqrt(row_mean(center * center) + 1e-05)
    return center * inverse, inverse


def norm_back(grad, norm, inverse, gain):
    scaled = grad * gain
    return inverse * (scaled - row_mean(scaled) - norm * row_mean(scaled * norm))


def low(values):
    return values.astype(jnp.bfloat16)


def gather_small(biases, up_bias, gains):
    width, up_width = biases.shape[1], up_bias.shape[0]
    packed = jnp.concatenate([biases.reshape(-1), gains.reshape(-1), up_bias])
    everyone = lax.all_gather(packed, "fsdp", axis=0, tiled=False).astype(jnp.float32)
    rows = everyone[:, : 8 * width].reshape(-1, 8, width).transpose(1, 0, 2).reshape(8, -1)
    return rows[:6], everyone[:, 8 * width : 8 * width + up_width].reshape(-1), rows[6:]


def reduce_weight(grad):
    shard = lax.psum_scatter(low(grad), "fsdp", scatter_dimension=0, tiled=True)
    return lax.psum(shard, "rep").astype(jnp.float32)


def portable(
    tokens,
    lengths,
    cotangent,
    qkv_weight,
    out_weight,
    up_weight,
    down_weight,
    biases,
    up_bias,
    gains,
):
    slots = lengths.shape[0]
    rows, width = tokens.shape
    seq = rows // slots
    heads = width // HEAD_SIZE
    scale = 1.0 / math.sqrt(HEAD_SIZE)
    w_qkv = lax.all_gather(qkv_weight, "fsdp", axis=0, tiled=True)
    w_out = lax.all_gather(out_weight, "fsdp", axis=0, tiled=True)
    w_up = lax.all_gather(up_weight, "fsdp", axis=0, tiled=True)
    w_down = lax.all_gather(down_weight, "fsdp", axis=0, tiled=True)
    bias_rows, bias_up, gain_rows = gather_small(biases, up_bias, gains)

    def split(values):
        return values.reshape(slots, seq, heads, HEAD_SIZE)

    def join(values):
        return values.reshape(rows, width)

    sums = matmul(tokens, w_qkv)
    query = split(low(sums[:, :width] + bias_rows[0]))
    key = split(low(sums[:, width : 2 * width]))
    value = split(low(sums[:, 2 * width :] + bias_rows[1]))
    live = jnp.arange(seq)[None, :] < lengths[:, None]
    scores = scale * jnp.einsum(
        "bshd,bthd->bhst", query, key, preferred_element_type=jnp.float32
    )
    scores = jnp.where(live[:, None, None, :], scores, -1e30)
    exps = jnp.exp(scores - jnp.max(scores, axis=-1, keepdims=True))
    probs = exps / jnp.sum(exps, axis=-1, keepdims=True)
    probs_low = low(probs)
    mixed = low(
        join(jnp.einsum("bhst,bthd->bshd", probs_low, value, preferred_element_type=jnp.float32))
    )
    first, first_inverse = normalize(
        tokens.astype(jnp.float32) + matmul(mixed, w_out) + bias_rows[2]
    )
    first_norm = first * gain_rows[0] + bias_rows[3]
    first_low = low(first_norm)
    inner = matmul(first_low, w_up) + bias_up
    cumulative = 0.5 * (1.0 + lax.erf(inner * math.sqrt(0.5)))
    act_low = low(inner * cumulative)
    slope = low(cumulative + inner * jnp.exp(-0.5 * inner * inner) / math.sqrt(2.0 * math.pi))
    second, second_inverse = normalize(first_norm + matmul(act_low, w_down) + bias_rows[4])
    layer_out = low(second * gain_rows[1] + bias_rows[5])

    grad_out = cotangent * live.reshape(rows, 1).astype(jnp.float32)
    grad_h2 = norm_back(grad_out, second, second_inverse, gain_rows[1])
    grad_branch = low(grad_h2)
    down_grad = reduce_weight(transposed_left(act_low, grad_branch))
    grad_inner = low(transposed_right(grad_branch, w_down) * slope)
    up_grad = reduce_weight(transposed_left(first_low, grad_inner))
    grad_first = grad_h2 + transposed_right(grad_inner, w_up)
    grad_h1 = norm_back(grad_first, first, first_inverse, gain_rows[0])
    grad_attn = low(grad_h1)
    out_grad = reduce_weight(transposed_left(mixed, grad_attn))
    grad_mixed = split(low(transposed_right(grad_attn, w_out)))
    grad_probs = jnp.einsum(
        "bshd,bthd->bhst", grad_mixed, value, preferred_element_type=jnp.float32
    )
    shared = jnp.sum(probs * grad_probs, axis=-1, keepdims=True)
    grad_scores = low(probs * (grad_probs - shared))
    grad_query = scale * jnp.einsum(
        "bhst,bthd->bshd", grad_scores, key, preferred_element_type=jnp.float32
    )
    grad_key = scale * jnp.einsum(
        "bhst,bshd->bthd", grad_scores, query, preferred_element_type=jnp.float32
    )
    grad_value = jnp.einsum(
        "bhst,bshd->bthd", probs_low, grad_mixed, preferred_element_type=jnp.float32
    )
    grad_qkv = jnp.concatenate(
        [join(low(grad_query)), join(low(grad_key)), join(low(grad_value))], axis=1
    )
    qkv_grad = reduce_weight(transposed_left(tokens, grad_qkv))
    token_grad = grad_h1 + transposed_right(grad_qkv, w_qkv)
    small = jnp.stack(
        [
            column_sum(grad_qkv[:, :width]),
            column_sum(grad_qkv[:, 2 * width :]),
            column_sum(grad_attn),
            column_sum(grad_first),
            column_sum(grad_branch),
            column_sum(grad_out),
            column_sum(grad_first * first),
            column_sum(grad_out * second),
        ]
    )
    owner = lax.axis_index("fsdp")
    small, up_sum = lax.psum((small, column_sum(grad_inner)), ("fsdp", "rep"))
    own, own_up = biases.shape[1], up_bias.shape[0]
    small = lax.dynamic_slice(small, (0, owner * own), (8, own))
    up_bias_grad = lax.dynamic_slice(up_sum, (owner * own_up,), (own_up,))
    return (
        layer_out,
        token_grad,
        qkv_grad,
        out_grad,
        up_grad,
        down_grad,
        small[:6],
        up_bias_grad,
        small[6:],
    )


MESH = pl.DeviceIdType.MESH
F32 = jnp.float32
BF16 = jnp.bfloat16
MIB = 1 << 20


def dot_nn(a, b):
    return lax.dot_general(a, b, (((1,), (0,)), ((), ())), preferred_element_type=F32)


def dot_nt(a, b):
    return lax.dot_general(a, b, (((1,), (1,)), ((), ())), preferred_element_type=F32)


def dot_tn(a, b):
    return lax.dot_general(a, b, (((0,), (0,)), ((), ())), preferred_element_type=F32)


class Place:
    def __init__(self):
        f, z = lax.axis_index("fsdp"), lax.axis_index("rep")
        self.f, self.z = f, z
        self.core = lax.rem(f, 2)
        self.x = lax.rem(lax.div(f, 2), 2)
        self.y = lax.div(f, 4)
        self.chip = lax.div(f, 2)
        self.fx = f + 2 - 4 * self.x
        self.fy = f + 4 - 8 * self.y
        self.fd = self.fx + 4 - 8 * self.y
        self.fs = f + 1 - 2 * self.core
        self.par = lax.rem(z, 2)
        self.zn = z + 1 - 2 * self.par

    def dev(self, f=None, z=None):
        return {"fsdp": self.f if f is None else f, "rep": self.z if z is None else z}


def remote(src, dst, send_sem, recv_sem, device):
    return pltpu.make_async_remote_copy(
        src_ref=src, dst_ref=dst, send_sem=send_sem, recv_sem=recv_sem,
        device_id=device, device_id_type=MESH,
    )


UNITS = (
    ("q", 0, 32, 0),
    ("q", 32, 32, 0),
    ("q", 64, 32, 0),
    ("q", 96, 32, 0),
    ("o", 0, 128, 0),
    ("u", 0, 64, 0),
    ("u", 64, 64, 0),
    ("d", 0, 128, 0),
    ("d", 128, 128, 0),
    ("d", 256, 128, 16),
    ("d", 384, 128, 16),
)
FORWARD_PLAN = (
    ("direct", 0), ("direct", 1), ("direct", 2), ("direct", 3), ("small", 0), ("fx", 0), ("fy", 0),
    ("direct", 4), ("fx", 1), ("fy", 1), ("fx", 2), ("fy", 2), ("r2", 0), ("fx", 3), ("fy", 3), ("r3", 0),
    ("r5", 0), ("r4", 0), ("r2", 1), ("r3", 1), ("direct", 5), ("fx", 4), ("fy", 4), ("r2", 2), ("r5", 1),
    ("r4", 1), ("r3", 2), ("r5", 2), ("r4", 2), ("r2", 3), ("r5", 3), ("r4", 3), ("r3", 3), ("direct", 6),
    ("done", 0), ("done", 1), ("done", 2), ("done", 3), ("qkv", 0), ("fx", 5), ("fy", 5), ("r2", 4),
    ("r3", 4), ("at", 0, 1), ("r4", 4), ("r5", 4), ("at", 1, 4), ("direct", 7), ("at", 4, 6), ("fx", 6),
    ("fy", 6), ("at", 6, 8), ("r2", 5), ("at", 8, 12), ("r4", 5), ("r5", 5), ("direct", 8), ("at", 12, 13),
    ("r3", 5), ("at", 13, 14), ("fx", 7), ("fy", 7), ("at", 14, 16), ("done", 4), ("out", 0), ("r2", 6),
    ("r4", 6), ("r5", 6), ("direct", 9), ("fx", 8), ("fy", 8), ("r3", 6), ("direct", 10), ("r5", 7),
    ("r4", 7), ("done", 5), ("done", 6), ("up", 0, 1), ("r2", 7), ("up", 1, 2), ("fx", 9), ("fy", 9),
    ("up", 2, 3), ("r3", 7), ("up", 3, 4), ("r4", 8), ("r5", 8), ("up", 4, 5), ("r2", 8), ("up", 5, 7),
    ("fx", 10), ("fy", 10), ("r3", 8), ("up", 7, 8), ("r2", 9), ("r4", 9), ("r5", 9), ("done", 7), ("dn", 7),
    ("r3", 9), ("done", 8), ("dn", 8), ("r2", 10), ("r4", 10), ("r5", 10), ("done", 9), ("tidy", 0),
    ("dn", 9), ("r3", 10), ("done", 10), ("dn", 10), ("last", 0),
)
KINDS = 13


class Gather:
    def __init__(self, place, unit, shard, full, base, rows, extra, send, recv, local):
        self.p, self.unit, self.shard, self.full = place, unit, shard, full
        self.base, self.rows, self.size = base, rows, shard.shape[0]
        self.send_sem, self.recv_sem, self.local_sem = send, recv, local
        p, half = place, rows // 2
        one, two = half * p.par, half * (1 - p.par)
        wide, rest = half + extra, half - extra
        near_x, near_y = rest * p.par, rest * (1 - p.par)
        far_x, far_y = wide * (1 - p.par), wide * p.par
        to_x, to_y, to_s, to_z = p.dev(f=p.fx), p.dev(f=p.fy), p.dev(f=p.fs), p.dev(z=p.zn)
        sx, sy, sd = (g + 1 - 2 * p.core for g in (p.fx, p.fy, p.fd))
        self.table = (
            ((p.fx, near_x), (p.f, near_x), wide, to_x),
            ((p.fy, near_y), (p.f, near_y), wide, to_y),
            ((p.fx, far_x), (p.fx, far_y), rest, to_z),
            ((p.fy, far_y), (p.fy, far_x), rest, to_z),
            ((p.fd, one), (p.fx, one), half, to_y),
            ((p.fd, two), (p.fy, two), half, to_x),
            ((p.fs, 0), (p.f, 0), rows, to_s),
            ((sx, near_x), (p.fx, near_x), wide, to_s),
            ((sy, near_y), (p.fy, near_y), wide, to_s),
            ((sx, far_x), (p.fx, far_x), rest, to_s),
            ((sy, far_y), (p.fy, far_y), rest, to_s),
            ((sd, one), (p.fd, one), half, to_s),
            ((sd, two), (p.fd, two), half, to_s),
        )

    def at(self, owner, lo, n):
        return self.full.at[pl.ds(pl.multiple_of(owner * self.size + self.base + lo, 16), n)]

    def copy(self, kind, sending):
        received, sent, n, device = self.table[kind]
        owner, lo = sent if sending else received
        here = self.at(owner, lo, n)
        src = self.shard.at[pl.ds(pl.multiple_of(self.base + lo, 16), n)] if kind in (0, 1, 6) else here
        return remote(src, here, self.send_sem.at[self.unit, kind], self.recv_sem.at[self.unit, kind], device)

    def start(self, *kinds):
        for kind in kinds:
            self.copy(kind, True).start()

    def got(self, *kinds):
        for kind in kinds:
            self.copy(kind, False).wait_recv()

    def sent(self):
        for kind in range(KINDS):
            self.copy(kind, True).wait_send()

    def own(self):
        src = self.shard.at[pl.ds(self.base, self.rows)]
        return pltpu.make_async_copy(src, self.at(self.p.f, 0, self.rows), self.local_sem.at[self.unit])

    def direct(self):
        self.start(0, 1, 6)
        self.own().start()

    def pass_on(self, arrived, *kinds):
        self.got(arrived)
        self.start(*kinds)

    def done(self):
        self.got(6, 7, 8, 9, 10, 11, 12)
        self.own().wait()


def forward_kernel(
    lengths, tokens, cot, small, sh_q, sh_o, sh_u, sh_d,
    layer_out, wq_out, wo_out, wu_out, wd_out, qkv_out, slope_out, act_pair, first_pair, mixed_pair,
    tok_pair, branch_pair, norm_out, inv_out, grad_out_ref, params_out, sums_out,
    x, wq, wo, wu, wd, qkv, mixed, norm, first_low, act, slope, acc, cot_v, gh2, out_v, gb, smalls, params,
    inv_v, sums, up_rows,
    ag_send, ag_recv, ag_local, sm_send, sm_recv, sm_local, io, pair_send, pair_recv, pair_local, wd_sem,
):
    p = Place()
    rows, width = x.shape
    slots = lengths.shape[0]
    seq = rows // slots
    others = [lax.rem(p.f + k, 8) for k in range(1, 8)]
    barrier = pltpu.get_barrier_semaphore()
    for g in others:
        pl.semaphore_signal(barrier, inc=1, device_id=p.dev(f=g), device_id_type=MESH)
    pl.semaphore_signal(barrier, inc=1, device_id=p.dev(z=p.zn), device_id_type=MESH)
    loads = [
        pltpu.make_async_copy(tokens, x, io.at[0]),
        pltpu.make_async_copy(cot, cot_v, io.at[1]),
        pltpu.make_async_copy(small, smalls.at[p.f], sm_local),
    ]
    for c in loads:
        c.start()
    pl.semaphore_wait(barrier, 8)

    def small_copy(k, owner, device):
        return remote(small, smalls.at[owner], sm_send.at[k], sm_recv.at[k], device)

    for k, g in enumerate(others):
        small_copy(k, p.f, p.dev(f=g)).start()

    weights = {"q": (sh_q, wq), "o": (sh_o, wo), "u": (sh_u, wu), "d": (sh_d, wd)}
    parts = [Gather(p, i, *weights[n], *piece, ag_send, ag_recv, ag_local) for i, (n, *piece) in enumerate(UNITS)]

    mine = pl.ds(pl.multiple_of(p.core * rows, rows), rows)

    def pair(index, chip, src, dst, cols):
        own = pl.ds(pl.multiple_of((2 * chip + p.core) * cols, cols), cols)
        other = pl.ds(pl.multiple_of((2 * chip + 1 - p.core) * cols, cols), cols)
        here = dst.at[mine, pl.ds(chip * cols, cols)]
        return (
            pltpu.make_async_copy(src.at[:, own], here, pair_local.at[index, chip]),
            remote(src.at[:, other], here, pair_send.at[index, chip], pair_recv.at[index, chip], p.dev(f=p.fs)),
        )

    pairs = []

    def start_pair(index, src, dst, cols, chips=range(4)):
        for chip in chips:
            for c in pair(index, chip, src, dst, cols):
                c.start()
            pairs.append((index, chip, src, dst, cols))

    stores = []

    def store(src, dst, sem):
        stores.append(pltpu.make_async_copy(src, dst, sem))
        stores[-1].start()

    def small_params(_):
        loads[0].wait()
        start_pair(0, x, tok_pair, 128)
        loads[2].wait()
        for k in range(7):
            back = lax.rem(p.f + 7 - k, 8)
            small_copy(k, back, p.dev(f=back)).wait_recv()
        for g in range(8):
            part = smalls[g].astype(F32)
            params[:, g * 128 : (g + 1) * 128] = part
            for j in range(4):
                up_rows[g : g + 1, j * 128 : (j + 1) * 128] = part[8 + j : 9 + j]

    def project(_):
        store(wq, wq_out, io.at[2])
        for j in range(3):
            part = dot_nn(x[...], wq[:, j * width : (j + 1) * width])
            if j == 0:
                part = part + params[0:1]
            if j == 2:
                part = part + params[1:2]
            qkv[:, j * width : (j + 1) * width] = part.astype(BF16)
        store(qkv, qkv_out, io.at[3])

    left = lax.broadcasted_iota(jnp.int32, (seq, 128), 1) < HEAD_SIZE
    key_row = lax.broadcasted_iota(jnp.int32, (seq, seq), 0)

    def attend(step, carry):
        slot, pair_of = lax.div(step, 8), lax.rem(step, 8)
        at_rows = pl.ds(pl.multiple_of(slot * seq, seq), seq)
        col = pl.multiple_of(pair_of * 128, 128)
        q = qkv[at_rows, pl.ds(col, 128)]
        k = qkv[at_rows, pl.ds(pl.multiple_of(width + col, 128), 128)]
        v = qkv[at_rows, pl.ds(pl.multiple_of(2 * width + col, 128), 128)]
        dead = key_row >= lengths[slot]
        outs = []
        for head in range(2):
            k_head = jnp.where(left if head == 0 else ~left, k, jnp.zeros_like(k))
            scores = dot_nt(k_head, q) * (1.0 / math.sqrt(HEAD_SIZE))
            scores = jnp.where(dead, -1e30, scores)
            exps = jnp.exp(scores - jnp.max(scores, axis=0, keepdims=True))
            probs = exps * (1.0 / jnp.sum(exps, axis=0, keepdims=True))
            outs.append(dot_tn(probs.astype(BF16), v))
        mixed[at_rows, pl.ds(col, 128)] = jnp.where(left, outs[0], outs[1]).astype(BF16)
        return carry

    steps = 8 * slots

    def attention(first, last):
        lax.fori_loop(first * steps // 16, last * steps // 16, attend, 0)
        if last == 16:
            start_pair(1, mixed, mixed_pair, 128)

    def first_norm(_):
        store(wo, wo_out, io.at[4])
        hidden = x[...].astype(F32) + dot_nn(mixed[...], wo[...]) + params[2:3]
        center = hidden - row_mean(hidden)
        inverse = lax.rsqrt(row_mean(center * center) + 1e-05)
        norm[...] = center * inverse
        inv_v[...] = jnp.broadcast_to(inverse, inv_v.shape)
        shifted = norm[...] * params[6:7] + params[3:4]
        first_low[...] = shifted.astype(BF16)
        acc[...] = shifted + params[4:5]
        start_pair(2, first_low, first_pair, 128)
        store(norm, norm_out, io.at[5])
        store(inv_v, inv_out, io.at[6])

    def up_step(j, carry):
        cols = pl.ds(pl.multiple_of(j * 512, 512), 512)
        inner = dot_nn(first_low[...], wu[:, cols]) + up_rows[pl.ds(j, 1), :]
        phi = 0.5 * (1.0 + lax.erf(inner * math.sqrt(0.5)))
        act[:, cols] = (inner * phi).astype(BF16)
        density = jnp.exp(-0.5 * inner * inner) * (1.0 / math.sqrt(2.0 * math.pi))
        slope[:, cols] = (phi + inner * density).astype(BF16)
        return carry

    def up(first, last):
        if first == 0:
            store(wu, wu_out, io.at[7])
        lax.fori_loop(first, last, up_step, 0)
        if last == 4:
            start_pair(3, act, act_pair, 512, range(2))
        if last == 8:
            start_pair(3, act, act_pair, 512, range(2, 4))
            store(slope, slope_out, io.at[8])

    def down(u):
        _, lo, n, _ = UNITS[u]
        for g in range(8):
            at = pl.ds(g * 512 + lo, n)
            store(wd.at[at], wd_out.at[at], wd_sem.at[g, u])
        for j in range(0, 8, 1024 // n):
            cols = [slice(512 * g + lo, 512 * g + lo + n) for g in range(j, j + 1024 // n)]
            left = jnp.concatenate([act[:, c] for c in cols], axis=1)
            right = jnp.concatenate([wd[c, :] for c in cols], axis=0)
            acc[...] += dot_nn(left, right)

    tidied = []

    def tidy(_):
        for k, g in enumerate(others):
            small_copy(k, p.f, p.dev(f=g)).wait_send()
        for part in parts:
            if UNITS[part.unit][0] != "d":
                part.sent()
        count = len(stores) - 8
        for c in stores[:count]:
            c.wait()
        for args in pairs[:12]:
            for c in pair(*args):
                c.wait()
        tidied.append(count)

    def second_norm(_):
        loads[1].wait()
        hidden = acc[...]
        center = hidden - row_mean(hidden)
        inverse = lax.rsqrt(row_mean(center * center) + 1e-05)
        second = center * inverse
        row_at = lax.broadcasted_iota(jnp.int32, (seq, 1), 0)
        live = jnp.concatenate([(row_at < lengths[s]).astype(F32) for s in range(slots)], axis=0)
        e = cot_v[...] * live
        scaled = e * params[7:8]
        gh2[...] = inverse * (scaled - row_mean(scaled) - second * row_mean(scaled * second))
        gb[...] = gh2[...].astype(BF16)
        swap = (
            pltpu.make_async_copy(gb, branch_pair.at[mine], pair_local.at[4, 0]),
            remote(gb, branch_pair.at[mine], pair_send.at[4, 0], pair_recv.at[4, 0], p.dev(f=p.fs)),
        )
        for c in swap:
            c.start()
        store(gh2, grad_out_ref, io.at[11])
        store(params, params_out, io.at[12])
        out_v[...] = (second * params[7:8] + params[5:6]).astype(BF16)
        store(out_v, layer_out, io.at[10])
        sums[...] = jnp.zeros_like(sums)
        sums[0:1] = jnp.sum(e * second, axis=0, keepdims=True)
        sums[1:2] = jnp.sum(e, axis=0, keepdims=True)
        sums[2:3] = jnp.sum(gb[...].astype(F32), axis=0, keepdims=True)
        store(sums, sums_out, io.at[13])
        for part in parts:
            if UNITS[part.unit][0] == "d":
                part.sent()
        for args in pairs[12:]:
            for c in pair(*args):
                c.wait()
        for c in stores[tidied[0] :]:
            c.wait()
        for c in swap:
            c.wait()

    work = {
        "small": small_params, "qkv": project, "at": attention, "out": first_norm, "up": up, "dn": down,
        "tidy": tidy, "last": second_norm,
        "direct": lambda u: parts[u].direct(), "done": lambda u: parts[u].done(),
        "fx": lambda u: parts[u].pass_on(0, 4, 2, 7), "fy": lambda u: parts[u].pass_on(1, 5, 3, 8),
        "r2": lambda u: parts[u].pass_on(2, 9), "r3": lambda u: parts[u].pass_on(3, 10),
        "r4": lambda u: parts[u].pass_on(4, 11), "r5": lambda u: parts[u].pass_on(5, 12),
    }
    for name, *which in FORWARD_PLAN:
        work[name](*which)


def forward_call(tokens, lengths, cotangent, qkv_w, out_w, up_w, down_w, small):
    rows, width = tokens.shape
    ff = up_w.shape[1]
    anyspace = pl.BlockSpec(memory_space=pl.ANY)
    shape = jax.ShapeDtypeStruct
    outs = [
        shape((rows, width), BF16),
        shape((width, 3 * width), BF16),
        shape((width, width), BF16),
        shape((width, ff), BF16),
        shape((ff, width), BF16),
        shape((rows, 3 * width), BF16),
        shape((rows, ff), BF16),
        shape((2 * rows, ff // 2), BF16),
        shape((2 * rows, width // 2), BF16),
        shape((2 * rows, width // 2), BF16),
        shape((2 * rows, width // 2), BF16),
        shape((2 * rows, width), BF16),
        shape((rows, width), F32),
        shape((rows, 128), F32),
        shape((rows, width), F32),
        shape((16, width), F32),
        shape((8, width), F32),
    ]
    dma = pltpu.SemaphoreType.DMA
    scratch = [
        pltpu.VMEM((rows, width), BF16),
        pltpu.VMEM((width, 3 * width), BF16),
        pltpu.VMEM((width, width), BF16),
        pltpu.VMEM((width, ff), BF16),
        pltpu.VMEM((ff, width), BF16),
        pltpu.VMEM((rows, 3 * width), BF16),
        pltpu.VMEM((rows, width), BF16),
        pltpu.VMEM((rows, width), F32),
        pltpu.VMEM((rows, width), BF16),
        pltpu.VMEM((rows, ff), BF16),
        pltpu.VMEM((rows, ff), BF16),
        pltpu.VMEM((rows, width), F32),
        pltpu.VMEM((rows, width), F32),
        pltpu.VMEM((rows, width), F32),
        pltpu.VMEM((rows, width), BF16),
        pltpu.VMEM((rows, width), BF16),
        pltpu.VMEM((8, 16, 128), BF16),
        pltpu.VMEM((16, width), F32),
        pltpu.VMEM((rows, 128), F32),
        pltpu.VMEM((8, width), F32),
        pltpu.VMEM((8, ff // 8), F32),
        dma((len(UNITS), KINDS)),
        dma((len(UNITS), KINDS)),
        dma((len(UNITS),)),
        dma((7,)),
        dma((7,)),
        dma,
        dma((14,)),
        dma((5, 4)),
        dma((5, 4)),
        dma((5, 4)),
        dma((8, len(UNITS))),
    ]
    return pl.pallas_call(
        forward_kernel,
        out_shape=outs,
        in_specs=[pl.BlockSpec(memory_space=pltpu.SMEM)] + [anyspace] * 7,
        out_specs=[anyspace] * len(outs),
        scratch_shapes=scratch,
        name="forward",
        cost_estimate=pl.CostEstimate(flops=2 * 512 * 12582912, bytes_accessed=60 * MIB, transcendentals=4 * MIB),
        compiler_params=pltpu.CompilerParams(
            collective_id=0, has_side_effects=True, vmem_limit_bytes=60 * MIB
        ),
    )(lengths, tokens, cotangent, small, qkv_w, out_w, up_w, down_w)


def pack_small(biases, up_bias, gains):
    return jnp.concatenate([biases, gains, up_bias.reshape(4, 128), jnp.zeros((4, 128), BF16)], axis=0)


BLOCKS = 12
SHARED = (2, 3)
PIECES = (
    (0, 0, 64),
    (1, 0, 64),
    (2, None, 32),
    (4, 0, 64),
    (3, None, 32),
    (5, 0, 64),
    (6, 0, 64),
    (7, 0, 64),
    (8, 0, 64),
    (9, 0, 32),
    (9, 32, 32),
    (10, 0, 32),
    (10, 32, 32),
    (11, 0, 16),
    (11, 16, 16),
    (11, 32, 16),
    (11, 48, 16),
)
PLAN = (
    ("start", 0), ("down", 0), ("begin", 0), ("down", 1), ("begin", 1), ("down", 2), ("down", 3), ("g", 0),
    ("h", 0), ("second", 0), ("g", 1), ("h", 1), ("u", 0), ("second", 1), ("begin", 3), ("g", 2),
    ("along", 0), ("h", 2), ("u", 1), ("along", 1), ("begin", 2), ("g", 3), ("begin", 5), ("h", 3), ("u", 2),
    ("second", 3), ("norm", 0), ("second", 2), ("u", 3), ("inward", 0), ("begin", 4), ("gm", 0),
    ("second", 5), ("o", 0), ("at", 0, 1), ("hand", 0), ("inward", 1), ("along", 3), ("at", 1, 2),
    ("along", 2), ("begin", 6), ("at", 2, 4), ("second", 4), ("at", 4, 5), ("pass", 0), ("inward", 3),
    ("at", 5, 6), ("along", 5), ("at", 6, 7), ("hand", 1), ("begin", 7), ("inward", 2), ("at", 7, 8),
    ("at", 8, 9), ("hand", 3), ("at", 9, 10), ("inward", 5), ("pass", 1), ("second", 6), ("at", 10, 11),
    ("along", 4), ("at", 11, 12), ("hand", 2), ("at", 12, 13), ("inward", 4), ("begin", 8), ("at", 13, 14),
    ("pass", 3), ("at", 14, 15), ("second", 7), ("at", 15, 16), ("hand", 5), ("q", 0), ("along", 6), ("q", 1),
    ("close", 0), ("pass", 2), ("begin", 9), ("q", 2), ("hand", 4), ("inward", 6), ("small", 0),
    ("second", 8), ("pass", 5), ("t", 0), ("t", 1), ("pass", 4), ("along", 7), ("begin", 10), ("close", 1),
    ("t", 2), ("second", 9), ("hand", 6), ("level", 1), ("inward", 7), ("begin", 11), ("along", 8),
    ("begin", 12), ("second", 10), ("along", 9), ("close", 3), ("begin", 13), ("pass", 6), ("inward", 8),
    ("begin", 14), ("hand", 7), ("inward", 9), ("hand", 8), ("second", 11), ("close", 2), ("begin", 15),
    ("pass", 7), ("hand", 9), ("second", 12), ("along", 10), ("inward", 10), ("begin", 16), ("close", 5),
    ("second", 13), ("second", 14), ("along", 11), ("close", 4), ("second", 15), ("pass", 8), ("inward", 11),
    ("pass", 9), ("along", 12), ("second", 16), ("hand", 10), ("along", 13), ("inward", 12), ("along", 14),
    ("hand", 11), ("along", 15), ("along", 16), ("inward", 13), ("close", 6), ("pass", 10), ("inward", 14),
    ("hand", 12), ("inward", 15), ("pass", 11), ("inward", 16), ("hand", 13), ("hand", 14), ("close", 7),
    ("pass", 12), ("hand", 15), ("level", 2), ("hand", 16), ("pass", 13), ("pass", 14), ("pass", 15),
    ("pass", 16), ("close", 8), ("close", 9), ("close", 10), ("close", 11), ("close", 12), ("close", 13),
    ("close", 14), ("close", 15), ("close", 16),
)
S1X, S1Y, S2X, S2Y, Z1G, Z1K, Z2, FM, FE, FF = range(10)


class Reduce:
    def __init__(self, place, prod, got_x, got_y, end_x, end_y, from_end, from_mid, swapped, out_at, send, recv, local, swap_send, swap_recv):
        self.p = place
        self.prod, self.got_x, self.got_y, self.end_x, self.end_y = prod, got_x, got_y, end_x, end_y
        self.from_end, self.from_mid, self.swapped, self.out_at = from_end, from_mid, swapped, out_at
        self.send, self.recv, self.local = send, recv, local
        self.swap_send, self.swap_recv = swap_send, swap_recv
        z = place.z
        self.mid = 1 + lax.div(z, 2)
        self.end = 3 * lax.div(z, 2)
        self.is_mid = z == self.mid
        self.is_end = z == self.end

    def rows(self, u, theirs=False):
        b, o, n = PIECES[u]
        if o is None:
            o = pl.multiple_of(32 * (1 - self.p.par if theirs else self.p.par), 32)
        return b, o, n

    def z_rows(self, u):
        b, o, n = PIECES[u]
        return (b, 0, 64) if o is None else (b, o, n)

    def keep(self, o, n):
        return pl.ds(pl.multiple_of(64 * (self.mid - 1) + o, 16), n)

    def give(self, o, n):
        return pl.ds(pl.multiple_of(64 * (2 - self.mid) + o, 16), n)

    def copy(self, kind, u, sending=True):
        p = self.p
        b, o, n = self.rows(u, theirs=kind in (Z1G, Z1K) and not sending)
        _, oz, nz = self.z_rows(u)
        x, y, xn, yn = p.x, p.y, 1 - p.x, 1 - p.y
        near, far = pl.ds(o, n), pl.ds(64 + o, n)
        keep, give = self.keep(oz, nz), self.give(oz, nz)
        to_mid, to_end, to_other = p.dev(z=self.mid), p.dev(z=self.end), p.dev(z=3 - self.mid)
        own = self.prod.at[b, y, x]
        if kind == S1X:
            src, dst, dev = self.prod.at[b, :, xn, near], self.got_x.at[b, :, near], p.dev(f=p.fx)
        elif kind == S1Y:
            src, dst, dev = self.prod.at[b, yn, :, far], self.got_y.at[b, :, near], p.dev(f=p.fy)
        elif kind == S2Y:
            src, dst, dev = self.prod.at[b, yn, x, near], self.end_y.at[b, near], p.dev(f=p.fy)
        elif kind == S2X:
            src, dst, dev = self.prod.at[b, y, xn, far], self.end_x.at[b, near], p.dev(f=p.fx)
        elif kind == Z1G:
            src, dst, dev = own.at[self.give(o, n)], self.from_end.at[b, self.give(o, n)], to_mid
        elif kind == Z1K:
            src, dst, dev = own.at[self.keep(o, n)], self.from_end.at[b, self.keep(o, n)], to_mid
        elif kind == Z2:
            src, dst, dev = own.at[give], self.from_mid.at[b, pl.ds(oz, nz)], to_other
        elif kind == FM:
            src, dst, dev = own.at[keep], self.out_at(b, keep if sending else give), to_other
        elif kind == FE:
            src, dst, dev = own.at[keep], self.out_at(b, keep), to_end
        else:
            src, dst, dev = self.out_at(b, give), self.out_at(b, give), to_end
        return remote(src, dst, self.send.at[kind, u], self.recv.at[kind, u], dev)

    def swap(self, b, half):
        i = SHARED.index(b)
        src = self.prod.at[b, :, :, pl.ds(pl.multiple_of(64 * half + 32 * (1 - self.p.par), 32), 32)]
        dst = self.swapped.at[i, :, :, pl.ds(32 * half, 32)]
        return remote(src, dst, self.swap_send.at[i, half], self.swap_recv.at[i, half], self.p.dev(z=self.p.zn))

    def produced(self, b):
        if b in SHARED:
            self.swap(b, 0).start()
            self.swap(b, 1).start()

    def begin(self, u):
        b, o, n = self.rows(u)
        for half, kind in enumerate((S1X, S1Y)):
            if b in SHARED:
                at = pl.ds(pl.multiple_of(64 * half + o, 32), n)
                self.swap(b, half).wait()
                part = self.swapped[SHARED.index(b), :, :, 32 * half : 32 * half + 32]
                self.prod[b, :, :, at] = self.prod[b, :, :, at] + part
            self.copy(kind, u).start()

    def second(self, u):
        x, y = self.p.x, self.p.y
        b, o, n = self.rows(u)
        near, far = pl.ds(o, n), pl.ds(64 + o, n)
        self.copy(S1X, u).wait_recv()
        self.prod[b, :, x, near] = self.prod[b, :, x, near] + self.got_x[b, :, near]
        self.copy(S2Y, u).start()
        self.copy(S1Y, u).wait_recv()
        self.prod[b, y, :, far] = self.prod[b, y, :, far] + self.got_y[b, :, near]
        self.copy(S2X, u).start()

    def along(self, u):
        x, y = self.p.x, self.p.y
        b, o, n = self.rows(u)
        near, far = pl.ds(o, n), pl.ds(64 + o, n)
        self.copy(S2Y, u).wait_recv()
        self.prod[b, y, x, near] = self.prod[b, y, x, near] + self.end_y[b, near]
        self.copy(S2X, u).wait_recv()
        self.prod[b, y, x, far] = self.prod[b, y, x, far] + self.end_x[b, near]

        @pl.when(self.is_end)
        def _():
            self.copy(Z1G, u).start()
            self.copy(Z1K, u).start()

    def inward(self, u):
        x, y = self.p.x, self.p.y
        b, o, n = self.rows(u, theirs=True)

        @pl.when(self.is_mid)
        def _():
            give = self.give(o, n)
            self.copy(Z1G, u, False).wait_recv()
            if b in SHARED:
                self.prod[b, y, x, give] = self.from_end[b, give]
            else:
                self.prod[b, y, x, give] = self.prod[b, y, x, give] + self.from_end[b, give]
            self.copy(Z2, u).start()

    def write(self, u):
        b, o, n = self.z_rows(u)
        keep = self.keep(o, n)
        return pltpu.make_async_copy(
            self.prod.at[b, self.p.y, self.p.x, keep], self.out_at(b, keep), self.local.at[u]
        )

    def hand_out(self, u):
        x, y = self.p.x, self.p.y
        b, o, n = self.z_rows(u)

        @pl.when(self.is_mid)
        def _():
            keep = self.keep(o, n)
            self.copy(Z1K, u, False).wait_recv()
            if b in SHARED:
                part = self.keep(*self.rows(u, theirs=True)[1:])
                self.prod[b, y, x, part] = self.from_end[b, part]
            self.copy(Z2, u).wait_recv()
            total = self.prod[b, y, x, keep].astype(F32) + self.from_mid[b, o : o + n].astype(F32)
            if b not in SHARED:
                total = total + self.from_end[b, keep].astype(F32)
            self.prod[b, y, x, keep] = total.astype(BF16)
            self.copy(FM, u).start()
            self.copy(FE, u).start()
            self.write(u).start()

    def hand_on(self, u):
        @pl.when(self.is_mid)
        def _():
            self.copy(FM, u, False).wait_recv()
            self.copy(FF, u).start()

    def close(self, u):
        for kind in (S1X, S1Y, S2X, S2Y):
            self.copy(kind, u).wait_send()

        @pl.when(self.is_end)
        def _():
            self.copy(Z1G, u).wait_send()
            self.copy(Z1K, u).wait_send()
            self.copy(FE, u).wait_recv()
            self.copy(FF, u, False).wait_recv()

        @pl.when(self.is_mid)
        def _():
            for kind in (Z2, FM, FE, FF):
                self.copy(kind, u).wait_send()
            self.write(u).wait()


def backward_kernel(
    lengths, wq, wo, wu, wd, qkv, slope, act_pair, first_pair, mixed_pair, tok_pair, branch_pair,
    norm_in, inv_in, gh2, params_in, sums_in,
    token_grad, out_q, out_o, out_u, out_d, small_out,
    lhs, wbuf, slope_v, branch, gi, gq, gm, gh, norm, inv, params, sums_v, upsum,
    prod, got_x, got_y, end_x, end_y, from_end, from_mid, swapped,
    s_send, s_got, s_total, s_all, s_out,
    rs_send, rs_recv, rs_local, pair_send, pair_recv, load_sem, lhs_sem, w_sem, slope_sem,
    sm_send, sm_recv, smz_send, smz_recv, store_sem, swap_send, swap_recv,
):
    p = Place()
    rows, width = gh.shape
    slots = lengths.shape[0]
    seq = rows // slots
    planes = [lax.rem(p.f + k, 8) for k in range(1, 8)]
    levels = [lax.rem(p.z + k, 4) for k in range(1, 4)]
    barrier = pltpu.get_barrier_semaphore()
    for g in planes:
        pl.semaphore_signal(barrier, inc=1, device_id=p.dev(f=g), device_id_type=MESH)
    for g in levels:
        pl.semaphore_signal(barrier, inc=1, device_id=p.dev(z=g), device_id_type=MESH)

    mine = pl.ds(pl.multiple_of(p.core * rows, rows), rows)

    def lhs_copies(i):
        if i < 4:
            return [
                pltpu.make_async_copy(
                    act_pair.at[:, pl.ds(chip * 512 + i * 128, 128)],
                    lhs.at[i % 2, :, pl.ds(chip * 128, 128)],
                    lhs_sem.at[i, chip],
                )
                for chip in range(4)
            ]
        src = (first_pair, mixed_pair, tok_pair)[i - 4]
        return [pltpu.make_async_copy(src, lhs.at[i % 2], lhs_sem.at[i, 0])]

    def w_copy(i):
        if i < 8:
            j = i // 2
            src = wu.at[:, pl.ds(j * 1024, 1024)] if i % 2 else wd.at[pl.ds(j * 1024, 1024)]
        elif i == 8:
            src = wo
        else:
            src = wq.at[:, pl.ds((i - 9) * 1024, 1024)]
        return pltpu.make_async_copy(src, wbuf.at[i % 2], w_sem.at[i])

    def slope_copy(j):
        return pltpu.make_async_copy(slope.at[:, pl.ds(j * 1024, 1024)], slope_v.at[j % 2], slope_sem.at[j])

    loads = [
        pltpu.make_async_copy(src, dst, load_sem.at[i])
        for i, (src, dst) in enumerate(
            (
                (branch_pair, branch), (gh2, gh), (qkv, gq.at[mine]), (norm_in, norm), (inv_in, inv),
                (params_in, params), (sums_in, sums_v),
            )
        )
    ]
    for c in lhs_copies(0):
        c.start()
    loads[0].start()
    for c in lhs_copies(1):
        c.start()
    w_copy(0).start()
    slope_copy(0).start()
    for c in loads[1:]:
        c.start()

    def out_at(b, at):
        if b < 4:
            return out_d.at[pl.ds(128 * b, 128)].at[at]
        if b < 8:
            return out_u.at[at, pl.ds((b - 4) * 1024, 1024)]
        if b == 8:
            return out_o.at[at]
        return out_q.at[at, pl.ds((b - 9) * 1024, 1024)]

    red = Reduce(
        p, prod, got_x, got_y, end_x, end_y, from_end, from_mid, swapped, out_at, rs_send, rs_recv, rs_local,
        swap_send, swap_recv,
    )

    def produce(b, left, right):
        prod[b] = dot_tn(left, right).astype(BF16).reshape(2, 2, 128, 1024)
        red.produced(b)

    def to_pair(index, ref, cols):
        here = ref.at[mine, cols]
        return remote(here, here, pair_send.at[index], pair_recv.at[index], p.dev(f=p.fs))

    def block_cols(j):
        return pl.ds(j * 1024, 1024)

    whole = pl.ds(0, 1024)
    ga = branch

    def start(_):
        pl.semaphore_wait(barrier, 10)
        loads[0].wait()

    def down(b):
        for c in lhs_copies(b):
            c.wait()
        produce(b, lhs[b % 2], branch[...])
        for c in lhs_copies(b + 2):
            c.start()
        if b == 3:
            loads[1].wait()

    def inner_step(j):
        w_copy(2 * j).wait()
        w_copy(2 * j + 1).start()
        slope_copy(j).wait()
        if j < 3:
            slope_copy(j + 1).start()
        inner = (dot_nt(branch[mine], wbuf[0]) * slope_v[j % 2].astype(F32)).astype(BF16)
        gi[mine, j * 1024 : (j + 1) * 1024] = inner
        to_pair(j, gi, block_cols(j)).start()
        upsum[j : j + 1] = jnp.sum(inner.astype(F32), axis=0, keepdims=True)

    def hidden_step(j):
        w_copy(2 * j + 1).wait()
        w_copy(2 * j + 2).start()
        gh[...] += dot_nt(gi[mine, j * 1024 : (j + 1) * 1024], wbuf[1])
        if j == 0:
            for c in lhs_copies(4):
                c.wait()

    def up_block(j):
        to_pair(j, gi, block_cols(j)).wait_recv()
        produce(4 + j, lhs[0], gi[:, j * 1024 : (j + 1) * 1024])
        if j == 3:
            for c in lhs_copies(6):
                c.start()

    def first_norm(_):
        for c in loads[2:]:
            c.wait()
        e = gh[...]
        scaled = e * params[6:7]
        n = norm[...]
        sums_v[3:4] = jnp.sum(e, axis=0, keepdims=True)
        sums_v[4:5] = jnp.sum(e * n, axis=0, keepdims=True)
        gh[...] = inv[:, 0:1] * (scaled - row_mean(scaled) - n * row_mean(scaled * n))
        ga[mine] = gh[...].astype(BF16)
        to_pair(4, ga, whole).start()
        sums_v[5:6] = jnp.sum(ga[mine].astype(F32), axis=0, keepdims=True)

    def grad_mixed(_):
        w_copy(8).wait()
        w_copy(9).start()
        gm[...] = dot_nt(ga[mine], wbuf[0]).astype(BF16)
        w_copy(10).start()

    def out_block(_):
        for c in lhs_copies(5):
            c.wait()
        to_pair(4, ga, whole).wait_recv()
        produce(8, lhs[1], ga[...])

    left = lax.broadcasted_iota(jnp.int32, (seq, 128), 1) < HEAD_SIZE
    key_row = lax.broadcasted_iota(jnp.int32, (seq, seq), 0)
    scale = 1.0 / math.sqrt(HEAD_SIZE)

    def attend(step, carry):
        slot, pair_of = lax.rem(step, slots), lax.div(step, slots)
        at_rows = pl.ds(pl.multiple_of(slot * seq, seq), seq)
        own_rows = pl.ds(pl.multiple_of(p.core * rows + slot * seq, seq), seq)
        col = pl.multiple_of(pair_of * 128, 128)
        at_q = pl.ds(col, 128)
        at_k = pl.ds(pl.multiple_of(width + col, 128), 128)
        at_v = pl.ds(pl.multiple_of(2 * width + col, 128), 128)
        q, k, v = gq[own_rows, at_q], gq[own_rows, at_k], gq[own_rows, at_v]
        do = gm[at_rows, at_q]
        dead = key_row >= lengths[slot]
        parts = []
        for head in range(2):
            lanes = left if head == 0 else ~left
            k_head = jnp.where(lanes, k, jnp.zeros_like(k))
            v_head = jnp.where(lanes, v, jnp.zeros_like(v))
            scores = jnp.where(dead, -1e30, dot_nt(k_head, q) * scale)
            exps = jnp.exp(scores - jnp.max(scores, axis=0, keepdims=True))
            probs = exps * (1.0 / jnp.sum(exps, axis=0, keepdims=True))
            d_probs = dot_nt(v_head, do)
            shared = jnp.sum(probs * d_probs, axis=0, keepdims=True)
            d_scores = (probs * (d_probs - shared)).astype(BF16)
            parts.append(
                (dot_tn(d_scores, k) * scale, dot_nn(d_scores, q) * scale, dot_nn(probs.astype(BF16), do))
            )
        for at, one, two in zip((at_q, at_k, at_v), *parts):
            gq[own_rows, at] = jnp.where(left, one, two).astype(BF16)
        return carry

    steps = 8 * slots

    def attention(first, last):
        lax.fori_loop(first * steps // 16, last * steps // 16, attend, 0)
        if last % 8 == 0:
            half = last // 8 - 1
            for j in range(3):
                to_pair(5 + 3 * half + j, gq, pl.ds(j * 1024 + 512 * half, 512)).start()

    def qkv_block(j):
        if j == 0:
            for c in lhs_copies(6):
                c.wait()
        for half in range(2):
            to_pair(5 + 3 * half + j, gq, pl.ds(j * 1024 + 512 * half, 512)).wait_recv()
        produce(9 + j, lhs[0], gq[:, j * 1024 : (j + 1) * 1024])

    order = (6, 7, 5, 3, 2, 1, 4, 0)

    def small_to(k):
        g = planes[k]
        return remote(s_send.at[g], s_got.at[p.f], sm_send.at[k], sm_recv.at[k], p.dev(f=g))

    def small_from(k):
        g = lax.rem(p.f + 7 - k, 8)
        return remote(s_send.at[g], s_got.at[g], sm_send.at[k], sm_recv.at[k], p.dev(f=g))

    def level_to(k):
        return remote(s_total, s_all.at[p.z], smz_send.at[k], smz_recv.at[k], p.dev(z=levels[k]))

    def level_from(k):
        g = lax.rem(p.z + 3 - k, 4)
        return remote(s_total, s_all.at[g], smz_send.at[k], smz_recv.at[k], p.dev(z=g))

    stores = (
        pltpu.make_async_copy(gh, token_grad, store_sem.at[0]),
        pltpu.make_async_copy(s_out, small_out, store_sem.at[1]),
    )

    def small(_):
        sums_v[6:7] = jnp.sum(gq[mine, 0:1024].astype(F32), axis=0, keepdims=True)
        sums_v[7:8] = jnp.sum(gq[mine, 2048:3072].astype(F32), axis=0, keepdims=True)
        for g in range(8):
            cols = slice(g * 128, (g + 1) * 128)
            for i, row in enumerate(order):
                s_send[g, i : i + 1] = sums_v[row : row + 1, cols]
            for i in range(4):
                lo = (g % 2) * 512 + i * 128
                s_send[g, 8 + i : 9 + i] = upsum[g // 2 : g // 2 + 1, lo : lo + 128]
        for k in range(7):
            small_to(k).start()
        s_got[p.f] = s_send[p.f]

    def token_step(j):
        w_copy(9 + j).wait()
        gh[...] += dot_nt(gq[mine, j * 1024 : (j + 1) * 1024], wbuf[(9 + j) % 2])
        if j == 0:
            w_copy(11).start()
        if j == 2:
            stores[0].start()

    def level(which):
        if which == 1:
            for k in range(7):
                small_from(k).wait_recv()
            total = s_got[0]
            for g in range(1, 8):
                total = total + s_got[g]
            s_total[...] = total
            for k in range(3):
                level_to(k).start()
            s_all[p.z] = total
            for j in range(4):
                to_pair(j, gi, block_cols(j)).wait_send()
            to_pair(4, ga, whole).wait_send()
            for j in range(3):
                for half in range(2):
                    to_pair(5 + 3 * half + j, gq, pl.ds(j * 1024 + 512 * half, 512)).wait_send()
            return
        for k in range(3):
            level_from(k).wait_recv()
        s_out[...] = (s_all[0] + s_all[1]) + (s_all[2] + s_all[3])
        stores[1].start()
        for k in range(7):
            small_to(k).wait_send()
        for k in range(3):
            level_to(k).wait_send()
        stores[0].wait()
        stores[1].wait()

    work = {
        "start": start, "down": down, "g": inner_step, "h": hidden_step, "u": up_block, "norm": first_norm,
        "gm": grad_mixed, "o": out_block, "at": attention, "q": qkv_block, "small": small, "t": token_step,
        "level": level, "begin": red.begin, "second": red.second, "along": red.along, "inward": red.inward,
        "hand": red.hand_out, "pass": red.hand_on, "close": red.close,
    }
    for name, *which in PLAN:
        work[name](*which)


def backward_call(lengths, saved):
    wq, wo, wu, wd, qkv, slope = saved[:6]
    rows, width = qkv.shape[0], wo.shape[0]
    ff = wu.shape[1]
    anyspace = pl.BlockSpec(memory_space=pl.ANY)
    shape = jax.ShapeDtypeStruct
    dma = pltpu.SemaphoreType.DMA
    outs = [
        shape((rows, width), F32),
        shape((width // 8, 3 * width), BF16),
        shape((width // 8, width), BF16),
        shape((width // 8, ff), BF16),
        shape((ff // 8, width), BF16),
        shape((16, 128), F32),
    ]
    scratch = [
        pltpu.VMEM((2, 2 * rows, 512), BF16),
        pltpu.VMEM((2, 1024, 1024), BF16),
        pltpu.VMEM((2, rows, 1024), BF16),
        pltpu.VMEM((2 * rows, width), BF16),
        pltpu.VMEM((2 * rows, ff), BF16),
        pltpu.VMEM((2 * rows, 3 * width), BF16),
        pltpu.VMEM((rows, width), BF16),
        pltpu.VMEM((rows, width), F32),
        pltpu.VMEM((rows, width), F32),
        pltpu.VMEM((rows, 128), F32),
        pltpu.VMEM((16, width), F32),
        pltpu.VMEM((8, width), F32),
        pltpu.VMEM((4, width), F32),
        pltpu.VMEM((BLOCKS, 2, 2, 128, 1024), BF16),
        pltpu.VMEM((BLOCKS, 2, 64, 1024), BF16),
        pltpu.VMEM((BLOCKS, 2, 64, 1024), BF16),
        pltpu.VMEM((BLOCKS, 64, 1024), BF16),
        pltpu.VMEM((BLOCKS, 64, 1024), BF16),
        pltpu.VMEM((BLOCKS, 128, 1024), BF16),
        pltpu.VMEM((BLOCKS, 64, 1024), BF16),
        pltpu.VMEM((len(SHARED), 2, 2, 64, 1024), BF16),
        pltpu.VMEM((8, 16, 128), F32),
        pltpu.VMEM((8, 16, 128), F32),
        pltpu.VMEM((16, 128), F32),
        pltpu.VMEM((4, 16, 128), F32),
        pltpu.VMEM((16, 128), F32),
        dma((10, len(PIECES))),
        dma((10, len(PIECES))),
        dma((len(PIECES),)),
        dma((11,)),
        dma((11,)),
        dma((7,)),
        dma((7, 4)),
        dma((12,)),
        dma((4,)),
        dma((7,)),
        dma((7,)),
        dma((3,)),
        dma((3,)),
        dma((2,)),
        dma((len(SHARED), 2)),
        dma((len(SHARED), 2)),
    ]
    return pl.pallas_call(
        backward_kernel,
        out_shape=outs,
        in_specs=[pl.BlockSpec(memory_space=pltpu.SMEM)] + [anyspace] * len(saved),
        out_specs=[anyspace] * len(outs),
        scratch_shapes=scratch,
        name="backward",
        cost_estimate=pl.CostEstimate(flops=4 * 512 * 12582912, bytes_accessed=60 * MIB, transcendentals=4 * MIB),
        compiler_params=pltpu.CompilerParams(
            collective_id=1, has_side_effects=True, vmem_limit_bytes=60 * MIB
        ),
    )(lengths, *saved)


def finish_kernel(
    layer_in, token_in, q_in, o_in, u_in, d_in, small,
    layer_out, token_out, q_out, o_out, u_out, d_out, biases_out, up_bias_out, gains_out,
    q_low, o_low, u_low, d_low, layer_v, token_v, small_v, q, o, u, d, sem,
):
    sources = (d_in, u_in, q_in, o_in, token_in, layer_in, small)
    lows, wides = (d_low, u_low, q_low, o_low, token_v, layer_v, small_v), (d, u, q, o, token_v, layer_v)
    results = (d_out, u_out, q_out, o_out, token_out, layer_out)
    ins = [pltpu.make_async_copy(a, b, sem.at[i]) for i, (a, b) in enumerate(zip(sources, lows))]
    outs = [pltpu.make_async_copy(a, b, sem.at[7 + i]) for i, (a, b) in enumerate(zip(wides, results))]
    for c in ins:
        c.start()
    for a, b, c_in, c_out in zip(lows, wides, ins, outs):
        c_in.wait()
        if a is not b:
            b[...] = a[...].astype(F32)
        c_out.start()
    ins[-1].wait()
    biases_out[...] = small_v[0:6]
    gains_out[...] = small_v[6:8]
    for i in range(4):
        up_bias_out[i * 128 : (i + 1) * 128] = small_v[8 + i]
    for c in outs:
        c.wait()


def finish_call(layer_out, token_grad, weight_grads, small):
    anyspace = pl.BlockSpec(memory_space=pl.ANY)
    vmem = pl.BlockSpec(memory_space=pltpu.VMEM)
    shape = jax.ShapeDtypeStruct
    wide = [shape(g.shape, F32) for g in weight_grads]
    outs = [
        shape(layer_out.shape, BF16), shape(token_grad.shape, F32), *wide,
        shape((6, 128), F32), shape((512,), F32), shape((2, 128), F32),
    ]
    return pl.pallas_call(
        finish_kernel,
        out_shape=outs,
        in_specs=[anyspace] * 7,
        out_specs=[anyspace] * 6 + [vmem] * 3,
        scratch_shapes=[pltpu.VMEM(g.shape, BF16) for g in weight_grads]
        + [pltpu.VMEM(g.shape, g.dtype) for g in (layer_out, token_grad, small)]
        + [pltpu.VMEM(g.shape, F32) for g in weight_grads]
        + [pltpu.SemaphoreType.DMA((13,))],
        name="finish",
        compiler_params=pltpu.CompilerParams(vmem_limit_bytes=60 * MIB),
    )(layer_out, token_grad, *weight_grads, small)


def plane(
    tokens,
    lengths,
    cotangent,
    qkv_weight,
    out_weight,
    up_weight,
    down_weight,
    biases,
    up_bias,
    gains,
):
    small_in = pack_small(biases, up_bias, gains)
    layer_out, *saved = forward_call(
        tokens, lengths, cotangent, qkv_weight, out_weight, up_weight, down_weight, small_in
    )
    token_grad, *weight_grads, small = backward_call(lengths, saved)
    return tuple(finish_call(layer_out, token_grad, weight_grads, small))


def solution(mesh):
    step = plane if dict(mesh.shape) == {"fsdp": 8, "rep": 4} else portable
    both = ("fsdp", "rep")
    in_specs = (
        P(both, None),
        P(both),
        P(both, None),
        P("fsdp", None),
        P("fsdp", None),
        P("fsdp", None),
        P("fsdp", None),
        P(None, "fsdp"),
        P("fsdp"),
        P(None, "fsdp"),
    )
    out_specs = (
        P(both, None),
        P(both, None),
        P("fsdp", None),
        P("fsdp", None),
        P("fsdp", None),
        P("fsdp", None),
        P(None, "fsdp"),
        P("fsdp"),
        P(None, "fsdp"),
    )
    return jax.shard_map(
        step, mesh=mesh, in_specs=in_specs, out_specs=out_specs, check_vma=False
    )
```

```python
import math

import jax
import jax.numpy as jnp
from jax import lax
from jax.experimental import pallas as pl
from jax.experimental.pallas import tpu as pltpu
from jax.sharding import PartitionSpec as P

HEAD_SIZE = 64


def matmul(left_side, right_side):
    return jnp.dot(left_side, right_side, preferred_element_type=jnp.float32)


def transposed_left(left_side, right_side):
    return lax.dot_general(
        left_side, right_side, (((0,), (0,)), ((), ())), preferred_element_type=jnp.float32
    )


def transposed_right(left_side, right_side):
    return lax.dot_general(
        left_side, right_side, (((1,), (1,)), ((), ())), preferred_element_type=jnp.float32
    )


def column_sum(values):
    return jnp.sum(values.astype(jnp.float32), axis=0)


def row_mean(values):
    return jnp.mean(values, axis=-1, keepdims=True)


def normalize(hidden):
    center = hidden - row_mean(hidden)
    inverse = lax.rsqrt(row_mean(center * center) + 1e-05)
    return center * inverse, inverse


def norm_back(grad, norm, inverse, gain):
    scaled = grad * gain
    return inverse * (scaled - row_mean(scaled) - norm * row_mean(scaled * norm))


def low(values):
    return values.astype(jnp.bfloat16)


def gather_small(biases, up_bias, gains):
    width, up_width = biases.shape[1], up_bias.shape[0]
    packed = jnp.concatenate([biases.reshape(-1), gains.reshape(-1), up_bias])
    everyone = lax.all_gather(packed, "fsdp", axis=0, tiled=False).astype(jnp.float32)
    rows = everyone[:, : 8 * width].reshape(-1, 8, width).transpose(1, 0, 2).reshape(8, -1)
    return rows[:6], everyone[:, 8 * width : 8 * width + up_width].reshape(-1), rows[6:]


def reduce_weight(grad):
    shard = lax.psum_scatter(low(grad), "fsdp", scatter_dimension=0, tiled=True)
    return lax.psum(shard, "rep").astype(jnp.float32)


def portable(
    tokens,
    lengths,
    cotangent,
    qkv_weight,
    out_weight,
    up_weight,
    down_weight,
    biases,
    up_bias,
    gains,
):
    slots = lengths.shape[0]
    rows, width = tokens.shape
    seq = rows // slots
    heads = width // HEAD_SIZE
    scale = 1.0 / math.sqrt(HEAD_SIZE)
    w_qkv = lax.all_gather(qkv_weight, "fsdp", axis=0, tiled=True)
    w_out = lax.all_gather(out_weight, "fsdp", axis=0, tiled=True)
    w_up = lax.all_gather(up_weight, "fsdp", axis=0, tiled=True)
    w_down = lax.all_gather(down_weight, "fsdp", axis=0, tiled=True)
    bias_rows, bias_up, gain_rows = gather_small(biases, up_bias, gains)

    def split(values):
        return values.reshape(slots, seq, heads, HEAD_SIZE)

    def join(values):
        return values.reshape(rows, width)

    sums = matmul(tokens, w_qkv)
    query = split(low(sums[:, :width] + bias_rows[0]))
    key = split(low(sums[:, width : 2 * width]))
    value = split(low(sums[:, 2 * width :] + bias_rows[1]))
    live = jnp.arange(seq)[None, :] < lengths[:, None]
    scores = scale * jnp.einsum(
        "bshd,bthd->bhst", query, key, preferred_element_type=jnp.float32
    )
    scores = jnp.where(live[:, None, None, :], scores, -1e30)
    exps = jnp.exp(scores - jnp.max(scores, axis=-1, keepdims=True))
    probs = exps / jnp.sum(exps, axis=-1, keepdims=True)
    probs_low = low(probs)
    mixed = low(
        join(jnp.einsum("bhst,bthd->bshd", probs_low, value, preferred_element_type=jnp.float32))
    )
    first, first_inverse = normalize(
        tokens.astype(jnp.float32) + matmul(mixed, w_out) + bias_rows[2]
    )
    first_norm = first * gain_rows[0] + bias_rows[3]
    first_low = low(first_norm)
    inner = matmul(first_low, w_up) + bias_up
    cumulative = 0.5 * (1.0 + lax.erf(inner * math.sqrt(0.5)))
    act_low = low(inner * cumulative)
    slope = low(cumulative + inner * jnp.exp(-0.5 * inner * inner) / math.sqrt(2.0 * math.pi))
    second, second_inverse = normalize(first_norm + matmul(act_low, w_down) + bias_rows[4])
    layer_out = low(second * gain_rows[1] + bias_rows[5])

    grad_out = cotangent * live.reshape(rows, 1).astype(jnp.float32)
    grad_h2 = norm_back(grad_out, second, second_inverse, gain_rows[1])
    grad_branch = low(grad_h2)
    down_grad = reduce_weight(transposed_left(act_low, grad_branch))
    grad_inner = low(transposed_right(grad_branch, w_down) * slope)
    up_grad = reduce_weight(transposed_left(first_low, grad_inner))
    grad_first = grad_h2 + transposed_right(grad_inner, w_up)
    grad_h1 = norm_back(grad_first, first, first_inverse, gain_rows[0])
    grad_attn = low(grad_h1)
    out_grad = reduce_weight(transposed_left(mixed, grad_attn))
    grad_mixed = split(low(transposed_right(grad_attn, w_out)))
    grad_probs = jnp.einsum(
        "bshd,bthd->bhst", grad_mixed, value, preferred_element_type=jnp.float32
    )
    shared = jnp.sum(probs * grad_probs, axis=-1, keepdims=True)
    grad_scores = low(probs * (grad_probs - shared))
    grad_query = scale * jnp.einsum(
        "bhst,bthd->bshd", grad_scores, key, preferred_element_type=jnp.float32
    )
    grad_key = scale * jnp.einsum(
        "bhst,bshd->bthd", grad_scores, query, preferred_element_type=jnp.float32
    )
    grad_value = jnp.einsum(
        "bhst,bshd->bthd", probs_low, grad_mixed, preferred_element_type=jnp.float32
    )
    grad_qkv = jnp.concatenate(
        [join(low(grad_query)), join(low(grad_key)), join(low(grad_value))], axis=1
    )
    qkv_grad = reduce_weight(transposed_left(tokens, grad_qkv))
    token_grad = grad_h1 + transposed_right(grad_qkv, w_qkv)
    small = jnp.stack(
        [
            column_sum(grad_qkv[:, :width]),
            column_sum(grad_qkv[:, 2 * width :]),
            column_sum(grad_attn),
            column_sum(grad_first),
            column_sum(grad_branch),
            column_sum(grad_out),
            column_sum(grad_first * first),
            column_sum(grad_out * second),
        ]
    )
    owner = lax.axis_index("fsdp")
    small, up_sum = lax.psum((small, column_sum(grad_inner)), ("fsdp", "rep"))
    own, own_up = biases.shape[1], up_bias.shape[0]
    small = lax.dynamic_slice(small, (0, owner * own), (8, own))
    up_bias_grad = lax.dynamic_slice(up_sum, (owner * own_up,), (own_up,))
    return (
        layer_out,
        token_grad,
        qkv_grad,
        out_grad,
        up_grad,
        down_grad,
        small[:6],
        up_bias_grad,
        small[6:],
    )


MESH = pl.DeviceIdType.MESH
F32 = jnp.float32
BF16 = jnp.bfloat16
MIB = 1 << 20


def dot_nn(a, b):
    return lax.dot_general(a, b, (((1,), (0,)), ((), ())), preferred_element_type=F32)


def dot_nt(a, b):
    return lax.dot_general(a, b, (((1,), (1,)), ((), ())), preferred_element_type=F32)


def dot_tn(a, b):
    return lax.dot_general(a, b, (((0,), (0,)), ((), ())), preferred_element_type=F32)


class Place:
    def __init__(self):
        f, z = lax.axis_index("fsdp"), lax.axis_index("rep")
        self.f, self.z = f, z
        self.core = lax.rem(f, 2)
        self.x = lax.rem(lax.div(f, 2), 2)
        self.y = lax.div(f, 4)
        self.chip = lax.div(f, 2)
        self.fx = f + 2 - 4 * self.x
        self.fy = f + 4 - 8 * self.y
        self.fd = self.fx + 4 - 8 * self.y
        self.fs = f + 1 - 2 * self.core
        self.par = lax.rem(z, 2)
        self.zn = z + 1 - 2 * self.par

    def dev(self, f=None, z=None):
        return {"fsdp": self.f if f is None else f, "rep": self.z if z is None else z}


def remote(src, dst, send_sem, recv_sem, device):
    return pltpu.make_async_remote_copy(
        src_ref=src, dst_ref=dst, send_sem=send_sem, recv_sem=recv_sem,
        device_id=device, device_id_type=MESH,
    )


UNITS = (
    ("q", 0, 32, 0),
    ("q", 32, 32, 0),
    ("q", 64, 32, 0),
    ("q", 96, 32, 0),
    ("o", 0, 128, 0),
    ("u", 0, 64, 0),
    ("u", 64, 64, 0),
    ("d", 0, 128, 0),
    ("d", 128, 128, 0),
    ("d", 256, 128, 16),
    ("d", 384, 128, 16),
)
FORWARD_PLAN = (
    ("direct", 0), ("direct", 1), ("direct", 2), ("direct", 3), ("small", 0), ("fx", 0), ("fy", 0),
    ("direct", 4), ("fx", 1), ("fy", 1), ("fx", 2), ("fy", 2), ("r2", 0), ("fx", 3), ("fy", 3), ("r3", 0),
    ("r5", 0), ("r4", 0), ("r2", 1), ("r3", 1), ("direct", 5), ("fx", 4), ("fy", 4), ("r2", 2), ("r5", 1),
    ("r4", 1), ("r3", 2), ("r5", 2), ("r4", 2), ("r2", 3), ("r5", 3), ("r4", 3), ("r3", 3), ("direct", 6),
    ("done", 0), ("done", 1), ("done", 2), ("done", 3), ("qkv", 0), ("fx", 5), ("fy", 5), ("r2", 4),
    ("r3", 4), ("at", 0, 1), ("r4", 4), ("r5", 4), ("at", 1, 4), ("direct", 7), ("at", 4, 6), ("fx", 6),
    ("fy", 6), ("at", 6, 8), ("r2", 5), ("at", 8, 12), ("r4", 5), ("r5", 5), ("direct", 8), ("at", 12, 13),
    ("r3", 5), ("at", 13, 14), ("fx", 7), ("fy", 7), ("at", 14, 16), ("done", 4), ("out", 0), ("r2", 6),
    ("r4", 6), ("r5", 6), ("direct", 9), ("fx", 8), ("fy", 8), ("r3", 6), ("direct", 10), ("r5", 7),
    ("r4", 7), ("done", 5), ("done", 6), ("up", 0, 1), ("r2", 7), ("up", 1, 2), ("fx", 9), ("fy", 9),
    ("up", 2, 3), ("r3", 7), ("up", 3, 4), ("r4", 8), ("r5", 8), ("up", 4, 5), ("r2", 8), ("up", 5, 7),
    ("fx", 10), ("fy", 10), ("r3", 8), ("up", 7, 8), ("r2", 9), ("r4", 9), ("r5", 9), ("done", 7), ("dn", 7),
    ("r3", 9), ("done", 8), ("dn", 8), ("r2", 10), ("r4", 10), ("r5", 10), ("done", 9), ("tidy", 0),
    ("dn", 9), ("r3", 10), ("done", 10), ("dn", 10), ("last", 0),
)
KINDS = 13


class Gather:
    def __init__(self, place, unit, shard, full, base, rows, extra, send, recv, local):
        self.p, self.unit, self.shard, self.full = place, unit, shard, full
        self.base, self.rows, self.size = base, rows, shard.shape[0]
        self.send_sem, self.recv_sem, self.local_sem = send, recv, local
        p, half = place, rows // 2
        one, two = half * p.par, half * (1 - p.par)
        wide, rest = half + extra, half - extra
        near_x, near_y = rest * p.par, rest * (1 - p.par)
        far_x, far_y = wide * (1 - p.par), wide * p.par
        to_x, to_y, to_s, to_z = p.dev(f=p.fx), p.dev(f=p.fy), p.dev(f=p.fs), p.dev(z=p.zn)
        sx, sy, sd = (g + 1 - 2 * p.core for g in (p.fx, p.fy, p.fd))
        self.table = (
            ((p.fx, near_x), (p.f, near_x), wide, to_x),
            ((p.fy, near_y), (p.f, near_y), wide, to_y),
            ((p.fx, far_x), (p.fx, far_y), rest, to_z),
            ((p.fy, far_y), (p.fy, far_x), rest, to_z),
            ((p.fd, one), (p.fx, one), half, to_y),
            ((p.fd, two), (p.fy, two), half, to_x),
            ((p.fs, 0), (p.f, 0), rows, to_s),
            ((sx, near_x), (p.fx, near_x), wide, to_s),
            ((sy, near_y), (p.fy, near_y), wide, to_s),
            ((sx, far_x), (p.fx, far_x), rest, to_s),
            ((sy, far_y), (p.fy, far_y), rest, to_s),
            ((sd, one), (p.fd, one), half, to_s),
            ((sd, two), (p.fd, two), half, to_s),
        )

    def at(self, owner, lo, n):
        return self.full.at[pl.ds(pl.multiple_of(owner * self.size + self.base + lo, 16), n)]

    def copy(self, kind, sending):
        received, sent, n, device = self.table[kind]
        owner, lo = sent if sending else received
        here = self.at(owner, lo, n)
        src = self.shard.at[pl.ds(pl.multiple_of(self.base + lo, 16), n)] if kind in (0, 1, 6) else here
        return remote(src, here, self.send_sem.at[self.unit, kind], self.recv_sem.at[self.unit, kind], device)

    def start(self, *kinds):
        for kind in kinds:
            self.copy(kind, True).start()

    def got(self, *kinds):
        for kind in kinds:
            self.copy(kind, False).wait_recv()

    def sent(self):
        for kind in range(KINDS):
            self.copy(kind, True).wait_send()

    def own(self):
        src = self.shard.at[pl.ds(self.base, self.rows)]
        return pltpu.make_async_copy(src, self.at(self.p.f, 0, self.rows), self.local_sem.at[self.unit])

    def direct(self):
        self.start(0, 1, 6)
        self.own().start()

    def pass_on(self, arrived, *kinds):
        self.got(arrived)
        self.start(*kinds)

    def done(self):
        self.got(6, 7, 8, 9, 10, 11, 12)
        self.own().wait()


def forward_kernel(
    lengths, biases, up_bias, gains, tokens, cot, sh_q, sh_o, sh_u, sh_d,
    layer_out, wq_out, wo_out, wu_out, wd_out, qkv_out, slope_out, act_pair, first_pair, mixed_pair,
    tok_pair, branch_pair, norm_out, inv_out, grad_out_ref, params_out, sums_out,
    x, wq, wo, wu, wd, qkv, mixed, norm, first_low, act, slope, acc, cot_v, gh2, out_v, gb, smalls, params,
    inv_v, sums, up_rows, small,
    ag_send, ag_recv, ag_local, sm_send, sm_recv, io, pair_send, pair_recv, pair_local, wd_sem,
):
    p = Place()
    rows, width = x.shape
    slots = lengths.shape[0]
    seq = rows // slots
    others = [lax.rem(p.f + k, 8) for k in range(1, 8)]
    barrier = pltpu.get_barrier_semaphore()
    for g in others:
        pl.semaphore_signal(barrier, inc=1, device_id=p.dev(f=g), device_id_type=MESH)
    pl.semaphore_signal(barrier, inc=1, device_id=p.dev(z=p.zn), device_id_type=MESH)
    loads = [
        pltpu.make_async_copy(tokens, x, io.at[0]),
        pltpu.make_async_copy(cot, cot_v, io.at[1]),
    ]
    for c in loads:
        c.start()
    small[...] = jnp.zeros_like(small)
    small[0:6] = biases[...].astype(F32)
    small[6:8] = gains[...].astype(F32)
    for i in range(4):
        small[8 + i] = up_bias[i * 128 : (i + 1) * 128].astype(F32)
    smalls[p.f] = small[...]
    pl.semaphore_wait(barrier, 8)

    def small_copy(k, owner, device):
        return remote(small, smalls.at[owner], sm_send.at[k], sm_recv.at[k], device)

    for k, g in enumerate(others):
        small_copy(k, p.f, p.dev(f=g)).start()

    weights = {"q": (sh_q, wq), "o": (sh_o, wo), "u": (sh_u, wu), "d": (sh_d, wd)}
    parts = [Gather(p, i, *weights[n], *piece, ag_send, ag_recv, ag_local) for i, (n, *piece) in enumerate(UNITS)]

    mine = pl.ds(pl.multiple_of(p.core * rows, rows), rows)

    def pair(index, chip, src, dst, cols):
        own = pl.ds(pl.multiple_of((2 * chip + p.core) * cols, cols), cols)
        other = pl.ds(pl.multiple_of((2 * chip + 1 - p.core) * cols, cols), cols)
        here = dst.at[mine, pl.ds(chip * cols, cols)]
        return (
            pltpu.make_async_copy(src.at[:, own], here, pair_local.at[index, chip]),
            remote(src.at[:, other], here, pair_send.at[index, chip], pair_recv.at[index, chip], p.dev(f=p.fs)),
        )

    pairs = []

    def start_pair(index, src, dst, cols, chips=range(4)):
        for chip in chips:
            for c in pair(index, chip, src, dst, cols):
                c.start()
            pairs.append((index, chip, src, dst, cols))

    stores = []

    def store(src, dst, sem):
        stores.append(pltpu.make_async_copy(src, dst, sem))
        stores[-1].start()

    def small_params(_):
        loads[0].wait()
        start_pair(0, x, tok_pair, 128)
        for k in range(7):
            back = lax.rem(p.f + 7 - k, 8)
            small_copy(k, back, p.dev(f=back)).wait_recv()
        for g in range(8):
            part = smalls[g]
            params[:, g * 128 : (g + 1) * 128] = part
            for j in range(4):
                up_rows[g : g + 1, j * 128 : (j + 1) * 128] = part[8 + j : 9 + j]

    def project(_):
        store(wq, wq_out, io.at[2])
        for j in range(3):
            part = dot_nn(x[...], wq[:, j * width : (j + 1) * width])
            if j == 0:
                part = part + params[0:1]
            if j == 2:
                part = part + params[1:2]
            qkv[:, j * width : (j + 1) * width] = part.astype(BF16)
        store(qkv, qkv_out, io.at[3])

    left = lax.broadcasted_iota(jnp.int32, (seq, 128), 1) < HEAD_SIZE
    key_row = lax.broadcasted_iota(jnp.int32, (seq, seq), 0)

    def attend(step, carry):
        slot, pair_of = lax.div(step, 8), lax.rem(step, 8)
        at_rows = pl.ds(pl.multiple_of(slot * seq, seq), seq)
        col = pl.multiple_of(pair_of * 128, 128)
        q = qkv[at_rows, pl.ds(col, 128)]
        k = qkv[at_rows, pl.ds(pl.multiple_of(width + col, 128), 128)]
        v = qkv[at_rows, pl.ds(pl.multiple_of(2 * width + col, 128), 128)]
        dead = key_row >= lengths[slot]
        outs = []
        for head in range(2):
            k_head = jnp.where(left if head == 0 else ~left, k, jnp.zeros_like(k))
            scores = dot_nt(k_head, q) * (1.0 / math.sqrt(HEAD_SIZE))
            scores = jnp.where(dead, -1e30, scores)
            exps = jnp.exp(scores - jnp.max(scores, axis=0, keepdims=True))
            probs = exps * (1.0 / jnp.sum(exps, axis=0, keepdims=True))
            outs.append(dot_tn(probs.astype(BF16), v))
        mixed[at_rows, pl.ds(col, 128)] = jnp.where(left, outs[0], outs[1]).astype(BF16)
        return carry

    steps = 8 * slots

    def attention(first, last):
        lax.fori_loop(first * steps // 16, last * steps // 16, attend, 0)
        if last == 16:
            start_pair(1, mixed, mixed_pair, 128)

    def first_norm(_):
        store(wo, wo_out, io.at[4])
        hidden = x[...].astype(F32) + dot_nn(mixed[...], wo[...]) + params[2:3]
        center = hidden - row_mean(hidden)
        inverse = lax.rsqrt(row_mean(center * center) + 1e-05)
        norm[...] = center * inverse
        inv_v[...] = jnp.broadcast_to(inverse, inv_v.shape)
        shifted = norm[...] * params[6:7] + params[3:4]
        first_low[...] = shifted.astype(BF16)
        acc[...] = shifted + params[4:5]
        start_pair(2, first_low, first_pair, 128)
        store(norm, norm_out, io.at[5])
        store(inv_v, inv_out, io.at[6])

    def up_step(j, carry):
        cols = pl.ds(pl.multiple_of(j * 512, 512), 512)
        inner = dot_nn(first_low[...], wu[:, cols]) + up_rows[pl.ds(j, 1), :]
        phi = 0.5 * (1.0 + lax.erf(inner * math.sqrt(0.5)))
        act[:, cols] = (inner * phi).astype(BF16)
        density = jnp.exp(-0.5 * inner * inner) * (1.0 / math.sqrt(2.0 * math.pi))
        slope[:, cols] = (phi + inner * density).astype(BF16)
        return carry

    def up(first, last):
        if first == 0:
            store(wu, wu_out, io.at[7])
        lax.fori_loop(first, last, up_step, 0)
        if last == 4:
            start_pair(3, act, act_pair, 512, range(2))
        if last == 8:
            start_pair(3, act, act_pair, 512, range(2, 4))
            store(slope, slope_out, io.at[8])

    def down(u):
        _, lo, n, _ = UNITS[u]
        for g in range(8):
            at = pl.ds(g * 512 + lo, n)
            store(wd.at[at], wd_out.at[at], wd_sem.at[g, u])
        for j in range(0, 8, 1024 // n):
            cols = [slice(512 * g + lo, 512 * g + lo + n) for g in range(j, j + 1024 // n)]
            left = jnp.concatenate([act[:, c] for c in cols], axis=1)
            right = jnp.concatenate([wd[c, :] for c in cols], axis=0)
            acc[...] += dot_nn(left, right)

    tidied = []

    def tidy(_):
        for k, g in enumerate(others):
            small_copy(k, p.f, p.dev(f=g)).wait_send()
        for part in parts:
            if UNITS[part.unit][0] != "d":
                part.sent()
        count = len(stores) - 8
        for c in stores[:count]:
            c.wait()
        for args in pairs[:12]:
            for c in pair(*args):
                c.wait()
        tidied.append(count)

    def second_norm(_):
        loads[1].wait()
        hidden = acc[...]
        center = hidden - row_mean(hidden)
        inverse = lax.rsqrt(row_mean(center * center) + 1e-05)
        second = center * inverse
        row_at = lax.broadcasted_iota(jnp.int32, (seq, 1), 0)
        live = jnp.concatenate([(row_at < lengths[s]).astype(F32) for s in range(slots)], axis=0)
        e = cot_v[...] * live
        scaled = e * params[7:8]
        gh2[...] = inverse * (scaled - row_mean(scaled) - second * row_mean(scaled * second))
        gb[...] = gh2[...].astype(BF16)
        swap = (
            pltpu.make_async_copy(gb, branch_pair.at[mine], pair_local.at[4, 0]),
            remote(gb, branch_pair.at[mine], pair_send.at[4, 0], pair_recv.at[4, 0], p.dev(f=p.fs)),
        )
        for c in swap:
            c.start()
        store(gh2, grad_out_ref, io.at[11])
        store(params, params_out, io.at[12])
        out_v[...] = (second * params[7:8] + params[5:6]).astype(BF16)
        store(out_v, layer_out, io.at[10])
        sums[...] = jnp.zeros_like(sums)
        sums[0:1] = jnp.sum(e * second, axis=0, keepdims=True)
        sums[1:2] = jnp.sum(e, axis=0, keepdims=True)
        sums[2:3] = jnp.sum(gb[...].astype(F32), axis=0, keepdims=True)
        store(sums, sums_out, io.at[13])
        for part in parts:
            if UNITS[part.unit][0] == "d":
                part.sent()
        for args in pairs[12:]:
            for c in pair(*args):
                c.wait()
        for c in stores[tidied[0] :]:
            c.wait()
        for c in swap:
            c.wait()

    work = {
        "small": small_params, "qkv": project, "at": attention, "out": first_norm, "up": up, "dn": down,
        "tidy": tidy, "last": second_norm,
        "direct": lambda u: parts[u].direct(), "done": lambda u: parts[u].done(),
        "fx": lambda u: parts[u].pass_on(0, 4, 2, 7), "fy": lambda u: parts[u].pass_on(1, 5, 3, 8),
        "r2": lambda u: parts[u].pass_on(2, 9), "r3": lambda u: parts[u].pass_on(3, 10),
        "r4": lambda u: parts[u].pass_on(4, 11), "r5": lambda u: parts[u].pass_on(5, 12),
    }
    for name, *which in FORWARD_PLAN:
        work[name](*which)


def forward_call(tokens, lengths, cotangent, qkv_w, out_w, up_w, down_w, biases, up_bias, gains):
    rows, width = tokens.shape
    ff = up_w.shape[1]
    anyspace = pl.BlockSpec(memory_space=pl.ANY)
    shape = jax.ShapeDtypeStruct
    outs = [
        shape((rows, width), BF16),
        shape((width, 3 * width), BF16),
        shape((width, width), BF16),
        shape((width, ff), BF16),
        shape((ff, width), BF16),
        shape((rows, 3 * width), BF16),
        shape((rows, ff), BF16),
        shape((2 * rows, ff // 2), BF16),
        shape((2 * rows, width // 2), BF16),
        shape((2 * rows, width // 2), BF16),
        shape((2 * rows, width // 2), BF16),
        shape((2 * rows, width), BF16),
        shape((rows, width), F32),
        shape((rows, 128), F32),
        shape((rows, width), F32),
        shape((16, width), F32),
        shape((8, width), F32),
    ]
    dma = pltpu.SemaphoreType.DMA
    scratch = [
        pltpu.VMEM((rows, width), BF16),
        pltpu.VMEM((width, 3 * width), BF16),
        pltpu.VMEM((width, width), BF16),
        pltpu.VMEM((width, ff), BF16),
        pltpu.VMEM((ff, width), BF16),
        pltpu.VMEM((rows, 3 * width), BF16),
        pltpu.VMEM((rows, width), BF16),
        pltpu.VMEM((rows, width), F32),
        pltpu.VMEM((rows, width), BF16),
        pltpu.VMEM((rows, ff), BF16),
        pltpu.VMEM((rows, ff), BF16),
        pltpu.VMEM((rows, width), F32),
        pltpu.VMEM((rows, width), F32),
        pltpu.VMEM((rows, width), F32),
        pltpu.VMEM((rows, width), BF16),
        pltpu.VMEM((rows, width), BF16),
        pltpu.VMEM((8, 16, 128), F32),
        pltpu.VMEM((16, width), F32),
        pltpu.VMEM((rows, 128), F32),
        pltpu.VMEM((8, width), F32),
        pltpu.VMEM((8, ff // 8), F32),
        pltpu.VMEM((16, 128), F32),
        dma((len(UNITS), KINDS)),
        dma((len(UNITS), KINDS)),
        dma((len(UNITS),)),
        dma((7,)),
        dma((7,)),
        dma((14,)),
        dma((5, 4)),
        dma((5, 4)),
        dma((5, 4)),
        dma((8, len(UNITS))),
    ]
    return pl.pallas_call(
        forward_kernel,
        out_shape=outs,
        in_specs=[pl.BlockSpec(memory_space=pltpu.SMEM)] + [pl.BlockSpec(memory_space=pltpu.VMEM)] * 3 + [anyspace] * 6,
        out_specs=[anyspace] * len(outs),
        scratch_shapes=scratch,
        name="forward",
        cost_estimate=pl.CostEstimate(flops=2 * 512 * 12582912, bytes_accessed=60 * MIB, transcendentals=4 * MIB),
        compiler_params=pltpu.CompilerParams(
            collective_id=0, has_side_effects=True, vmem_limit_bytes=60 * MIB
        ),
    )(lengths, biases, up_bias, gains, tokens, cotangent, qkv_w, out_w, up_w, down_w)


BLOCKS = 12
FAR = 2
SHARED = (1, 2)
PIECES = (
    (0, 0, 64),
    (3, 0, 64),
    (2, None, 32),
    (4, 0, 64),
    (1, None, 32),
    (5, 0, 64),
    (7, 0, 64),
    (6, 0, 64),
    (8, 0, 64),
    (9, 0, 32),
    (9, 32, 32),
    (10, 0, 32),
    (10, 32, 32),
    (11, 0, 16),
    (11, 16, 16),
    (11, 32, 16),
    (11, 48, 16),
)
PLAN = (
    ("start", 0), ("down", 0), ("begin", 0), ("down", 1), ("swap", 1, 0), ("swap", 1, 1), ("down", 2),
    ("down", 3), ("swap", 2, 0), ("begin", 1), ("g", 0), ("h", 0), ("second", 0), ("g", 1), ("swap", 2, 1),
    ("h", 1), ("second", 1), ("u", 0), ("begin", 4), ("along", 0), ("begin", 3), ("g", 2), ("along", 1),
    ("h", 2), ("u", 1), ("second", 4), ("begin", 5), ("g", 3), ("h", 3), ("u", 2), ("second", 3),
    ("along", 4), ("inward", 0), ("norm", 0), ("begin", 2), ("u", 3), ("second", 5), ("hand", 0),
    ("inward", 1), ("gm", 0), ("begin", 6), ("o", 0), ("along", 3), ("inward", 4), ("at", 0, 1),
    ("second", 2), ("pass", 0), ("at", 1, 3), ("hand", 1), ("inward", 3), ("along", 5), ("at", 3, 4),
    ("begin", 7), ("at", 4, 5), ("hand", 4), ("at", 5, 7), ("second", 6), ("pass", 1), ("inward", 5),
    ("at", 7, 8), ("along", 2), ("hand", 3), ("at", 8, 10), ("inward", 2), ("pass", 4), ("begin", 8),
    ("at", 10, 12), ("second", 7), ("hand", 5), ("at", 12, 14), ("pass", 3), ("along", 6), ("close", 0),
    ("at", 14, 16), ("hand", 2), ("q", 0), ("inward", 6), ("begin", 9), ("pass", 5), ("q", 1), ("second", 8),
    ("q", 2), ("pass", 2), ("along", 7), ("begin", 10), ("close", 1), ("small", 0), ("hand", 6),
    ("begin", 11), ("t", 0), ("second", 9), ("inward", 7), ("t", 1), ("along", 8), ("close", 4), ("t", 2),
    ("pass", 6), ("begin", 12), ("level", 1), ("inward", 8), ("second", 10), ("hand", 7), ("begin", 13),
    ("close", 3), ("second", 11), ("along", 9), ("begin", 14), ("begin", 15), ("second", 12), ("hand", 8),
    ("inward", 9), ("along", 10), ("close", 5), ("begin", 16), ("second", 13), ("pass", 7), ("along", 11),
    ("close", 2), ("inward", 10), ("pass", 8), ("second", 14), ("hand", 9), ("inward", 11), ("hand", 10),
    ("second", 15), ("along", 12), ("second", 16), ("along", 13), ("along", 14), ("pass", 9), ("close", 6),
    ("inward", 12), ("hand", 11), ("along", 15), ("along", 16), ("pass", 10), ("inward", 13), ("inward", 14),
    ("hand", 12), ("inward", 15), ("pass", 11), ("hand", 13), ("hand", 14), ("inward", 16), ("pass", 12),
    ("hand", 15), ("level", 2), ("pass", 13), ("close", 7), ("pass", 14), ("hand", 16), ("pass", 15),
    ("close", 8), ("pass", 16), ("close", 9), ("close", 10), ("close", 11), ("close", 12), ("close", 13),
    ("close", 14), ("close", 15), ("close", 16),
)
S1X, S1Y, S2X, S2Y, Z1G, Z1K, Z2, FM, FE, FF = range(10)


class Reduce:
    def __init__(self, place, prod, got_x, got_y, end_x, end_y, from_end, from_mid, swapped, out_at, send, recv, local, swap_send, swap_recv):
        self.p = place
        self.prod, self.got_x, self.got_y, self.end_x, self.end_y = prod, got_x, got_y, end_x, end_y
        self.from_end, self.from_mid, self.swapped, self.out_at = from_end, from_mid, swapped, out_at
        self.send, self.recv, self.local = send, recv, local
        self.swap_send, self.swap_recv = swap_send, swap_recv
        z = place.z
        self.mid = 1 + lax.div(z, 2)
        self.end = 3 * lax.div(z, 2)
        self.is_mid = z == self.mid
        self.is_end = z == self.end

    def rows(self, u, theirs=False):
        b, o, n = PIECES[u]
        if o is None:
            o = pl.multiple_of(32 * (1 - self.p.par if theirs else self.p.par), 32)
        return b, o, n

    def z_rows(self, u):
        b, o, n = PIECES[u]
        return (b, 0, 64) if o is None else (b, o, n)

    def keep(self, o, n):
        return pl.ds(pl.multiple_of(64 * (self.mid - 1) + o, 16), n)

    def give(self, o, n):
        return pl.ds(pl.multiple_of(64 * (2 - self.mid) + o, 16), n)

    def copy(self, kind, u, sending=True):
        p = self.p
        b, o, n = self.rows(u, theirs=kind in (Z1G, Z1K) and not sending)
        _, oz, nz = self.z_rows(u)
        x, y, xn, yn = p.x, p.y, 1 - p.x, 1 - p.y
        near, far = pl.ds(o, n), pl.ds(64 + o, n)
        keep, give = self.keep(oz, nz), self.give(oz, nz)
        to_mid, to_end, to_other = p.dev(z=self.mid), p.dev(z=self.end), p.dev(z=3 - self.mid)
        own = self.prod.at[b, y, x]
        if kind == S1X:
            src, dst, dev = self.prod.at[b, :, xn, near], self.got_x.at[b, :, near], p.dev(f=p.fx)
        elif kind == S1Y:
            src, dst, dev = self.prod.at[b, yn, :, far], self.got_y.at[b, :, near], p.dev(f=p.fy)
        elif kind == S2Y:
            src, dst, dev = self.prod.at[b, yn, x, near], self.end_y.at[b, near], p.dev(f=p.fy)
        elif kind == S2X:
            src, dst, dev = self.prod.at[b, y, xn, far], self.end_x.at[b, near], p.dev(f=p.fx)
        elif kind == Z1G:
            src, dst, dev = own.at[self.give(o, n)], self.from_end.at[b, self.give(o, n)], to_mid
        elif kind == Z1K:
            src, dst, dev = own.at[self.keep(o, n)], self.from_end.at[b, self.keep(o, n)], to_mid
        elif kind == Z2:
            src, dst, dev = own.at[give], self.from_mid.at[b, pl.ds(oz, nz)], to_other
        elif kind == FM:
            src, dst, dev = own.at[keep], self.out_at(b, keep if sending else give), to_other
        elif kind == FE:
            src, dst, dev = own.at[keep], self.out_at(b, keep), to_end
        elif u >= len(PIECES) - FAR:
            src, dst, dev = own.at[keep], self.out_at(b, keep if sending else give), p.dev(z=3 - self.end)
        else:
            src, dst, dev = self.out_at(b, give), self.out_at(b, give), to_end
        return remote(src, dst, self.send.at[kind, u], self.recv.at[kind, u], dev)

    def swap(self, b, half):
        i = SHARED.index(b)
        src = self.prod.at[b, :, :, pl.ds(pl.multiple_of(64 * half + 32 * (1 - self.p.par), 32), 32)]
        dst = self.swapped.at[i, :, :, pl.ds(32 * half, 32)]
        return remote(src, dst, self.swap_send.at[i, half], self.swap_recv.at[i, half], self.p.dev(z=self.p.zn))

    def swap_out(self, b, half):
        self.swap(b, half).start()

    def begin(self, u):
        b, o, n = self.rows(u)
        for half, kind in enumerate((S1X, S1Y)):
            if b in SHARED:
                at = pl.ds(pl.multiple_of(64 * half + o, 32), n)
                self.swap(b, half).wait()
                part = self.swapped[SHARED.index(b), :, :, 32 * half : 32 * half + 32]
                self.prod[b, :, :, at] = self.prod[b, :, :, at] + part
            self.copy(kind, u).start()

    def second(self, u):
        x, y = self.p.x, self.p.y
        b, o, n = self.rows(u)
        near, far = pl.ds(o, n), pl.ds(64 + o, n)
        self.copy(S1X, u).wait_recv()
        self.prod[b, :, x, near] = self.prod[b, :, x, near] + self.got_x[b, :, near]
        self.copy(S2Y, u).start()
        self.copy(S1Y, u).wait_recv()
        self.prod[b, y, :, far] = self.prod[b, y, :, far] + self.got_y[b, :, near]
        self.copy(S2X, u).start()

    def along(self, u):
        x, y = self.p.x, self.p.y
        b, o, n = self.rows(u)
        near, far = pl.ds(o, n), pl.ds(64 + o, n)
        self.copy(S2Y, u).wait_recv()
        self.prod[b, y, x, near] = self.prod[b, y, x, near] + self.end_y[b, near]
        self.copy(S2X, u).wait_recv()
        self.prod[b, y, x, far] = self.prod[b, y, x, far] + self.end_x[b, near]

        @pl.when(self.is_end)
        def _():
            self.copy(Z1G, u).start()
            self.copy(Z1K, u).start()

    def inward(self, u):
        x, y = self.p.x, self.p.y
        b, o, n = self.rows(u, theirs=True)

        @pl.when(self.is_mid)
        def _():
            give = self.give(o, n)
            self.copy(Z1G, u, False).wait_recv()
            if b in SHARED:
                self.prod[b, y, x, give] = self.from_end[b, give]
            else:
                self.prod[b, y, x, give] = self.prod[b, y, x, give] + self.from_end[b, give]
            self.copy(Z2, u).start()

    def write(self, u):
        b, o, n = self.z_rows(u)
        keep = self.keep(o, n)
        return pltpu.make_async_copy(
            self.prod.at[b, self.p.y, self.p.x, keep], self.out_at(b, keep), self.local.at[u]
        )

    def hand_out(self, u):
        x, y = self.p.x, self.p.y
        b, o, n = self.z_rows(u)

        @pl.when(self.is_mid)
        def _():
            keep = self.keep(o, n)
            self.copy(Z1K, u, False).wait_recv()
            if b in SHARED:
                part = self.keep(*self.rows(u, theirs=True)[1:])
                self.prod[b, y, x, part] = self.from_end[b, part]
            self.copy(Z2, u).wait_recv()
            total = self.prod[b, y, x, keep].astype(F32) + self.from_mid[b, o : o + n].astype(F32)
            if b not in SHARED:
                total = total + self.from_end[b, keep].astype(F32)
            self.prod[b, y, x, keep] = total.astype(BF16)
            if u >= len(PIECES) - FAR:
                self.copy(FF, u).start()
            self.copy(FM, u).start()
            self.copy(FE, u).start()
            self.write(u).start()

    def hand_on(self, u):
        @pl.when(self.is_mid)
        def _():
            self.copy(FM, u, False).wait_recv()
            if u < len(PIECES) - FAR:
                self.copy(FF, u).start()

    def close(self, u):
        for kind in (S1X, S1Y, S2X, S2Y):
            self.copy(kind, u).wait_send()

        @pl.when(self.is_end)
        def _():
            self.copy(Z1G, u).wait_send()
            self.copy(Z1K, u).wait_send()
            self.copy(FE, u).wait_recv()
            self.copy(FF, u, False).wait_recv()

        @pl.when(self.is_mid)
        def _():
            for kind in (Z2, FM, FE, FF):
                self.copy(kind, u).wait_send()
            self.write(u).wait()


def backward_kernel(
    lengths, wq, wo, wu, wd, qkv, slope, act_pair, first_pair, mixed_pair, tok_pair, branch_pair,
    norm_in, inv_in, gh2, params_in, sums_in,
    token_grad, out_q, out_o, out_u, out_d, small_out,
    lhs, wbuf, slope_v, branch, gi, gq, gm, gh, norm, inv, params, sums_v, upsum,
    prod, got_x, got_y, end_x, end_y, from_end, from_mid, swapped,
    s_send, s_got, s_total, s_all, s_out,
    rs_send, rs_recv, rs_local, pair_send, pair_recv, load_sem, lhs_sem, w_sem, slope_sem,
    sm_send, sm_recv, smz_send, smz_recv, store_sem, swap_send, swap_recv,
):
    p = Place()
    rows, width = gh.shape
    slots = lengths.shape[0]
    seq = rows // slots
    planes = [lax.rem(p.f + k, 8) for k in range(1, 8)]
    levels = [lax.rem(p.z + k, 4) for k in range(1, 4)]
    barrier = pltpu.get_barrier_semaphore()
    for g in planes:
        pl.semaphore_signal(barrier, inc=1, device_id=p.dev(f=g), device_id_type=MESH)
    for g in levels:
        pl.semaphore_signal(barrier, inc=1, device_id=p.dev(z=g), device_id_type=MESH)

    mine = pl.ds(pl.multiple_of(p.core * rows, rows), rows)

    def lhs_copies(i):
        if i < 4:
            return [
                pltpu.make_async_copy(
                    act_pair.at[:, pl.ds(chip * 512 + i * 128, 128)],
                    lhs.at[i % 2, :, pl.ds(chip * 128, 128)],
                    lhs_sem.at[i, chip],
                )
                for chip in range(4)
            ]
        src = (first_pair, mixed_pair, tok_pair)[i - 4]
        return [pltpu.make_async_copy(src, lhs.at[i % 2], lhs_sem.at[i, 0])]

    def w_copy(i):
        if i < 8:
            j = i // 2
            src = wu.at[:, pl.ds(j * 1024, 1024)] if i % 2 else wd.at[pl.ds(j * 1024, 1024)]
        elif i == 8:
            src = wo
        else:
            src = wq.at[:, pl.ds((i - 9) * 1024, 1024)]
        return pltpu.make_async_copy(src, wbuf.at[i % 2], w_sem.at[i])

    def slope_copy(j):
        return pltpu.make_async_copy(slope.at[:, pl.ds(j * 1024, 1024)], slope_v.at[j % 2], slope_sem.at[j])

    loads = [
        pltpu.make_async_copy(src, dst, load_sem.at[i])
        for i, (src, dst) in enumerate(
            (
                (branch_pair, branch), (gh2, gh), (qkv, gq.at[mine]), (norm_in, norm), (inv_in, inv),
                (params_in, params), (sums_in, sums_v),
            )
        )
    ]
    for c in lhs_copies(0):
        c.start()
    loads[0].start()

    def out_at(b, at):
        if b < 4:
            return out_d.at[pl.ds(128 * b, 128)].at[at]
        if b < 8:
            return out_u.at[at, pl.ds((b - 4) * 1024, 1024)]
        if b == 8:
            return out_o.at[at]
        return out_q.at[at, pl.ds((b - 9) * 1024, 1024)]

    red = Reduce(
        p, prod, got_x, got_y, end_x, end_y, from_end, from_mid, swapped, out_at, rs_send, rs_recv, rs_local,
        swap_send, swap_recv,
    )

    def produce(b, left, right):
        prod[b] = dot_tn(left, right).astype(BF16).reshape(2, 2, 128, 1024)

    def to_pair(index, ref, cols):
        here = ref.at[mine, cols]
        return remote(here, here, pair_send.at[index], pair_recv.at[index], p.dev(f=p.fs))

    def block_cols(j):
        return pl.ds(j * 1024, 1024)

    whole = pl.ds(0, 1024)
    ga = branch

    def start(_):
        for c in lhs_copies(0):
            c.wait()
        loads[0].wait()
        for c in lhs_copies(1):
            c.start()
        w_copy(0).start()
        slope_copy(0).start()
        for c in loads[1:]:
            c.start()

    def down(b):
        for c in lhs_copies(b) if b > 0 else ():
            c.wait()
        produce(b, lhs[b % 2], branch[...])
        for c in lhs_copies(b + 2):
            c.start()
        if b == 0:
            pl.semaphore_wait(barrier, 10)
        if b == 3:
            loads[1].wait()

    def inner_step(j):
        w_copy(2 * j).wait()
        w_copy(2 * j + 1).start()
        slope_copy(j).wait()
        if j < 3:
            slope_copy(j + 1).start()
        inner = (dot_nt(branch[mine], wbuf[0]) * slope_v[j % 2].astype(F32)).astype(BF16)
        gi[mine, j * 1024 : (j + 1) * 1024] = inner
        to_pair(j, gi, block_cols(j)).start()
        upsum[j : j + 1] = jnp.sum(inner.astype(F32), axis=0, keepdims=True)

    def hidden_step(j):
        w_copy(2 * j + 1).wait()
        w_copy(2 * j + 2).start()
        gh[...] += dot_nt(gi[mine, j * 1024 : (j + 1) * 1024], wbuf[1])
        if j == 0:
            for c in lhs_copies(4):
                c.wait()

    def up_block(j):
        to_pair(j, gi, block_cols(j)).wait_recv()
        produce(4 + j, lhs[0], gi[:, j * 1024 : (j + 1) * 1024])
        if j == 3:
            for c in lhs_copies(6):
                c.start()

    def first_norm(_):
        for c in loads[2:]:
            c.wait()
        e = gh[...]
        scaled = e * params[6:7]
        n = norm[...]
        sums_v[3:4] = jnp.sum(e, axis=0, keepdims=True)
        sums_v[4:5] = jnp.sum(e * n, axis=0, keepdims=True)
        gh[...] = inv[:, 0:1] * (scaled - row_mean(scaled) - n * row_mean(scaled * n))
        ga[mine] = gh[...].astype(BF16)
        to_pair(4, ga, whole).start()
        sums_v[5:6] = jnp.sum(ga[mine].astype(F32), axis=0, keepdims=True)

    def grad_mixed(_):
        w_copy(8).wait()
        w_copy(9).start()
        gm[...] = dot_nt(ga[mine], wbuf[0]).astype(BF16)
        w_copy(10).start()

    def out_block(_):
        for c in lhs_copies(5):
            c.wait()
        to_pair(4, ga, whole).wait_recv()
        produce(8, lhs[1], ga[...])

    left = lax.broadcasted_iota(jnp.int32, (seq, 128), 1) < HEAD_SIZE
    key_row = lax.broadcasted_iota(jnp.int32, (seq, seq), 0)
    scale = 1.0 / math.sqrt(HEAD_SIZE)

    def attend(step, carry):
        slot, pair_of = lax.rem(step, slots), lax.div(step, slots)
        at_rows = pl.ds(pl.multiple_of(slot * seq, seq), seq)
        own_rows = pl.ds(pl.multiple_of(p.core * rows + slot * seq, seq), seq)
        col = pl.multiple_of(pair_of * 128, 128)
        at_q = pl.ds(col, 128)
        at_k = pl.ds(pl.multiple_of(width + col, 128), 128)
        at_v = pl.ds(pl.multiple_of(2 * width + col, 128), 128)
        q, k, v = gq[own_rows, at_q], gq[own_rows, at_k], gq[own_rows, at_v]
        do = gm[at_rows, at_q]
        dead = key_row >= lengths[slot]
        parts = []
        for head in range(2):
            lanes = left if head == 0 else ~left
            k_head = jnp.where(lanes, k, jnp.zeros_like(k))
            v_head = jnp.where(lanes, v, jnp.zeros_like(v))
            scores = jnp.where(dead, -1e30, dot_nt(k_head, q) * scale)
            exps = jnp.exp(scores - jnp.max(scores, axis=0, keepdims=True))
            probs = exps * (1.0 / jnp.sum(exps, axis=0, keepdims=True))
            d_probs = dot_nt(v_head, do)
            shared = jnp.sum(probs * d_probs, axis=0, keepdims=True)
            d_scores = (probs * (d_probs - shared)).astype(BF16)
            parts.append(
                (dot_tn(d_scores, k) * scale, dot_nn(d_scores, q) * scale, dot_nn(probs.astype(BF16), do))
            )
        for at, one, two in zip((at_q, at_k, at_v), *parts):
            gq[own_rows, at] = jnp.where(left, one, two).astype(BF16)
        return carry

    steps = 8 * slots

    def attention(first, last):
        lax.fori_loop(first * steps // 16, last * steps // 16, attend, 0)
        if last % 8 == 0:
            half = last // 8 - 1
            for j in range(3):
                to_pair(5 + 3 * half + j, gq, pl.ds(j * 1024 + 512 * half, 512)).start()

    def qkv_block(j):
        if j == 0:
            for c in lhs_copies(6):
                c.wait()
        for half in range(2):
            to_pair(5 + 3 * half + j, gq, pl.ds(j * 1024 + 512 * half, 512)).wait_recv()
        produce(9 + j, lhs[0], gq[:, j * 1024 : (j + 1) * 1024])

    order = (6, 7, 5, 3, 2, 1, 4, 0)

    def small_to(k):
        g = planes[k]
        return remote(s_send.at[g], s_got.at[p.f], sm_send.at[k], sm_recv.at[k], p.dev(f=g))

    def small_from(k):
        g = lax.rem(p.f + 7 - k, 8)
        return remote(s_send.at[g], s_got.at[g], sm_send.at[k], sm_recv.at[k], p.dev(f=g))

    def level_to(k):
        return remote(s_total, s_all.at[p.z], smz_send.at[k], smz_recv.at[k], p.dev(z=levels[k]))

    def level_from(k):
        g = lax.rem(p.z + 3 - k, 4)
        return remote(s_total, s_all.at[g], smz_send.at[k], smz_recv.at[k], p.dev(z=g))

    stores = (
        pltpu.make_async_copy(gh, token_grad, store_sem.at[0]),
        pltpu.make_async_copy(s_out, small_out, store_sem.at[1]),
    )

    def small(_):
        sums_v[6:7] = jnp.sum(gq[mine, 0:1024].astype(F32), axis=0, keepdims=True)
        sums_v[7:8] = jnp.sum(gq[mine, 2048:3072].astype(F32), axis=0, keepdims=True)
        for g in range(8):
            cols = slice(g * 128, (g + 1) * 128)
            for i, row in enumerate(order):
                s_send[g, i : i + 1] = sums_v[row : row + 1, cols]
            for i in range(4):
                lo = (g % 2) * 512 + i * 128
                s_send[g, 8 + i : 9 + i] = upsum[g // 2 : g // 2 + 1, lo : lo + 128]
        for k in range(7):
            small_to(k).start()
        s_got[p.f] = s_send[p.f]

    def token_step(j):
        w_copy(9 + j).wait()
        gh[...] += dot_nt(gq[mine, j * 1024 : (j + 1) * 1024], wbuf[(9 + j) % 2])
        if j == 0:
            w_copy(11).start()
        if j == 2:
            stores[0].start()

    def level(which):
        if which == 1:
            for k in range(7):
                small_from(k).wait_recv()
            total = s_got[0]
            for g in range(1, 8):
                total = total + s_got[g]
            s_total[...] = total
            for k in range(3):
                level_to(k).start()
            s_all[p.z] = total
            for j in range(4):
                to_pair(j, gi, block_cols(j)).wait_send()
            to_pair(4, ga, whole).wait_send()
            for j in range(3):
                for half in range(2):
                    to_pair(5 + 3 * half + j, gq, pl.ds(j * 1024 + 512 * half, 512)).wait_send()
            return
        for k in range(3):
            level_from(k).wait_recv()
        s_out[...] = (s_all[0] + s_all[1]) + (s_all[2] + s_all[3])
        stores[1].start()
        for k in range(7):
            small_to(k).wait_send()
        for k in range(3):
            level_to(k).wait_send()
        stores[0].wait()
        stores[1].wait()

    work = {
        "start": start, "down": down, "g": inner_step, "h": hidden_step, "u": up_block, "norm": first_norm,
        "gm": grad_mixed, "o": out_block, "at": attention, "q": qkv_block, "small": small, "t": token_step,
        "level": level, "begin": red.begin, "second": red.second, "along": red.along, "inward": red.inward,
        "swap": red.swap_out, "hand": red.hand_out, "pass": red.hand_on, "close": red.close,
    }
    for name, *which in PLAN:
        work[name](*which)


def backward_call(lengths, saved):
    wq, wo, wu, wd, qkv, slope = saved[:6]
    rows, width = qkv.shape[0], wo.shape[0]
    ff = wu.shape[1]
    anyspace = pl.BlockSpec(memory_space=pl.ANY)
    shape = jax.ShapeDtypeStruct
    dma = pltpu.SemaphoreType.DMA
    outs = [
        shape((rows, width), F32),
        shape((width // 8, 3 * width), BF16),
        shape((width // 8, width), BF16),
        shape((width // 8, ff), BF16),
        shape((ff // 8, width), BF16),
        shape((16, 128), F32),
    ]
    scratch = [
        pltpu.VMEM((2, 2 * rows, 512), BF16),
        pltpu.VMEM((2, 1024, 1024), BF16),
        pltpu.VMEM((2, rows, 1024), BF16),
        pltpu.VMEM((2 * rows, width), BF16),
        pltpu.VMEM((2 * rows, ff), BF16),
        pltpu.VMEM((2 * rows, 3 * width), BF16),
        pltpu.VMEM((rows, width), BF16),
        pltpu.VMEM((rows, width), F32),
        pltpu.VMEM((rows, width), F32),
        pltpu.VMEM((rows, 128), F32),
        pltpu.VMEM((16, width), F32),
        pltpu.VMEM((8, width), F32),
        pltpu.VMEM((4, width), F32),
        pltpu.VMEM((BLOCKS, 2, 2, 128, 1024), BF16),
        pltpu.VMEM((BLOCKS, 2, 64, 1024), BF16),
        pltpu.VMEM((BLOCKS, 2, 64, 1024), BF16),
        pltpu.VMEM((BLOCKS, 64, 1024), BF16),
        pltpu.VMEM((BLOCKS, 64, 1024), BF16),
        pltpu.VMEM((BLOCKS, 128, 1024), BF16),
        pltpu.VMEM((BLOCKS, 64, 1024), BF16),
        pltpu.VMEM((len(SHARED), 2, 2, 64, 1024), BF16),
        pltpu.VMEM((8, 16, 128), F32),
        pltpu.VMEM((8, 16, 128), F32),
        pltpu.VMEM((16, 128), F32),
        pltpu.VMEM((4, 16, 128), F32),
        pltpu.VMEM((16, 128), F32),
        dma((10, len(PIECES))),
        dma((10, len(PIECES))),
        dma((len(PIECES),)),
        dma((11,)),
        dma((11,)),
        dma((7,)),
        dma((7, 4)),
        dma((12,)),
        dma((4,)),
        dma((7,)),
        dma((7,)),
        dma((3,)),
        dma((3,)),
        dma((2,)),
        dma((len(SHARED), 2)),
        dma((len(SHARED), 2)),
    ]
    return pl.pallas_call(
        backward_kernel,
        out_shape=outs,
        in_specs=[pl.BlockSpec(memory_space=pltpu.SMEM)] + [anyspace] * len(saved),
        out_specs=[anyspace] * len(outs),
        scratch_shapes=scratch,
        name="backward",
        cost_estimate=pl.CostEstimate(flops=4 * 512 * 12582912, bytes_accessed=60 * MIB, transcendentals=4 * MIB),
        compiler_params=pltpu.CompilerParams(
            collective_id=1, has_side_effects=True, vmem_limit_bytes=60 * MIB
        ),
    )(lengths, *saved)


def finish_kernel(
    layer_in, token_in, q_in, o_in, u_in, d_in, small,
    layer_out, token_out, q_out, o_out, u_out, d_out, biases_out, up_bias_out, gains_out,
    q_low, o_low, u_low, d_low, layer_v, token_v, small_v, q, o, u, d, sem,
):
    sources = (d_in, u_in, q_in, o_in, token_in, layer_in, small)
    lows, wides = (d_low, u_low, q_low, o_low, token_v, layer_v, small_v), (d, u, q, o, token_v, layer_v)
    results = (d_out, u_out, q_out, o_out, token_out, layer_out)
    ins = [pltpu.make_async_copy(a, b, sem.at[i]) for i, (a, b) in enumerate(zip(sources, lows))]
    outs = [pltpu.make_async_copy(a, b, sem.at[7 + i]) for i, (a, b) in enumerate(zip(wides, results))]
    for c in ins:
        c.start()
    for a, b, c_in, c_out in zip(lows, wides, ins, outs):
        c_in.wait()
        if a is not b:
            b[...] = a[...].astype(F32)
        c_out.start()
    ins[-1].wait()
    biases_out[...] = small_v[0:6]
    gains_out[...] = small_v[6:8]
    for i in range(4):
        up_bias_out[i * 128 : (i + 1) * 128] = small_v[8 + i]
    for c in outs:
        c.wait()


def finish_call(layer_out, token_grad, weight_grads, small):
    anyspace = pl.BlockSpec(memory_space=pl.ANY)
    vmem = pl.BlockSpec(memory_space=pltpu.VMEM)
    shape = jax.ShapeDtypeStruct
    wide = [shape(g.shape, F32) for g in weight_grads]
    outs = [
        shape(layer_out.shape, BF16), shape(token_grad.shape, F32), *wide,
        shape((6, 128), F32), shape((512,), F32), shape((2, 128), F32),
    ]
    return pl.pallas_call(
        finish_kernel,
        out_shape=outs,
        in_specs=[anyspace] * 7,
        out_specs=[anyspace] * 6 + [vmem] * 3,
        scratch_shapes=[pltpu.VMEM(g.shape, BF16) for g in weight_grads]
        + [pltpu.VMEM(g.shape, g.dtype) for g in (layer_out, token_grad, small)]
        + [pltpu.VMEM(g.shape, F32) for g in weight_grads]
        + [pltpu.SemaphoreType.DMA((13,))],
        name="finish",
        compiler_params=pltpu.CompilerParams(vmem_limit_bytes=60 * MIB),
    )(layer_out, token_grad, *weight_grads, small)


def plane(
    tokens,
    lengths,
    cotangent,
    qkv_weight,
    out_weight,
    up_weight,
    down_weight,
    biases,
    up_bias,
    gains,
):
    layer_out, *saved = forward_call(
        tokens, lengths, cotangent, qkv_weight, out_weight, up_weight, down_weight, biases, up_bias, gains
    )
    token_grad, *weight_grads, small = backward_call(lengths, saved)
    return tuple(finish_call(layer_out, token_grad, weight_grads, small))


def solution(mesh):
    step = plane if dict(mesh.shape) == {"fsdp": 8, "rep": 4} else portable
    both = ("fsdp", "rep")
    in_specs = (
        P(both, None),
        P(both),
        P(both, None),
        P("fsdp", None),
        P("fsdp", None),
        P("fsdp", None),
        P("fsdp", None),
        P(None, "fsdp"),
        P("fsdp"),
        P(None, "fsdp"),
    )
    out_specs = (
        P(both, None),
        P(both, None),
        P("fsdp", None),
        P("fsdp", None),
        P("fsdp", None),
        P("fsdp", None),
        P(None, "fsdp"),
        P("fsdp"),
        P(None, "fsdp"),
    )
    return jax.shard_map(
        step, mesh=mesh, in_specs=in_specs, out_specs=out_specs, check_vma=False
    )
```

```python
import math

import jax
import jax.numpy as jnp
from jax import lax
from jax.experimental import pallas as pl
from jax.experimental.pallas import tpu as pltpu
from jax.sharding import PartitionSpec as P

HEAD_SIZE = 64


def matmul(left_side, right_side):
    return jnp.dot(left_side, right_side, preferred_element_type=jnp.float32)


def transposed_left(left_side, right_side):
    return lax.dot_general(
        left_side, right_side, (((0,), (0,)), ((), ())), preferred_element_type=jnp.float32
    )


def transposed_right(left_side, right_side):
    return lax.dot_general(
        left_side, right_side, (((1,), (1,)), ((), ())), preferred_element_type=jnp.float32
    )


def column_sum(values):
    return jnp.sum(values.astype(jnp.float32), axis=0)


def row_mean(values):
    return jnp.mean(values, axis=-1, keepdims=True)


def normalize(hidden):
    center = hidden - row_mean(hidden)
    inverse = lax.rsqrt(row_mean(center * center) + 1e-05)
    return center * inverse, inverse


def norm_back(grad, norm, inverse, gain):
    scaled = grad * gain
    return inverse * (scaled - row_mean(scaled) - norm * row_mean(scaled * norm))


def low(values):
    return values.astype(jnp.bfloat16)


def gather_small(biases, up_bias, gains):
    width, up_width = biases.shape[1], up_bias.shape[0]
    packed = jnp.concatenate([biases.reshape(-1), gains.reshape(-1), up_bias])
    everyone = lax.all_gather(packed, "fsdp", axis=0, tiled=False).astype(jnp.float32)
    rows = everyone[:, : 8 * width].reshape(-1, 8, width).transpose(1, 0, 2).reshape(8, -1)
    return rows[:6], everyone[:, 8 * width : 8 * width + up_width].reshape(-1), rows[6:]


def reduce_weight(grad):
    shard = lax.psum_scatter(low(grad), "fsdp", scatter_dimension=0, tiled=True)
    return lax.psum(shard, "rep").astype(jnp.float32)


def portable(
    tokens,
    lengths,
    cotangent,
    qkv_weight,
    out_weight,
    up_weight,
    down_weight,
    biases,
    up_bias,
    gains,
):
    slots = lengths.shape[0]
    rows, width = tokens.shape
    seq = rows // slots
    heads = width // HEAD_SIZE
    scale = 1.0 / math.sqrt(HEAD_SIZE)
    w_qkv = lax.all_gather(qkv_weight, "fsdp", axis=0, tiled=True)
    w_out = lax.all_gather(out_weight, "fsdp", axis=0, tiled=True)
    w_up = lax.all_gather(up_weight, "fsdp", axis=0, tiled=True)
    w_down = lax.all_gather(down_weight, "fsdp", axis=0, tiled=True)
    bias_rows, bias_up, gain_rows = gather_small(biases, up_bias, gains)

    def split(values):
        return values.reshape(slots, seq, heads, HEAD_SIZE)

    def join(values):
        return values.reshape(rows, width)

    sums = matmul(tokens, w_qkv)
    query = split(low(sums[:, :width] + bias_rows[0]))
    key = split(low(sums[:, width : 2 * width]))
    value = split(low(sums[:, 2 * width :] + bias_rows[1]))
    live = jnp.arange(seq)[None, :] < lengths[:, None]
    scores = scale * jnp.einsum(
        "bshd,bthd->bhst", query, key, preferred_element_type=jnp.float32
    )
    scores = jnp.where(live[:, None, None, :], scores, -1e30)
    exps = jnp.exp(scores - jnp.max(scores, axis=-1, keepdims=True))
    probs = exps / jnp.sum(exps, axis=-1, keepdims=True)
    probs_low = low(probs)
    mixed = low(
        join(jnp.einsum("bhst,bthd->bshd", probs_low, value, preferred_element_type=jnp.float32))
    )
    first, first_inverse = normalize(
        tokens.astype(jnp.float32) + matmul(mixed, w_out) + bias_rows[2]
    )
    first_norm = first * gain_rows[0] + bias_rows[3]
    first_low = low(first_norm)
    inner = matmul(first_low, w_up) + bias_up
    cumulative = 0.5 * (1.0 + lax.erf(inner * math.sqrt(0.5)))
    act_low = low(inner * cumulative)
    slope = low(cumulative + inner * jnp.exp(-0.5 * inner * inner) / math.sqrt(2.0 * math.pi))
    second, second_inverse = normalize(first_norm + matmul(act_low, w_down) + bias_rows[4])
    layer_out = low(second * gain_rows[1] + bias_rows[5])

    grad_out = cotangent * live.reshape(rows, 1).astype(jnp.float32)
    grad_h2 = norm_back(grad_out, second, second_inverse, gain_rows[1])
    grad_branch = low(grad_h2)
    down_grad = reduce_weight(transposed_left(act_low, grad_branch))
    grad_inner = low(transposed_right(grad_branch, w_down) * slope)
    up_grad = reduce_weight(transposed_left(first_low, grad_inner))
    grad_first = grad_h2 + transposed_right(grad_inner, w_up)
    grad_h1 = norm_back(grad_first, first, first_inverse, gain_rows[0])
    grad_attn = low(grad_h1)
    out_grad = reduce_weight(transposed_left(mixed, grad_attn))
    grad_mixed = split(low(transposed_right(grad_attn, w_out)))
    grad_probs = jnp.einsum(
        "bshd,bthd->bhst", grad_mixed, value, preferred_element_type=jnp.float32
    )
    shared = jnp.sum(probs * grad_probs, axis=-1, keepdims=True)
    grad_scores = low(probs * (grad_probs - shared))
    grad_query = scale * jnp.einsum(
        "bhst,bthd->bshd", grad_scores, key, preferred_element_type=jnp.float32
    )
    grad_key = scale * jnp.einsum(
        "bhst,bshd->bthd", grad_scores, query, preferred_element_type=jnp.float32
    )
    grad_value = jnp.einsum(
        "bhst,bshd->bthd", probs_low, grad_mixed, preferred_element_type=jnp.float32
    )
    grad_qkv = jnp.concatenate(
        [join(low(grad_query)), join(low(grad_key)), join(low(grad_value))], axis=1
    )
    qkv_grad = reduce_weight(transposed_left(tokens, grad_qkv))
    token_grad = grad_h1 + transposed_right(grad_qkv, w_qkv)
    small = jnp.stack(
        [
            column_sum(grad_qkv[:, :width]),
            column_sum(grad_qkv[:, 2 * width :]),
            column_sum(grad_attn),
            column_sum(grad_first),
            column_sum(grad_branch),
            column_sum(grad_out),
            column_sum(grad_first * first),
            column_sum(grad_out * second),
        ]
    )
    owner = lax.axis_index("fsdp")
    small, up_sum = lax.psum((small, column_sum(grad_inner)), ("fsdp", "rep"))
    own, own_up = biases.shape[1], up_bias.shape[0]
    small = lax.dynamic_slice(small, (0, owner * own), (8, own))
    up_bias_grad = lax.dynamic_slice(up_sum, (owner * own_up,), (own_up,))
    return (
        layer_out,
        token_grad,
        qkv_grad,
        out_grad,
        up_grad,
        down_grad,
        small[:6],
        up_bias_grad,
        small[6:],
    )


MESH = pl.DeviceIdType.MESH
F32 = jnp.float32
BF16 = jnp.bfloat16
MIB = 1 << 20


def dot_nn(a, b):
    return lax.dot_general(a, b, (((1,), (0,)), ((), ())), preferred_element_type=F32)


def dot_nt(a, b):
    return lax.dot_general(a, b, (((1,), (1,)), ((), ())), preferred_element_type=F32)


def dot_tn(a, b):
    return lax.dot_general(a, b, (((0,), (0,)), ((), ())), preferred_element_type=F32)


class Place:
    def __init__(self):
        f, z = lax.axis_index("fsdp"), lax.axis_index("rep")
        self.f, self.z = f, z
        self.core = lax.rem(f, 2)
        self.x = lax.rem(lax.div(f, 2), 2)
        self.y = lax.div(f, 4)
        self.chip = lax.div(f, 2)
        self.fx = f + 2 - 4 * self.x
        self.fy = f + 4 - 8 * self.y
        self.fd = self.fx + 4 - 8 * self.y
        self.fs = f + 1 - 2 * self.core
        self.par = lax.rem(z, 2)
        self.zn = z + 1 - 2 * self.par

    def dev(self, f=None, z=None):
        return {"fsdp": self.f if f is None else f, "rep": self.z if z is None else z}


def remote(src, dst, send_sem, recv_sem, device):
    return pltpu.make_async_remote_copy(
        src_ref=src, dst_ref=dst, send_sem=send_sem, recv_sem=recv_sem,
        device_id=device, device_id_type=MESH,
    )


UNITS = (
    ("q", 0, 32, 0),
    ("q", 32, 32, 0),
    ("q", 64, 32, 0),
    ("q", 96, 32, 0),
    ("o", 0, 128, 0),
    ("u", 0, 64, 0),
    ("u", 64, 64, 0),
    ("d", 0, 128, 0),
    ("d", 128, 128, 0),
    ("d", 256, 128, 16),
    ("d", 384, 128, 16),
)
FORWARD_PLAN = (
    ("direct", 0), ("direct", 1), ("direct", 2), ("direct", 3), ("small", 0), ("fx", 0), ("fy", 0),
    ("direct", 4), ("fx", 1), ("fy", 1), ("fx", 2), ("fy", 2), ("r2", 0), ("fx", 3), ("fy", 3), ("r3", 0),
    ("r5", 0), ("r4", 0), ("r2", 1), ("r3", 1), ("direct", 5), ("fx", 4), ("fy", 4), ("r2", 2), ("r5", 1),
    ("r4", 1), ("r3", 2), ("r5", 2), ("r4", 2), ("r2", 3), ("r5", 3), ("r4", 3), ("r3", 3), ("direct", 6),
    ("done", 0), ("done", 1), ("done", 2), ("done", 3), ("qkv", 0), ("fx", 5), ("fy", 5), ("r2", 4),
    ("r3", 4), ("at", 0, 1), ("r4", 4), ("r5", 4), ("at", 1, 4), ("direct", 7), ("at", 4, 6), ("fx", 6),
    ("fy", 6), ("at", 6, 8), ("r2", 5), ("at", 8, 12), ("r4", 5), ("r5", 5), ("direct", 8), ("at", 12, 13),
    ("r3", 5), ("at", 13, 14), ("fx", 7), ("fy", 7), ("at", 14, 16), ("done", 4), ("out", 0), ("r2", 6),
    ("r4", 6), ("r5", 6), ("direct", 9), ("fx", 8), ("fy", 8), ("r3", 6), ("direct", 10), ("r5", 7),
    ("r4", 7), ("done", 5), ("done", 6), ("up", 0, 1), ("r2", 7), ("up", 1, 2), ("fx", 9), ("fy", 9),
    ("up", 2, 3), ("r3", 7), ("up", 3, 4), ("r4", 8), ("r5", 8), ("up", 4, 5), ("r2", 8), ("up", 5, 7),
    ("fx", 10), ("fy", 10), ("r3", 8), ("up", 7, 8), ("r2", 9), ("r4", 9), ("r5", 9), ("done", 7), ("dn", 7),
    ("r3", 9), ("done", 8), ("dn", 8), ("r2", 10), ("r4", 10), ("r5", 10), ("done", 9), ("tidy", 0),
    ("dn", 9), ("r3", 10), ("done", 10), ("dn", 10), ("last", 0),
)
KINDS = 13


class Gather:
    def __init__(self, place, unit, shard, full, base, rows, extra, send, recv, local):
        self.p, self.unit, self.shard, self.full = place, unit, shard, full
        self.base, self.rows, self.size = base, rows, shard.shape[0]
        self.send_sem, self.recv_sem, self.local_sem = send, recv, local
        p, half = place, rows // 2
        one, two = half * p.par, half * (1 - p.par)
        wide, rest = half + extra, half - extra
        near_x, near_y = rest * p.par, rest * (1 - p.par)
        far_x, far_y = wide * (1 - p.par), wide * p.par
        to_x, to_y, to_s, to_z = p.dev(f=p.fx), p.dev(f=p.fy), p.dev(f=p.fs), p.dev(z=p.zn)
        sx, sy, sd = (g + 1 - 2 * p.core for g in (p.fx, p.fy, p.fd))
        self.table = (
            ((p.fx, near_x), (p.f, near_x), wide, to_x),
            ((p.fy, near_y), (p.f, near_y), wide, to_y),
            ((p.fx, far_x), (p.fx, far_y), rest, to_z),
            ((p.fy, far_y), (p.fy, far_x), rest, to_z),
            ((p.fd, one), (p.fx, one), half, to_y),
            ((p.fd, two), (p.fy, two), half, to_x),
            ((p.fs, 0), (p.f, 0), rows, to_s),
            ((sx, near_x), (p.fx, near_x), wide, to_s),
            ((sy, near_y), (p.fy, near_y), wide, to_s),
            ((sx, far_x), (p.fx, far_x), rest, to_s),
            ((sy, far_y), (p.fy, far_y), rest, to_s),
            ((sd, one), (p.fd, one), half, to_s),
            ((sd, two), (p.fd, two), half, to_s),
        )

    def at(self, owner, lo, n):
        return self.full.at[pl.ds(pl.multiple_of(owner * self.size + self.base + lo, 16), n)]

    def copy(self, kind, sending):
        received, sent, n, device = self.table[kind]
        owner, lo = sent if sending else received
        here = self.at(owner, lo, n)
        src = self.shard.at[pl.ds(pl.multiple_of(self.base + lo, 16), n)] if kind in (0, 1, 6) else here
        return remote(src, here, self.send_sem.at[self.unit, kind], self.recv_sem.at[self.unit, kind], device)

    def start(self, *kinds):
        for kind in kinds:
            self.copy(kind, True).start()

    def got(self, *kinds):
        for kind in kinds:
            self.copy(kind, False).wait_recv()

    def sent(self):
        for kind in range(KINDS):
            self.copy(kind, True).wait_send()

    def own(self):
        src = self.shard.at[pl.ds(self.base, self.rows)]
        return pltpu.make_async_copy(src, self.at(self.p.f, 0, self.rows), self.local_sem.at[self.unit])

    def direct(self):
        self.start(0, 1, 6)
        self.own().start()

    def pass_on(self, arrived, *kinds):
        self.got(arrived)
        self.start(*kinds)

    def done(self):
        self.got(6, 7, 8, 9, 10, 11, 12)
        self.own().wait()


def forward_kernel(
    lengths, biases, up_bias, gains, tokens, cot, sh_q, sh_o, sh_u, sh_d,
    layer_out, wq_out, wo_out, wu_out, wd_out, qkv_out, slope_out, act_pair, first_pair, mixed_pair,
    tok_pair, branch_pair, norm_out, inv_out, grad_out_ref, params_out, sums_out,
    x, wq, wo, wu, wd, qkv, mixed, norm, first_low, act, slope, acc, cot_v, gh2, out_v, gb, smalls, params,
    inv_v, sums, up_rows, small,
    ag_send, ag_recv, ag_local, sm_send, sm_recv, io, pair_send, pair_recv, pair_local, wd_sem, half_sem,
):
    p = Place()
    rows, width = x.shape
    slots = lengths.shape[0]
    seq = rows // slots
    others = [lax.rem(p.f + k, 8) for k in range(1, 8)]
    barrier = pltpu.get_barrier_semaphore()
    for g in others:
        pl.semaphore_signal(barrier, inc=1, device_id=p.dev(f=g), device_id_type=MESH)
    pl.semaphore_signal(barrier, inc=1, device_id=p.dev(z=p.zn), device_id_type=MESH)
    loads = [
        pltpu.make_async_copy(tokens, x, io.at[0]),
        pltpu.make_async_copy(cot, cot_v, io.at[1]),
    ]
    for c in loads:
        c.start()
    small[...] = jnp.zeros_like(small)
    small[0:6] = biases[...].astype(F32)
    small[6:8] = gains[...].astype(F32)
    for i in range(4):
        small[8 + i] = up_bias[i * 128 : (i + 1) * 128].astype(F32)
    smalls[p.f] = small[...]
    pl.semaphore_wait(barrier, 8)

    def small_copy(k, owner, device):
        return remote(small, smalls.at[owner], sm_send.at[k], sm_recv.at[k], device)

    for k, g in enumerate(others):
        small_copy(k, p.f, p.dev(f=g)).start()

    weights = {"q": (sh_q, wq), "o": (sh_o, wo), "u": (sh_u, wu), "d": (sh_d, wd)}
    parts = [Gather(p, i, *weights[n], *piece, ag_send, ag_recv, ag_local) for i, (n, *piece) in enumerate(UNITS)]

    mine = pl.ds(pl.multiple_of(p.core * rows, rows), rows)

    def pair(index, chip, src, dst, cols):
        own = pl.ds(pl.multiple_of((2 * chip + p.core) * cols, cols), cols)
        other = pl.ds(pl.multiple_of((2 * chip + 1 - p.core) * cols, cols), cols)
        here = dst.at[mine, pl.ds(chip * cols, cols)]
        return (
            pltpu.make_async_copy(src.at[:, own], here, pair_local.at[index, chip]),
            remote(src.at[:, other], here, pair_send.at[index, chip], pair_recv.at[index, chip], p.dev(f=p.fs)),
        )

    pairs = []

    def start_pair(index, src, dst, cols, chips=range(4)):
        for chip in chips:
            for c in pair(index, chip, src, dst, cols):
                c.start()
            pairs.append((index, chip, src, dst, cols))

    stores = []

    def store(src, dst, sem):
        stores.append(pltpu.make_async_copy(src, dst, sem))
        stores[-1].start()

    def small_params(_):
        loads[0].wait()
        start_pair(0, x, tok_pair, 128)
        for k in range(7):
            back = lax.rem(p.f + 7 - k, 8)
            small_copy(k, back, p.dev(f=back)).wait_recv()
        for g in range(8):
            part = smalls[g]
            params[:, g * 128 : (g + 1) * 128] = part
            for j in range(4):
                up_rows[g : g + 1, j * 128 : (j + 1) * 128] = part[8 + j : 9 + j]

    def project(_):
        store(wq, wq_out, io.at[2])
        for j in range(3):
            part = dot_nn(x[...], wq[:, j * width : (j + 1) * width])
            if j == 0:
                part = part + params[0:1]
            if j == 2:
                part = part + params[1:2]
            qkv[:, j * width : (j + 1) * width] = part.astype(BF16)
        store(qkv, qkv_out, io.at[3])

    left = lax.broadcasted_iota(jnp.int32, (seq, 128), 1) < HEAD_SIZE
    key_row = lax.broadcasted_iota(jnp.int32, (seq, seq), 0)

    def attend(step, carry):
        slot, pair_of = lax.div(step, 8), lax.rem(step, 8)
        at_rows = pl.ds(pl.multiple_of(slot * seq, seq), seq)
        col = pl.multiple_of(pair_of * 128, 128)
        q = qkv[at_rows, pl.ds(col, 128)]
        k = qkv[at_rows, pl.ds(pl.multiple_of(width + col, 128), 128)]
        v = qkv[at_rows, pl.ds(pl.multiple_of(2 * width + col, 128), 128)]
        dead = key_row >= lengths[slot]
        outs = []
        for head in range(2):
            k_head = jnp.where(left if head == 0 else ~left, k, jnp.zeros_like(k))
            scores = dot_nt(k_head, q) * (1.0 / math.sqrt(HEAD_SIZE))
            scores = jnp.where(dead, -1e30, scores)
            exps = jnp.exp(scores - jnp.max(scores, axis=0, keepdims=True))
            probs = exps * (1.0 / jnp.sum(exps, axis=0, keepdims=True))
            outs.append(dot_tn(probs.astype(BF16), v))
        mixed[at_rows, pl.ds(col, 128)] = jnp.where(left, outs[0], outs[1]).astype(BF16)
        return carry

    steps = 8 * slots

    def attention(first, last):
        lax.fori_loop(first * steps // 16, last * steps // 16, attend, 0)
        if last == 16:
            start_pair(1, mixed, mixed_pair, 128)

    def first_norm(_):
        store(wo, wo_out, io.at[4])
        hidden = x[...].astype(F32) + dot_nn(mixed[...], wo[...]) + params[2:3]
        center = hidden - row_mean(hidden)
        inverse = lax.rsqrt(row_mean(center * center) + 1e-05)
        norm[...] = center * inverse
        inv_v[...] = jnp.broadcast_to(inverse, inv_v.shape)
        shifted = norm[...] * params[6:7] + params[3:4]
        first_low[...] = shifted.astype(BF16)
        acc[...] = shifted + params[4:5]
        start_pair(2, first_low, first_pair, 128)
        store(norm, norm_out, io.at[5])
        store(inv_v, inv_out, io.at[6])

    def up_step(j, carry):
        cols = pl.ds(pl.multiple_of(j * 512, 512), 512)
        inner = dot_nn(first_low[...], wu[:, cols]) + up_rows[pl.ds(j, 1), :]
        phi = 0.5 * (1.0 + lax.erf(inner * math.sqrt(0.5)))
        act[:, cols] = (inner * phi).astype(BF16)
        density = jnp.exp(-0.5 * inner * inner) * (1.0 / math.sqrt(2.0 * math.pi))
        slope[:, cols] = (phi + inner * density).astype(BF16)
        return carry

    def up(first, last):
        if first == 0:
            store(wu, wu_out, io.at[7])
        lax.fori_loop(first, last, up_step, 0)
        if last == 4:
            start_pair(3, act, act_pair, 512, range(2))
        if last == 8:
            start_pair(3, act, act_pair, 512, range(2, 4))
            store(slope, slope_out, io.at[8])

    def down(u):
        _, lo, n, _ = UNITS[u]
        for g in range(8):
            at = pl.ds(g * 512 + lo, n)
            store(wd.at[at], wd_out.at[at], wd_sem.at[g, u])
        for j in range(0, 8, 1024 // n):
            cols = [slice(512 * g + lo, 512 * g + lo + n) for g in range(j, j + 1024 // n)]
            left = jnp.concatenate([act[:, c] for c in cols], axis=1)
            right = jnp.concatenate([wd[c, :] for c in cols], axis=0)
            acc[...] += dot_nn(left, right)

    tidied = []

    def tidy(_):
        for k, g in enumerate(others):
            small_copy(k, p.f, p.dev(f=g)).wait_send()
        for part in parts:
            if UNITS[part.unit][0] != "d":
                part.sent()
        count = len(stores) - 8
        for c in stores[:count]:
            c.wait()
        for args in pairs[:12]:
            for c in pair(*args):
                c.wait()
        tidied.append(count)

    def second_norm(_):
        loads[1].wait()
        swap = []
        totals = []
        for s in range(slots):
            at = pl.ds(s * seq, seq)
            hidden = acc[at]
            center = hidden - row_mean(hidden)
            inverse = lax.rsqrt(row_mean(center * center) + 1e-05)
            second = center * inverse
            row_at = lax.broadcasted_iota(jnp.int32, (seq, 1), 0)
            e = cot_v[at] * (row_at < lengths[s]).astype(F32)
            scaled = e * params[7:8]
            gh2[at] = inverse * (scaled - row_mean(scaled) - second * row_mean(scaled * second))
            gb[at] = gh2[at].astype(BF16)
            src = gb.at[at]
            dst = branch_pair.at[pl.ds(pl.multiple_of(p.core * rows + s * seq, seq), seq)]
            swap.append(remote(src, dst, pair_send.at[4, s], pair_recv.at[4, s], p.dev(f=p.fs)))
            swap.append(pltpu.make_async_copy(src, dst, pair_local.at[4, s]))
            for c in swap[-2:]:
                c.start()
            store(gh2.at[at], grad_out_ref.at[at], half_sem.at[0, s])
            out_v[at] = (second * params[7:8] + params[5:6]).astype(BF16)
            store(out_v.at[at], layer_out.at[at], half_sem.at[1, s])
            totals.append([jnp.sum(t, axis=0, keepdims=True) for t in (e * second, e, gb[at].astype(F32))])
        store(params, params_out, io.at[12])
        sums[...] = jnp.zeros_like(sums)
        for i in range(3):
            sums[i : i + 1] = sum(t[i] for t in totals)
        store(sums, sums_out, io.at[13])
        for part in parts:
            if UNITS[part.unit][0] == "d":
                part.sent()
        for args in pairs[12:]:
            for c in pair(*args):
                c.wait()
        for c in stores[tidied[0] :]:
            c.wait()
        for c in swap:
            c.wait()

    work = {
        "small": small_params, "qkv": project, "at": attention, "out": first_norm, "up": up, "dn": down,
        "tidy": tidy, "last": second_norm,
        "direct": lambda u: parts[u].direct(), "done": lambda u: parts[u].done(),
        "fx": lambda u: parts[u].pass_on(0, 4, 2, 7), "fy": lambda u: parts[u].pass_on(1, 5, 3, 8),
        "r2": lambda u: parts[u].pass_on(2, 9), "r3": lambda u: parts[u].pass_on(3, 10),
        "r4": lambda u: parts[u].pass_on(4, 11), "r5": lambda u: parts[u].pass_on(5, 12),
    }
    for name, *which in FORWARD_PLAN:
        work[name](*which)


def forward_call(tokens, lengths, cotangent, qkv_w, out_w, up_w, down_w, biases, up_bias, gains):
    rows, width = tokens.shape
    ff = up_w.shape[1]
    anyspace = pl.BlockSpec(memory_space=pl.ANY)
    shape = jax.ShapeDtypeStruct
    outs = [
        shape((rows, width), BF16),
        shape((width, 3 * width), BF16),
        shape((width, width), BF16),
        shape((width, ff), BF16),
        shape((ff, width), BF16),
        shape((rows, 3 * width), BF16),
        shape((rows, ff), BF16),
        shape((2 * rows, ff // 2), BF16),
        shape((2 * rows, width // 2), BF16),
        shape((2 * rows, width // 2), BF16),
        shape((2 * rows, width // 2), BF16),
        shape((2 * rows, width), BF16),
        shape((rows, width), F32),
        shape((rows, 128), F32),
        shape((rows, width), F32),
        shape((16, width), F32),
        shape((8, width), F32),
    ]
    dma = pltpu.SemaphoreType.DMA
    scratch = [
        pltpu.VMEM((rows, width), BF16),
        pltpu.VMEM((width, 3 * width), BF16),
        pltpu.VMEM((width, width), BF16),
        pltpu.VMEM((width, ff), BF16),
        pltpu.VMEM((ff, width), BF16),
        pltpu.VMEM((rows, 3 * width), BF16),
        pltpu.VMEM((rows, width), BF16),
        pltpu.VMEM((rows, width), F32),
        pltpu.VMEM((rows, width), BF16),
        pltpu.VMEM((rows, ff), BF16),
        pltpu.VMEM((rows, ff), BF16),
        pltpu.VMEM((rows, width), F32),
        pltpu.VMEM((rows, width), F32),
        pltpu.VMEM((rows, width), F32),
        pltpu.VMEM((rows, width), BF16),
        pltpu.VMEM((rows, width), BF16),
        pltpu.VMEM((8, 16, 128), F32),
        pltpu.VMEM((16, width), F32),
        pltpu.VMEM((rows, 128), F32),
        pltpu.VMEM((8, width), F32),
        pltpu.VMEM((8, ff // 8), F32),
        pltpu.VMEM((16, 128), F32),
        dma((len(UNITS), KINDS)),
        dma((len(UNITS), KINDS)),
        dma((len(UNITS),)),
        dma((7,)),
        dma((7,)),
        dma((14,)),
        dma((5, 4)),
        dma((5, 4)),
        dma((5, 4)),
        dma((8, len(UNITS))),
        dma((2, 2)),
    ]
    return pl.pallas_call(
        forward_kernel,
        out_shape=outs,
        in_specs=[pl.BlockSpec(memory_space=pltpu.SMEM)] + [pl.BlockSpec(memory_space=pltpu.VMEM)] * 3 + [anyspace] * 6,
        out_specs=[anyspace] * len(outs),
        scratch_shapes=scratch,
        name="forward",
        cost_estimate=pl.CostEstimate(flops=2 * 512 * 12582912, bytes_accessed=60 * MIB, transcendentals=4 * MIB),
        compiler_params=pltpu.CompilerParams(
            collective_id=0, has_side_effects=True, vmem_limit_bytes=60 * MIB
        ),
    )(lengths, biases, up_bias, gains, tokens, cotangent, qkv_w, out_w, up_w, down_w)


BLOCKS = 12
FAR = 2
SHARED = (1, 2)
PIECES = (
    (0, 0, 64),
    (3, 0, 64),
    (2, None, 32),
    (4, 0, 64),
    (1, None, 32),
    (5, 0, 64),
    (7, 0, 64),
    (6, 0, 64),
    (8, 0, 64),
    (9, 0, 32),
    (9, 32, 32),
    (10, 0, 32),
    (10, 32, 32),
    (11, 0, 16),
    (11, 16, 16),
    (11, 32, 16),
    (11, 48, 16),
)
PLAN = (
    ("start", 0), ("down", 0), ("begin", 0), ("down", 1), ("swap", 1, 0), ("swap", 1, 1), ("down", 2),
    ("down", 3), ("swap", 2, 0), ("begin", 1), ("g", 0), ("h", 0), ("second", 0), ("g", 1), ("swap", 2, 1),
    ("h", 1), ("second", 1), ("u", 0), ("begin", 4), ("along", 0), ("begin", 3), ("g", 2), ("along", 1),
    ("h", 2), ("u", 1), ("second", 4), ("begin", 5), ("g", 3), ("h", 3), ("u", 2), ("second", 3),
    ("along", 4), ("inward", 0), ("norm", 0), ("begin", 2), ("u", 3), ("second", 5), ("hand", 0),
    ("inward", 1), ("gm", 0), ("begin", 6), ("o", 0), ("along", 3), ("inward", 4), ("at", 0, 1),
    ("second", 2), ("pass", 0), ("at", 1, 3), ("hand", 1), ("inward", 3), ("along", 5), ("at", 3, 4),
    ("begin", 7), ("at", 4, 5), ("hand", 4), ("at", 5, 7), ("second", 6), ("pass", 1), ("inward", 5),
    ("at", 7, 8), ("along", 2), ("hand", 3), ("at", 8, 10), ("inward", 2), ("pass", 4), ("begin", 8),
    ("at", 10, 12), ("second", 7), ("hand", 5), ("at", 12, 14), ("pass", 3), ("along", 6), ("close", 0),
    ("at", 14, 16), ("hand", 2), ("q", 0), ("inward", 6), ("begin", 9), ("pass", 5), ("q", 1), ("second", 8),
    ("q", 2), ("pass", 2), ("along", 7), ("begin", 10), ("close", 1), ("small", 0), ("hand", 6),
    ("begin", 11), ("t", 0), ("second", 9), ("inward", 7), ("t", 1), ("along", 8), ("close", 4), ("t", 2),
    ("pass", 6), ("begin", 12), ("level", 1), ("inward", 8), ("second", 10), ("hand", 7), ("begin", 13),
    ("close", 3), ("second", 11), ("along", 9), ("begin", 14), ("begin", 15), ("second", 12), ("hand", 8),
    ("inward", 9), ("along", 10), ("close", 5), ("begin", 16), ("second", 13), ("pass", 7), ("along", 11),
    ("close", 2), ("inward", 10), ("pass", 8), ("second", 14), ("hand", 9), ("inward", 11), ("hand", 10),
    ("second", 15), ("along", 12), ("second", 16), ("along", 13), ("along", 14), ("pass", 9), ("close", 6),
    ("inward", 12), ("hand", 11), ("along", 15), ("along", 16), ("pass", 10), ("inward", 13), ("inward", 14),
    ("hand", 12), ("inward", 15), ("pass", 11), ("hand", 13), ("hand", 14), ("inward", 16), ("pass", 12),
    ("hand", 15), ("level", 2), ("pass", 13), ("close", 7), ("pass", 14), ("hand", 16), ("pass", 15),
    ("close", 8), ("pass", 16), ("close", 9), ("close", 10), ("close", 11), ("close", 12), ("close", 13),
    ("close", 14), ("close", 15), ("close", 16),
)
S1X, S1Y, S2X, S2Y, Z1G, Z1K, Z2, FM, FE, FF = range(10)


class Reduce:
    def __init__(self, place, prod, got_x, got_y, end_x, end_y, from_end, from_mid, swapped, out_at, send, recv, local, swap_send, swap_recv):
        self.p = place
        self.prod, self.got_x, self.got_y, self.end_x, self.end_y = prod, got_x, got_y, end_x, end_y
        self.from_end, self.from_mid, self.swapped, self.out_at = from_end, from_mid, swapped, out_at
        self.send, self.recv, self.local = send, recv, local
        self.swap_send, self.swap_recv = swap_send, swap_recv
        z = place.z
        self.mid = 1 + lax.div(z, 2)
        self.end = 3 * lax.div(z, 2)
        self.is_mid = z == self.mid
        self.is_end = z == self.end

    def rows(self, u, theirs=False):
        b, o, n = PIECES[u]
        if o is None:
            o = pl.multiple_of(32 * (1 - self.p.par if theirs else self.p.par), 32)
        return b, o, n

    def z_rows(self, u):
        b, o, n = PIECES[u]
        return (b, 0, 64) if o is None else (b, o, n)

    def keep(self, o, n):
        return pl.ds(pl.multiple_of(64 * (self.mid - 1) + o, 16), n)

    def give(self, o, n):
        return pl.ds(pl.multiple_of(64 * (2 - self.mid) + o, 16), n)

    def copy(self, kind, u, sending=True):
        p = self.p
        b, o, n = self.rows(u, theirs=kind in (Z1G, Z1K) and not sending)
        _, oz, nz = self.z_rows(u)
        x, y, xn, yn = p.x, p.y, 1 - p.x, 1 - p.y
        near, far = pl.ds(o, n), pl.ds(64 + o, n)
        keep, give = self.keep(oz, nz), self.give(oz, nz)
        to_mid, to_end, to_other = p.dev(z=self.mid), p.dev(z=self.end), p.dev(z=3 - self.mid)
        own = self.prod.at[b, y, x]
        if kind == S1X:
            src, dst, dev = self.prod.at[b, :, xn, near], self.got_x.at[b, :, near], p.dev(f=p.fx)
        elif kind == S1Y:
            src, dst, dev = self.prod.at[b, yn, :, far], self.got_y.at[b, :, near], p.dev(f=p.fy)
        elif kind == S2Y:
            src, dst, dev = self.prod.at[b, yn, x, near], self.end_y.at[b, near], p.dev(f=p.fy)
        elif kind == S2X:
            src, dst, dev = self.prod.at[b, y, xn, far], self.end_x.at[b, near], p.dev(f=p.fx)
        elif kind == Z1G:
            src, dst, dev = own.at[self.give(o, n)], self.from_end.at[b, self.give(o, n)], to_mid
        elif kind == Z1K:
            src, dst, dev = own.at[self.keep(o, n)], self.from_end.at[b, self.keep(o, n)], to_mid
        elif kind == Z2:
            src, dst, dev = own.at[give], self.from_mid.at[b, pl.ds(oz, nz)], to_other
        elif kind == FM:
            src, dst, dev = own.at[keep], self.out_at(b, keep if sending else give), to_other
        elif kind == FE:
            src, dst, dev = own.at[keep], self.out_at(b, keep), to_end
        elif u >= len(PIECES) - FAR:
            src, dst, dev = own.at[keep], self.out_at(b, keep if sending else give), p.dev(z=3 - self.end)
        else:
            src, dst, dev = self.out_at(b, give), self.out_at(b, give), to_end
        return remote(src, dst, self.send.at[kind, u], self.recv.at[kind, u], dev)

    def swap(self, b, half):
        i = SHARED.index(b)
        src = self.prod.at[b, :, :, pl.ds(pl.multiple_of(64 * half + 32 * (1 - self.p.par), 32), 32)]
        dst = self.swapped.at[i, :, :, pl.ds(32 * half, 32)]
        return remote(src, dst, self.swap_send.at[i, half], self.swap_recv.at[i, half], self.p.dev(z=self.p.zn))

    def swap_out(self, b, half):
        self.swap(b, half).start()

    def begin(self, u):
        b, o, n = self.rows(u)
        for half, kind in enumerate((S1X, S1Y)):
            if b in SHARED:
                at = pl.ds(pl.multiple_of(64 * half + o, 32), n)
                self.swap(b, half).wait()
                part = self.swapped[SHARED.index(b), :, :, 32 * half : 32 * half + 32]
                self.prod[b, :, :, at] = self.prod[b, :, :, at] + part
            self.copy(kind, u).start()

    def second(self, u):
        x, y = self.p.x, self.p.y
        b, o, n = self.rows(u)
        near, far = pl.ds(o, n), pl.ds(64 + o, n)
        self.copy(S1X, u).wait_recv()
        self.prod[b, :, x, near] = self.prod[b, :, x, near] + self.got_x[b, :, near]
        self.copy(S2Y, u).start()
        self.copy(S1Y, u).wait_recv()
        self.prod[b, y, :, far] = self.prod[b, y, :, far] + self.got_y[b, :, near]
        self.copy(S2X, u).start()

    def along(self, u):
        x, y = self.p.x, self.p.y
        b, o, n = self.rows(u)
        near, far = pl.ds(o, n), pl.ds(64 + o, n)
        self.copy(S2Y, u).wait_recv()
        self.prod[b, y, x, near] = self.prod[b, y, x, near] + self.end_y[b, near]
        self.copy(S2X, u).wait_recv()
        self.prod[b, y, x, far] = self.prod[b, y, x, far] + self.end_x[b, near]

        @pl.when(self.is_end)
        def _():
            self.copy(Z1G, u).start()
            self.copy(Z1K, u).start()

    def inward(self, u):
        x, y = self.p.x, self.p.y
        b, o, n = self.rows(u, theirs=True)

        @pl.when(self.is_mid)
        def _():
            give = self.give(o, n)
            self.copy(Z1G, u, False).wait_recv()
            if b in SHARED:
                self.prod[b, y, x, give] = self.from_end[b, give]
            else:
                self.prod[b, y, x, give] = self.prod[b, y, x, give] + self.from_end[b, give]
            self.copy(Z2, u).start()

    def write(self, u):
        b, o, n = self.z_rows(u)
        keep = self.keep(o, n)
        return pltpu.make_async_copy(
            self.prod.at[b, self.p.y, self.p.x, keep], self.out_at(b, keep), self.local.at[u]
        )

    def hand_out(self, u):
        x, y = self.p.x, self.p.y
        b, o, n = self.z_rows(u)

        @pl.when(self.is_mid)
        def _():
            keep = self.keep(o, n)
            self.copy(Z1K, u, False).wait_recv()
            if b in SHARED:
                part = self.keep(*self.rows(u, theirs=True)[1:])
                self.prod[b, y, x, part] = self.from_end[b, part]
            self.copy(Z2, u).wait_recv()
            total = self.prod[b, y, x, keep].astype(F32) + self.from_mid[b, o : o + n].astype(F32)
            if b not in SHARED:
                total = total + self.from_end[b, keep].astype(F32)
            self.prod[b, y, x, keep] = total.astype(BF16)
            if u >= len(PIECES) - FAR:
                self.copy(FF, u).start()
            self.copy(FM, u).start()
            self.copy(FE, u).start()
            self.write(u).start()

    def hand_on(self, u):
        @pl.when(self.is_mid)
        def _():
            self.copy(FM, u, False).wait_recv()
            if u < len(PIECES) - FAR:
                self.copy(FF, u).start()

    def close(self, u):
        for kind in (S1X, S1Y, S2X, S2Y):
            self.copy(kind, u).wait_send()

        @pl.when(self.is_end)
        def _():
            self.copy(Z1G, u).wait_send()
            self.copy(Z1K, u).wait_send()
            self.copy(FE, u).wait_recv()
            self.copy(FF, u, False).wait_recv()

        @pl.when(self.is_mid)
        def _():
            for kind in (Z2, FM, FE, FF):
                self.copy(kind, u).wait_send()
            self.write(u).wait()


def backward_kernel(
    lengths, wq, wo, wu, wd, qkv, slope, act_pair, first_pair, mixed_pair, tok_pair, branch_pair,
    norm_in, inv_in, gh2, params_in, sums_in,
    token_grad, out_q, out_o, out_u, out_d, small_out,
    lhs, wbuf, slope_v, branch, gi, gq, gm, gh, norm, inv, params, sums_v, upsum,
    prod, got_x, got_y, end_x, end_y, from_end, from_mid, swapped,
    s_send, s_got, s_total, s_all, s_out,
    rs_send, rs_recv, rs_local, pair_send, pair_recv, load_sem, lhs_sem, w_sem, slope_sem,
    sm_send, sm_recv, smz_send, smz_recv, store_sem, swap_send, swap_recv,
):
    p = Place()
    rows, width = gh.shape
    slots = lengths.shape[0]
    seq = rows // slots
    planes = [lax.rem(p.f + k, 8) for k in range(1, 8)]
    levels = [lax.rem(p.z + k, 4) for k in range(1, 4)]
    barrier = pltpu.get_barrier_semaphore()
    for g in planes:
        pl.semaphore_signal(barrier, inc=1, device_id=p.dev(f=g), device_id_type=MESH)
    for g in levels:
        pl.semaphore_signal(barrier, inc=1, device_id=p.dev(z=g), device_id_type=MESH)

    mine = pl.ds(pl.multiple_of(p.core * rows, rows), rows)

    def lhs_copies(i):
        if i < 4:
            return [
                pltpu.make_async_copy(
                    act_pair.at[:, pl.ds(chip * 512 + i * 128, 128)],
                    lhs.at[i % 2, :, pl.ds(chip * 128, 128)],
                    lhs_sem.at[i, chip],
                )
                for chip in range(4)
            ]
        src = (first_pair, mixed_pair, tok_pair)[i - 4]
        return [pltpu.make_async_copy(src, lhs.at[i % 2], lhs_sem.at[i, 0])]

    def w_copy(i):
        if i < 8:
            j = i // 2
            src = wu.at[:, pl.ds(j * 1024, 1024)] if i % 2 else wd.at[pl.ds(j * 1024, 1024)]
        elif i == 8:
            src = wo
        else:
            src = wq.at[:, pl.ds((i - 9) * 1024, 1024)]
        return pltpu.make_async_copy(src, wbuf.at[i % 2], w_sem.at[i])

    def slope_copy(j):
        return pltpu.make_async_copy(slope.at[:, pl.ds(j * 1024, 1024)], slope_v.at[j % 2], slope_sem.at[j])

    loads = [
        pltpu.make_async_copy(src, dst, load_sem.at[i])
        for i, (src, dst) in enumerate(
            (
                (branch_pair, branch), (gh2, gh), (qkv, gq.at[mine]), (norm_in, norm), (inv_in, inv),
                (params_in, params), (sums_in, sums_v),
            )
        )
    ]
    for c in lhs_copies(0):
        c.start()
    loads[0].start()

    def out_at(b, at):
        if b < 4:
            return out_d.at[pl.ds(128 * b, 128)].at[at]
        if b < 8:
            return out_u.at[at, pl.ds((b - 4) * 1024, 1024)]
        if b == 8:
            return out_o.at[at]
        return out_q.at[at, pl.ds((b - 9) * 1024, 1024)]

    red = Reduce(
        p, prod, got_x, got_y, end_x, end_y, from_end, from_mid, swapped, out_at, rs_send, rs_recv, rs_local,
        swap_send, swap_recv,
    )

    def produce(b, left, right):
        prod[b] = dot_tn(left, right).astype(BF16).reshape(2, 2, 128, 1024)

    def to_pair(index, ref, cols):
        here = ref.at[mine, cols]
        return remote(here, here, pair_send.at[index], pair_recv.at[index], p.dev(f=p.fs))

    def block_cols(j):
        return pl.ds(j * 1024, 1024)

    whole = pl.ds(0, 1024)
    ga = branch

    def start(_):
        for c in lhs_copies(0):
            c.wait()
        loads[0].wait()
        for c in lhs_copies(1):
            c.start()
        w_copy(0).start()
        slope_copy(0).start()
        for c in loads[1:]:
            c.start()

    def down(b):
        for c in lhs_copies(b) if b > 0 else ():
            c.wait()
        produce(b, lhs[b % 2], branch[...])
        for c in lhs_copies(b + 2):
            c.start()
        if b == 0:
            pl.semaphore_wait(barrier, 10)
        if b == 3:
            loads[1].wait()

    def inner_step(j):
        w_copy(2 * j).wait()
        w_copy(2 * j + 1).start()
        slope_copy(j).wait()
        if j < 3:
            slope_copy(j + 1).start()
        inner = (dot_nt(branch[mine], wbuf[0]) * slope_v[j % 2].astype(F32)).astype(BF16)
        gi[mine, j * 1024 : (j + 1) * 1024] = inner
        to_pair(j, gi, block_cols(j)).start()
        upsum[j : j + 1] = jnp.sum(inner.astype(F32), axis=0, keepdims=True)

    def hidden_step(j):
        w_copy(2 * j + 1).wait()
        w_copy(2 * j + 2).start()
        gh[...] += dot_nt(gi[mine, j * 1024 : (j + 1) * 1024], wbuf[1])
        if j == 0:
            for c in lhs_copies(4):
                c.wait()

    def up_block(j):
        to_pair(j, gi, block_cols(j)).wait_recv()
        produce(4 + j, lhs[0], gi[:, j * 1024 : (j + 1) * 1024])
        if j == 3:
            for c in lhs_copies(6):
                c.start()

    def first_norm(_):
        for c in loads[2:]:
            c.wait()
        e = gh[...]
        scaled = e * params[6:7]
        n = norm[...]
        sums_v[3:4] = jnp.sum(e, axis=0, keepdims=True)
        sums_v[4:5] = jnp.sum(e * n, axis=0, keepdims=True)
        gh[...] = inv[:, 0:1] * (scaled - row_mean(scaled) - n * row_mean(scaled * n))
        ga[mine] = gh[...].astype(BF16)
        to_pair(4, ga, whole).start()
        sums_v[5:6] = jnp.sum(ga[mine].astype(F32), axis=0, keepdims=True)

    def grad_mixed(_):
        w_copy(8).wait()
        w_copy(9).start()
        gm[...] = dot_nt(ga[mine], wbuf[0]).astype(BF16)
        w_copy(10).start()

    def out_block(_):
        for c in lhs_copies(5):
            c.wait()
        to_pair(4, ga, whole).wait_recv()
        produce(8, lhs[1], ga[...])

    left = lax.broadcasted_iota(jnp.int32, (seq, 128), 1) < HEAD_SIZE
    key_row = lax.broadcasted_iota(jnp.int32, (seq, seq), 0)
    scale = 1.0 / math.sqrt(HEAD_SIZE)

    def attend(step, carry):
        slot, pair_of = lax.rem(step, slots), lax.div(step, slots)
        at_rows = pl.ds(pl.multiple_of(slot * seq, seq), seq)
        own_rows = pl.ds(pl.multiple_of(p.core * rows + slot * seq, seq), seq)
        col = pl.multiple_of(pair_of * 128, 128)
        at_q = pl.ds(col, 128)
        at_k = pl.ds(pl.multiple_of(width + col, 128), 128)
        at_v = pl.ds(pl.multiple_of(2 * width + col, 128), 128)
        q, k, v = gq[own_rows, at_q], gq[own_rows, at_k], gq[own_rows, at_v]
        do = gm[at_rows, at_q]
        dead = key_row >= lengths[slot]
        parts = []
        for head in range(2):
            lanes = left if head == 0 else ~left
            k_head = jnp.where(lanes, k, jnp.zeros_like(k))
            v_head = jnp.where(lanes, v, jnp.zeros_like(v))
            scores = jnp.where(dead, -1e30, dot_nt(k_head, q) * scale)
            exps = jnp.exp(scores - jnp.max(scores, axis=0, keepdims=True))
            probs = exps * (1.0 / jnp.sum(exps, axis=0, keepdims=True))
            d_probs = dot_nt(v_head, do)
            shared = jnp.sum(probs * d_probs, axis=0, keepdims=True)
            d_scores = (probs * (d_probs - shared)).astype(BF16)
            parts.append(
                (dot_tn(d_scores, k) * scale, dot_nn(d_scores, q) * scale, dot_nn(probs.astype(BF16), do))
            )
        for at, one, two in zip((at_q, at_k, at_v), *parts):
            gq[own_rows, at] = jnp.where(left, one, two).astype(BF16)
        return carry

    steps = 8 * slots

    def attention(first, last):
        lax.fori_loop(first * steps // 16, last * steps // 16, attend, 0)
        if last % 8 == 0:
            half = last // 8 - 1
            for j in range(3):
                to_pair(5 + 3 * half + j, gq, pl.ds(j * 1024 + 512 * half, 512)).start()

    def qkv_block(j):
        if j == 0:
            for c in lhs_copies(6):
                c.wait()
        for half in range(2):
            to_pair(5 + 3 * half + j, gq, pl.ds(j * 1024 + 512 * half, 512)).wait_recv()
        produce(9 + j, lhs[0], gq[:, j * 1024 : (j + 1) * 1024])

    order = (6, 7, 5, 3, 2, 1, 4, 0)

    def small_to(k):
        g = planes[k]
        return remote(s_send.at[g], s_got.at[p.f], sm_send.at[k], sm_recv.at[k], p.dev(f=g))

    def small_from(k):
        g = lax.rem(p.f + 7 - k, 8)
        return remote(s_send.at[g], s_got.at[g], sm_send.at[k], sm_recv.at[k], p.dev(f=g))

    def level_to(k):
        return remote(s_total, s_all.at[p.z], smz_send.at[k], smz_recv.at[k], p.dev(z=levels[k]))

    def level_from(k):
        g = lax.rem(p.z + 3 - k, 4)
        return remote(s_total, s_all.at[g], smz_send.at[k], smz_recv.at[k], p.dev(z=g))

    stores = (
        pltpu.make_async_copy(gh, token_grad, store_sem.at[0]),
        pltpu.make_async_copy(s_out, small_out, store_sem.at[1]),
    )

    def small(_):
        sums_v[6:7] = jnp.sum(gq[mine, 0:1024].astype(F32), axis=0, keepdims=True)
        sums_v[7:8] = jnp.sum(gq[mine, 2048:3072].astype(F32), axis=0, keepdims=True)
        for g in range(8):
            cols = slice(g * 128, (g + 1) * 128)
            for i, row in enumerate(order):
                s_send[g, i : i + 1] = sums_v[row : row + 1, cols]
            for i in range(4):
                lo = (g % 2) * 512 + i * 128
                s_send[g, 8 + i : 9 + i] = upsum[g // 2 : g // 2 + 1, lo : lo + 128]
        for k in range(7):
            small_to(k).start()
        s_got[p.f] = s_send[p.f]

    def token_step(j):
        w_copy(9 + j).wait()
        gh[...] += dot_nt(gq[mine, j * 1024 : (j + 1) * 1024], wbuf[(9 + j) % 2])
        if j == 0:
            w_copy(11).start()
        if j == 2:
            stores[0].start()

    def level(which):
        if which == 1:
            for k in range(7):
                small_from(k).wait_recv()
            total = s_got[0]
            for g in range(1, 8):
                total = total + s_got[g]
            s_total[...] = total
            for k in range(3):
                level_to(k).start()
            s_all[p.z] = total
            for j in range(4):
                to_pair(j, gi, block_cols(j)).wait_send()
            to_pair(4, ga, whole).wait_send()
            for j in range(3):
                for half in range(2):
                    to_pair(5 + 3 * half + j, gq, pl.ds(j * 1024 + 512 * half, 512)).wait_send()
            return
        for k in range(3):
            level_from(k).wait_recv()
        s_out[...] = (s_all[0] + s_all[1]) + (s_all[2] + s_all[3])
        stores[1].start()
        for k in range(7):
            small_to(k).wait_send()
        for k in range(3):
            level_to(k).wait_send()
        stores[0].wait()
        stores[1].wait()

    work = {
        "start": start, "down": down, "g": inner_step, "h": hidden_step, "u": up_block, "norm": first_norm,
        "gm": grad_mixed, "o": out_block, "at": attention, "q": qkv_block, "small": small, "t": token_step,
        "level": level, "begin": red.begin, "second": red.second, "along": red.along, "inward": red.inward,
        "swap": red.swap_out, "hand": red.hand_out, "pass": red.hand_on, "close": red.close,
    }
    for name, *which in PLAN:
        work[name](*which)


def backward_call(lengths, saved):
    wq, wo, wu, wd, qkv, slope = saved[:6]
    rows, width = qkv.shape[0], wo.shape[0]
    ff = wu.shape[1]
    anyspace = pl.BlockSpec(memory_space=pl.ANY)
    shape = jax.ShapeDtypeStruct
    dma = pltpu.SemaphoreType.DMA
    outs = [
        shape((rows, width), F32),
        shape((width // 8, 3 * width), BF16),
        shape((width // 8, width), BF16),
        shape((width // 8, ff), BF16),
        shape((ff // 8, width), BF16),
        shape((16, 128), F32),
    ]
    scratch = [
        pltpu.VMEM((2, 2 * rows, 512), BF16),
        pltpu.VMEM((2, 1024, 1024), BF16),
        pltpu.VMEM((2, rows, 1024), BF16),
        pltpu.VMEM((2 * rows, width), BF16),
        pltpu.VMEM((2 * rows, ff), BF16),
        pltpu.VMEM((2 * rows, 3 * width), BF16),
        pltpu.VMEM((rows, width), BF16),
        pltpu.VMEM((rows, width), F32),
        pltpu.VMEM((rows, width), F32),
        pltpu.VMEM((rows, 128), F32),
        pltpu.VMEM((16, width), F32),
        pltpu.VMEM((8, width), F32),
        pltpu.VMEM((4, width), F32),
        pltpu.VMEM((BLOCKS, 2, 2, 128, 1024), BF16),
        pltpu.VMEM((BLOCKS, 2, 64, 1024), BF16),
        pltpu.VMEM((BLOCKS, 2, 64, 1024), BF16),
        pltpu.VMEM((BLOCKS, 64, 1024), BF16),
        pltpu.VMEM((BLOCKS, 64, 1024), BF16),
        pltpu.VMEM((BLOCKS, 128, 1024), BF16),
        pltpu.VMEM((BLOCKS, 64, 1024), BF16),
        pltpu.VMEM((len(SHARED), 2, 2, 64, 1024), BF16),
        pltpu.VMEM((8, 16, 128), F32),
        pltpu.VMEM((8, 16, 128), F32),
        pltpu.VMEM((16, 128), F32),
        pltpu.VMEM((4, 16, 128), F32),
        pltpu.VMEM((16, 128), F32),
        dma((10, len(PIECES))),
        dma((10, len(PIECES))),
        dma((len(PIECES),)),
        dma((11,)),
        dma((11,)),
        dma((7,)),
        dma((7, 4)),
        dma((12,)),
        dma((4,)),
        dma((7,)),
        dma((7,)),
        dma((3,)),
        dma((3,)),
        dma((2,)),
        dma((len(SHARED), 2)),
        dma((len(SHARED), 2)),
    ]
    return pl.pallas_call(
        backward_kernel,
        out_shape=outs,
        in_specs=[pl.BlockSpec(memory_space=pltpu.SMEM)] + [anyspace] * len(saved),
        out_specs=[anyspace] * len(outs),
        scratch_shapes=scratch,
        name="backward",
        cost_estimate=pl.CostEstimate(flops=4 * 512 * 12582912, bytes_accessed=60 * MIB, transcendentals=4 * MIB),
        compiler_params=pltpu.CompilerParams(
            collective_id=1, has_side_effects=True, vmem_limit_bytes=60 * MIB
        ),
    )(lengths, *saved)


def finish_kernel(
    layer_in, token_in, q_in, o_in, u_in, d_in, small,
    layer_out, token_out, q_out, o_out, u_out, d_out, biases_out, up_bias_out, gains_out,
    q_low, o_low, u_low, d_low, layer_v, token_v, small_v, q, o, u, d, sem,
):
    sources = (d_in, u_in, q_in, o_in, token_in, layer_in, small)
    lows, wides = (d_low, u_low, q_low, o_low, token_v, layer_v, small_v), (d, u, q, o, token_v, layer_v)
    results = (d_out, u_out, q_out, o_out, token_out, layer_out)
    ins = [pltpu.make_async_copy(a, b, sem.at[i]) for i, (a, b) in enumerate(zip(sources, lows))]
    outs = [pltpu.make_async_copy(a, b, sem.at[7 + i]) for i, (a, b) in enumerate(zip(wides, results))]
    for c in ins:
        c.start()
    for a, b, c_in, c_out in zip(lows, wides, ins, outs):
        c_in.wait()
        if a is not b:
            b[...] = a[...].astype(F32)
        c_out.start()
    ins[-1].wait()
    biases_out[...] = small_v[0:6]
    gains_out[...] = small_v[6:8]
    for i in range(4):
        up_bias_out[i * 128 : (i + 1) * 128] = small_v[8 + i]
    for c in outs:
        c.wait()


def finish_call(layer_out, token_grad, weight_grads, small):
    anyspace = pl.BlockSpec(memory_space=pl.ANY)
    vmem = pl.BlockSpec(memory_space=pltpu.VMEM)
    shape = jax.ShapeDtypeStruct
    wide = [shape(g.shape, F32) for g in weight_grads]
    outs = [
        shape(layer_out.shape, BF16), shape(token_grad.shape, F32), *wide,
        shape((6, 128), F32), shape((512,), F32), shape((2, 128), F32),
    ]
    return pl.pallas_call(
        finish_kernel,
        out_shape=outs,
        in_specs=[anyspace] * 7,
        out_specs=[anyspace] * 6 + [vmem] * 3,
        scratch_shapes=[pltpu.VMEM(g.shape, BF16) for g in weight_grads]
        + [pltpu.VMEM(g.shape, g.dtype) for g in (layer_out, token_grad, small)]
        + [pltpu.VMEM(g.shape, F32) for g in weight_grads]
        + [pltpu.SemaphoreType.DMA((13,))],
        name="finish",
        compiler_params=pltpu.CompilerParams(vmem_limit_bytes=60 * MIB),
    )(layer_out, token_grad, *weight_grads, small)


def plane(
    tokens,
    lengths,
    cotangent,
    qkv_weight,
    out_weight,
    up_weight,
    down_weight,
    biases,
    up_bias,
    gains,
):
    layer_out, *saved = forward_call(
        tokens, lengths, cotangent, qkv_weight, out_weight, up_weight, down_weight, biases, up_bias, gains
    )
    token_grad, *weight_grads, small = backward_call(lengths, saved)
    return tuple(finish_call(layer_out, token_grad, weight_grads, small))


def solution(mesh):
    step = plane if dict(mesh.shape) == {"fsdp": 8, "rep": 4} else portable
    both = ("fsdp", "rep")
    in_specs = (
        P(both, None),
        P(both),
        P(both, None),
        P("fsdp", None),
        P("fsdp", None),
        P("fsdp", None),
        P("fsdp", None),
        P(None, "fsdp"),
        P("fsdp"),
        P(None, "fsdp"),
    )
    out_specs = (
        P(both, None),
        P(both, None),
        P("fsdp", None),
        P("fsdp", None),
        P("fsdp", None),
        P("fsdp", None),
        P(None, "fsdp"),
        P("fsdp"),
        P(None, "fsdp"),
    )
    return jax.shard_map(
        step, mesh=mesh, in_specs=in_specs, out_specs=out_specs, check_vma=False
    )
```
